128 devices in a mesh: tile: 2 (over x_hi), kern: 4 (over x_lo, core), noise: 16 (over y, z).
Axes of the slice: x: 4 (x_hi: 2, x_lo: 2; x = x_hi * 2 + x_lo), y: 4, z: 4, core: 2. Of those that a mesh axis runs over, the one named last changes fastest.
Arguments:
- mask_values: float32 [2048, 4096], P(('kern', 'noise'), 'tile'), may hold values from 0 to 1
- kernels: float32 [24, 2, 128, 128], P('kern'), may hold values from -6 to 6
- weights: float32 [24], P('kern'), may hold values from 0.02 to 0.5
- target: bfloat16 [2048, 4096], P(('kern', 'noise'), 'tile'), may hold values from 0 to 1
- dose_noise: bfloat16 [32, 2048, 4096], P('noise', 'kern', 'tile'), may hold values from -4 to 4
Outputs:
- mask_grad: float32 [2048, 4096], P(('kern', 'noise'), 'tile')
The draws below stay inside these ranges and needn't reach their ends.
All inputs are finite; a program needn't handle non-finite values.
Results may differ from the reference program's by a relative error of at most 0.0019.
Values may be sent and summed in bfloat16 or wider, within the bound.
No kernel may reach another device: no remote copies, remote signals or barrier semaphores. Data moves between devices by JAX's collectives and lax.ppermute only.
A program may use at most 192 MiB of HBM per device.

```python
import math
import jax
import jax.numpy as jnp
from jax import lax

P_SIZE = 2048
Q = 128
HALO = 16
KERNELS = 24
SAMPLES = 32
BAND = 4096
N_TILE = 2


def block_scale(stream_key, dims, shards, low, top_value):
    def one(axis_at, shards_of):
        steps = jax.random.uniform(jax.random.fold_in(jax.random.fold_in(stream_key, 6), axis_at), (shards_of,), jnp.float32, low / len(shards), top_value / len(shards))
        return jnp.repeat(jnp.exp(steps), dims[axis_at] // shards_of).reshape((-1,) + (1,) * (len(dims) - axis_at - 1))

    loudness = one(*shards[0])
    for cut in shards[1:]:
        loudness = loudness * one(*cut)
    return loudness


def bell_draw(own_key, extent, spread, reach, split=(), held_as=jnp.bfloat16):
    array = jax.random.normal(own_key, extent, jnp.float32) * spread
    if len(split) > 0:
        array = block_scale(own_key, extent, split, -0.22, 0.18) * array
    return jnp.clip(array, min=-reach, max=reach).astype(held_as)


def setup_inputs(seed: int = 0) -> dict:
    key_list = jax.random.split(jax.random.key(seed), 6)
    mask_values = jnp.clip(1.0 * jax.random.uniform(key_list[0], (P_SIZE, BAND), jnp.float32) ** block_scale(key_list[0], (P_SIZE, BAND), ((0, 64), (1, 2)), -0.2, 0.2), 0.0, 1.0)
    kernels = bell_draw(key_list[1], (KERNELS, 2, Q, Q), 1.0, 6.0, ((0, 4),), jnp.float32)
    weights = jnp.clip(jnp.exp(math.log(0.5) - 3.218876 * jax.random.uniform(key_list[2], (KERNELS,), jnp.float32) ** block_scale(key_list[2], (KERNELS,), ((0, 4),), -0.2, 0.2)), 0.02, 0.5)
    target = jnp.clip(1.0 * jax.random.uniform(key_list[3], (P_SIZE, BAND), jnp.float32) ** block_scale(key_list[3], (P_SIZE, BAND), ((0, 64), (1, 2)), -0.2, 0.2), 0.0, 1.0).astype(jnp.bfloat16)
    dose_noise = bell_draw(key_list[4], (SAMPLES, P_SIZE, BAND), 1.0, 4.0, ((0, 16), (1, 4), (2, 2)))
    return dict(mask_values=mask_values, kernels=kernels, weights=weights, target=target, dose_noise=dose_noise)


two_pi = 6.283185307179586
slope = 2.0
thresh = 2.0
dose_sigma = 0.25
penalty = 4.0

def matmul(left, right):
    return jnp.dot(left, right, precision=lax.Precision.HIGHEST, preferred_element_type=jnp.float32)

def wave_tables(row_ids, freq_count, period):
    centred = jnp.arange(freq_count, dtype=jnp.int32) - freq_count // 2
    wrapped = centred[:, None] * row_ids[None, :] % period
    angles = wrapped.astype(jnp.float32) * (two_pi / period)
    return (jnp.cos(angles), jnp.sin(angles))

def spectrum(transmit, row_cos, row_sin, col_cos, col_sin):
    period = transmit.shape[1]
    by_cos = matmul(transmit, col_cos.T)
    by_sin = matmul(transmit, col_sin.T)
    real_part = (matmul(row_cos, by_cos) - matmul(row_sin, by_sin)) / period
    imag_part = -(matmul(row_cos, by_sin) + matmul(row_sin, by_cos)) / period
    return jnp.stack([real_part, imag_part])

def kernel_intensity(spectral, kernel, weight, row_cos, row_sin, col_cos, col_sin):
    freq_count = spectral.shape[1]
    near_real = kernel[0] * spectral[0] - kernel[1] * spectral[1]
    near_imag = kernel[0] * spectral[1] + kernel[1] * spectral[0]
    left_real = matmul(row_cos.T, near_real) - matmul(row_sin.T, near_imag)
    left_imag = matmul(row_cos.T, near_imag) + matmul(row_sin.T, near_real)
    field_real = (matmul(left_real, col_cos) - matmul(left_imag, col_sin)) / freq_count
    field_imag = (matmul(left_real, col_sin) + matmul(left_imag, col_cos)) / freq_count
    return weight * (field_real * field_real + field_imag * field_imag)

def blur_taps(halo_width):
    offsets = jnp.arange(2 * halo_width + 1, dtype=jnp.int32) - halo_width
    deviation = halo_width / 2.0
    profile = jnp.exp(-offsets.astype(jnp.float32) ** 2 / (2.0 * deviation * deviation))
    return profile / jnp.sum(profile)

def diffuse(source):
    taps = blur_taps(HALO)
    row_count, col_count = source.shape
    padded = jnp.pad(source, HALO)
    across = jnp.zeros((row_count, col_count + 2 * HALO), jnp.float32)
    for offset in range(2 * HALO + 1):
        across = across + taps[offset] * padded[offset:offset + row_count, :]
    result = jnp.zeros((row_count, col_count), jnp.float32)
    for offset in range(2 * HALO + 1):
        result = result + taps[offset] * across[:, offset:offset + col_count]
    return result

def reference(mask_values, kernels, weights, target, dose_noise):
    pixel_ids = jnp.arange(P_SIZE, dtype=jnp.int32)
    col_cos, col_sin = wave_tables(pixel_ids, Q, P_SIZE)

    def tile_intensity(spectral):

        def step(running, pair):
            kernel, weight = pair
            return (running + kernel_intensity(spectral, kernel, weight, col_cos, col_sin, col_cos, col_sin), None)
        return lax.scan(step, jnp.zeros((P_SIZE, P_SIZE), jnp.float32), (kernels, weights))[0]

    def tile_spectrum(values):
        return spectrum(values, col_cos, col_sin, col_cos, col_sin)
    spectra = []
    images = []
    for which_tile in range(N_TILE):
        transmit = 2.0 * mask_values[:, which_tile * P_SIZE:(which_tile + 1) * P_SIZE] - 1.0
        spectral = tile_spectrum(transmit)
        spectra.append(spectral)
        images.append(tile_intensity(spectral))
    intensity = jnp.concatenate(images, axis=1)
    acid = diffuse(intensity)

    def mean_step(running, sample):
        dose_factor = 1.0 + dose_sigma * sample.astype(jnp.float32)
        response = jax.nn.sigmoid(slope * (acid * dose_factor - thresh))
        return (running + response, None)
    mean_resp = lax.scan(mean_step, jnp.zeros(acid.shape, jnp.float32), dose_noise)[0] / SAMPLES

    def grad_step(carry, sample):
        upper_sum, lower_sum = carry
        dose_factor = 1.0 + dose_sigma * sample.astype(jnp.float32)
        response = jax.nn.sigmoid(slope * (acid * dose_factor - thresh))
        response_slope = slope * response * (1.0 - response) * dose_factor
        upper_sum = upper_sum + response_slope * ((1.0 + penalty) * response - penalty * mean_resp)
        return ((upper_sum, lower_sum + response_slope), None)
    zeros_field = jnp.zeros(acid.shape, jnp.float32)
    upper_sum, lower_sum = lax.scan(grad_step, (zeros_field, zeros_field), dose_noise)[0]
    acid_grad = 2.0 / SAMPLES * (upper_sum - target.astype(jnp.float32) * lower_sum)
    intensity_grad = diffuse(acid_grad)
    grads = []
    for which_tile in range(N_TILE):
        transmit = 2.0 * mask_values[:, which_tile * P_SIZE:(which_tile + 1) * P_SIZE] - 1.0
        unused_spec, pull_mask = jax.vjp(tile_spectrum, transmit)
        unused_image, pull_spec = jax.vjp(tile_intensity, spectra[which_tile])
        spec_grad = pull_spec(intensity_grad[:, which_tile * P_SIZE:(which_tile + 1) * P_SIZE])[0]
        grads.append(2.0 * pull_mask(spec_grad)[0])
    return jnp.concatenate(grads, axis=1)
```

```python
import math

import jax
import jax.numpy as jnp
import numpy as np
from jax import lax
from jax.experimental import pallas as pl
from jax.experimental.pallas import tpu as pltpu
from jax.sharding import PartitionSpec as P

HALO = 16
FREQ = 128
COARSE = 256
PERIOD = 2048
ROWS = 32
REACH = ROWS + 2 * HALO
EDGE = 128
GROUP = 6
KERNELS = 24
SAMPLES = 32
VMEM_BYTES = 48 * 1024 * 1024
BF = jnp.bfloat16
F32 = jnp.float32


def np_split(table):
    table = np.asarray(table, np.float32)
    high = table.astype(jnp.bfloat16)
    low = (table - high.astype(np.float32)).astype(jnp.bfloat16)
    return high, low


def np_waves(ids):
    centred = np.arange(FREQ) - FREQ // 2
    angles = 2.0 * np.pi * ((centred[:, None] * ids[None, :]) % PERIOD) / PERIOD
    return np.cos(angles), np.sin(angles)


def tables():
    cos, sin = np_waves(np.arange(PERIOD))
    waves = np.concatenate([cos, sin], 0).T
    reach = np.zeros((PERIOD + 2 * HALO, 4 * FREQ))
    reach[HALO:-HALO] = np.concatenate([cos, -sin, sin, cos], 0).T
    ccos, csin = np_waves(np.arange(COARSE) * (PERIOD // COARSE))
    grid = np.block([[ccos, csin], [-csin, ccos]]) / FREQ
    offsets = np.arange(-HALO, HALO + 1)
    taps = np.exp(-(offsets.astype(np.float64) ** 2) / (2.0 * (HALO / 2.0) ** 2))
    taps = taps / taps.sum()
    row_blur = np.zeros((ROWS, REACH))
    for row in range(ROWS):
        row_blur[row, row : row + 2 * HALO + 1] = taps
    shift = np.arange(PERIOD)[:, None] - (PERIOD // COARSE) * np.arange(COARSE)[None, :]
    freqs = np.arange(1, FREQ)
    line = (1.0 + 2.0 * np.cos(2.0 * np.pi * np.outer(np.arange(PERIOD), freqs) / PERIOD).sum(1)) / COARSE
    interp = line[shift % PERIOD]
    padded = np.zeros((PERIOD + 2 * HALO, COARSE))
    padded[HALO:-HALO] = interp
    own = np.zeros((PERIOD, COARSE))
    for index, tap in enumerate(taps):
        own += tap * padded[index : index + PERIOD]
    cross = np.zeros((2, COARSE, 2 * EDGE))
    for column in range(HALO):
        for index, offset in enumerate(offsets):
            if column + offset < 0:
                cross[1, :, column] += taps[index] * interp[PERIOD + column + offset]
            place = PERIOD - 1 - column + offset
            if place >= PERIOD:
                cross[0, :, 2 * EDGE - 1 - column] += taps[index] * interp[place - PERIOD]
    return waves, reach, grid, row_blur, own.T, cross


WAVES, REACH_WAVES, GRID, ROW_BLUR, OWN, CROSS = tables()
WAVES_HI, WAVES_LO = np_split(WAVES)
GRID_HI, GRID_LO = np_split(GRID)
OWN_HI, OWN_LO = np_split(OWN)
CROSS_HI, CROSS_LO = np_split(CROSS)


def split(value):
    high = value.astype(BF)
    return high, (value - high.astype(F32)).astype(BF)


NN = (((1,), (0,)), ((), ()))
NT = (((1,), (1,)), ((), ()))
TN = (((0,), (0,)), ((), ()))


def dot3(left, right, dims=NN):
    lh, ll = left
    rh, rl = right

    def one(a, b):
        return lax.dot_general(a, b, dims, preferred_element_type=F32)

    return one(lh, rh) + (one(lh, rl) + one(ll, rh))


def call(body, out_shape, args, **kw):
    return pl.pallas_call(
        body,
        out_shape=out_shape,
        compiler_params=pltpu.CompilerParams(vmem_limit_bytes=VMEM_BYTES),
        **kw,
    )(*args)


def spectrum_body(mask_ref, wh_ref, wl_ref, block_ref, out_ref):
    transmit = 2.0 * mask_ref[...] - 1.0
    by_col = dot3(split(transmit), (wh_ref[...], wl_ref[...]))
    both = dot3(split(block_ref[...]), split(by_col), TN)
    out_ref[:FREQ] = (both[:FREQ, :FREQ] - both[FREQ:, FREQ:]) * (1.0 / PERIOD)
    out_ref[FREQ:] = (both[:FREQ, FREQ:] + both[FREQ:, :FREQ]) * (-1.0 / PERIOD)


def field_body(spec_ref, kern_ref, reach_ref, gh_ref, gl_ref, blur_ref, field_ref, rows_ref, total_ref):
    step = pl.program_id(0)
    spec_re = spec_ref[:FREQ]
    spec_im = spec_ref[FREQ:]
    wave = split(jnp.concatenate([reach_ref[:, : 2 * FREQ], reach_ref[:, 2 * FREQ :]], 0))
    lefts = []
    for pair in range(GROUP // 2):
        near_re, near_im = [], []
        for index in (2 * pair, 2 * pair + 1):
            kern_re, kern_im = kern_ref[index, 0], kern_ref[index, 1]
            near_re.append(kern_re * spec_re - kern_im * spec_im)
            near_im.append(kern_re * spec_im + kern_im * spec_re)
        near = jnp.concatenate([jnp.concatenate(near_re, 1), jnp.concatenate(near_im, 1)], 0)
        left = dot3(wave, split(near))
        for half in range(2):
            cols = left[:, half * FREQ : (half + 1) * FREQ]
            lefts.append(jnp.concatenate([cols[:REACH], cols[REACH:]], 1))
    field = dot3(split(jnp.concatenate(lefts, 0)), (gh_ref[...], gl_ref[...]))
    field_ref[...] = field
    power = field * field
    power = power[:, :COARSE] + power[:, COARSE:]
    total = power[:REACH]
    for index in range(1, GROUP):
        total = total + power[index * REACH : (index + 1) * REACH]

    @pl.when(step == 0)
    def _():
        total_ref[...] = total

    @pl.when(step > 0)
    def _():
        total_ref[...] += total

    @pl.when(step == pl.num_programs(0) - 1)
    def _():
        rows_ref[...] = dot3(split(blur_ref[...]), split(total_ref[...]))


def own_body(rows_ref, oh_ref, ol_ref, out_ref):
    out_ref[...] = dot3(split(rows_ref[...]), (oh_ref[...], ol_ref[...]))


CHUNK = 512
LANES = 256


def dose_body(own_ref, other_ref, ch_ref, cl_ref, target_ref, noise_ref, grad_ref, send_ref, edge_ref, acid_ref):
    step = pl.program_id(0)
    last = pl.num_programs(0) - 1
    acid_ref[...] = own_ref[...]

    @pl.when(step == 0)
    def _():
        edge_ref[...] = dot3(split(other_ref[...]), (ch_ref[...], cl_ref[...]))
        acid_ref[:, :EDGE] += edge_ref[:, :EDGE]

    @pl.when(step == last)
    def _():
        acid_ref[:, CHUNK - EDGE :] += edge_ref[:, EDGE:]

    for row in range(0, ROWS, 16):
        for col in range(0, CHUNK, LANES):
            place = (slice(row, row + 16), slice(col, col + LANES))
            acid = acid_ref[place]
            quarter = 0.25 * acid
            base = acid - 2.0

            def sample(index, carry):
                sum_u, sum_q, sum_qu = carry
                noise = noise_ref[(index,) + place].astype(F32)
                u = jnp.tanh(quarter * noise + base)
                q = (1.0 - u * u) * (1.0 + 0.25 * noise)
                return sum_u + u, sum_q + q, sum_qu + q * u

            zero = jnp.zeros((16, LANES), F32)
            sum_u, sum_q, sum_qu = lax.fori_loop(0, SAMPLES, sample, (zero, zero, zero), unroll=8)
            target = target_ref[place].astype(F32)
            inner = 0.25 - sum_u * (1.0 / SAMPLES) - 0.5 * target
            grad_ref[place] = (1.0 / 16.0) * (sum_q * inner + 1.25 * sum_qu)

    @pl.when(step == 0)
    def _():
        edge_ref[:, :EDGE] = grad_ref[:, :EDGE]

    @pl.when(step == last)
    def _():
        edge_ref[:, EDGE:] = grad_ref[:, CHUNK - EDGE :]
        send_ref[...] = dot3(split(edge_ref[...]), (ch_ref[...], cl_ref[...]), NT)


def back_own_body(grad_ref, oh_ref, ol_ref, out_ref):
    out_ref[...] = dot3(split(grad_ref[...]), (oh_ref[...], ol_ref[...]), NT)


def back_body(own_ref, other_ref, field_ref, kern_ref, reach_ref, gh_ref, gl_ref, blur_ref, out_ref, grad_ref):
    step = pl.program_id(0)

    @pl.when(step == 0)
    def _():
        rows = own_ref[...] + other_ref[...]
        part = 2.0 * dot3(split(blur_ref[...]), split(rows), TN)
        grad_ref[:, :COARSE] = part
        grad_ref[:, COARSE:] = part
        out_ref[...] = jnp.zeros_like(out_ref)

    grad = grad_ref[...]
    pulled = jnp.concatenate(
        [field_ref[index * REACH : (index + 1) * REACH] * grad for index in range(GROUP)], 0
    )
    lefts = dot3(split(pulled), (gh_ref[...], gl_ref[...]), NT)
    wave = split(jnp.concatenate([reach_ref[:, : 2 * FREQ], reach_ref[:, 2 * FREQ :]], 0))
    sum_re = out_ref[:FREQ]
    sum_im = out_ref[FREQ:]
    for pair in range(GROUP // 2):
        stack = []
        for index in (2 * pair, 2 * pair + 1):
            left = lefts[index * REACH : (index + 1) * REACH]
            stack.append(jnp.concatenate([left[:, :FREQ], left[:, FREQ:]], 0))
        near = dot3(wave, split(jnp.concatenate(stack, 1)), TN)
        for half in range(2):
            index = 2 * pair + half
            near_re = near[:FREQ, half * FREQ : (half + 1) * FREQ]
            near_im = near[FREQ:, half * FREQ : (half + 1) * FREQ]
            kern_re, kern_im = kern_ref[index, 0], kern_ref[index, 1]
            sum_re = sum_re + (kern_re * near_re + kern_im * near_im)
            sum_im = sum_im + (kern_re * near_im - kern_im * near_re)
    out_ref[:FREQ] = sum_re
    out_ref[FREQ:] = sum_im


def final_body(spec_ref, block_ref, wh_ref, wl_ref, out_ref):
    grad_re = spec_ref[:FREQ]
    grad_im = spec_ref[FREQ:]
    mix = jnp.concatenate(
        [jnp.concatenate([grad_re, -grad_im], 1), jnp.concatenate([-grad_im, -grad_re], 1)], 0
    ) * (2.0 / PERIOD)
    rows = dot3(split(block_ref[...]), split(mix))
    out_ref[...] = dot3(split(rows), (wh_ref[...], wl_ref[...]), NT)


def sum_blocks(part):
    axes = ("kern", "noise")
    count = lax.axis_size(axes)
    pieces = part.reshape(count, part.shape[0] // count, part.shape[1])
    got = lax.all_to_all(pieces, axes, 0, 0, tiled=True)
    mine = jnp.sum(got, 0, keepdims=True)
    return lax.all_to_all(jnp.broadcast_to(mine, pieces.shape), axes, 0, 0, tiled=True).reshape(part.shape)


def body(mask_values, kernels, weights, target, dose_noise):
    noise_count = lax.axis_size("noise")
    block = lax.axis_index("kern") * noise_count + lax.axis_index("noise")
    tile = lax.axis_index("tile")
    first = block * ROWS
    whole = pl.BlockSpec(memory_space=pltpu.VMEM)
    f32 = lambda *shape: jax.ShapeDtypeStruct(shape, F32)
    steps = KERNELS // GROUP

    scaled = kernels * jnp.sqrt(weights)[:, None, None, None]
    kern = lax.all_gather(scaled, "kern", axis=0, tiled=True)
    samples = lax.all_to_all(dose_noise, "noise", 1, 0, tiled=True)

    block_waves = lax.dynamic_slice(jnp.asarray(WAVES, F32), (first, 0), (ROWS, 2 * FREQ))
    reach_waves = lax.dynamic_slice(jnp.asarray(REACH_WAVES, F32), (first, 0), (REACH, 4 * FREQ))
    waves = (jnp.asarray(WAVES_HI), jnp.asarray(WAVES_LO))
    grid = (jnp.asarray(GRID_HI), jnp.asarray(GRID_LO))
    own = (jnp.asarray(OWN_HI), jnp.asarray(OWN_LO))
    cross = tuple(lax.dynamic_index_in_dim(jnp.asarray(t), tile, 0, keepdims=False) for t in (CROSS_HI, CROSS_LO))
    blur = jnp.asarray(ROW_BLUR, F32)

    part = call(spectrum_body, f32(2 * FREQ, FREQ), (mask_values, *waves, block_waves))
    spec = sum_blocks(part)

    def fixed(*shape):
        return pl.BlockSpec(shape, lambda i: (0,) * len(shape))

    kern_spec = pl.BlockSpec((GROUP, 2, FREQ, FREQ), lambda i: (i, 0, 0, 0))
    field_spec = pl.BlockSpec((GROUP * REACH, 2 * COARSE), lambda i: (i, 0))
    const_specs = [
        fixed(REACH, 4 * FREQ),
        fixed(2 * FREQ, 2 * COARSE),
        fixed(2 * FREQ, 2 * COARSE),
        fixed(ROWS, REACH),
    ]
    field, rows = call(
        field_body,
        (f32(KERNELS * REACH, 2 * COARSE), f32(ROWS, COARSE)),
        (spec, kern, reach_waves, *grid, blur),
        grid=(steps,),
        in_specs=[fixed(2 * FREQ, FREQ), kern_spec] + const_specs,
        out_specs=(field_spec, fixed(ROWS, COARSE)),
        scratch_shapes=[pltpu.VMEM((REACH, COARSE), F32)],
    )
    swap = [(0, 1), (1, 0)]
    rows_other = lax.ppermute(rows, "tile", swap)
    acid = call(own_body, f32(ROWS, PERIOD), (rows, *own))
    chunk = lambda: pl.BlockSpec((ROWS, CHUNK), lambda i: (0, i))
    grad, send = call(
        dose_body,
        (f32(ROWS, PERIOD), f32(ROWS, COARSE)),
        (acid, rows_other, *cross, target, samples),
        grid=(PERIOD // CHUNK,),
        in_specs=[
            chunk(),
            fixed(ROWS, COARSE),
            fixed(COARSE, 2 * EDGE),
            fixed(COARSE, 2 * EDGE),
            chunk(),
            pl.BlockSpec((SAMPLES, ROWS, CHUNK), lambda i: (0, 0, i)),
        ],
        out_specs=(chunk(), fixed(ROWS, COARSE)),
        scratch_shapes=[pltpu.VMEM((ROWS, 2 * EDGE), F32), pltpu.VMEM((ROWS, CHUNK), F32)],
    )
    grad_other = lax.ppermute(send, "tile", swap)
    grad_own = call(back_own_body, f32(ROWS, COARSE), (grad, *own))
    spec_part = call(
        back_body,
        f32(2 * FREQ, FREQ),
        (grad_own, grad_other, field, kern, reach_waves, *grid, blur),
        grid=(steps,),
        in_specs=[fixed(ROWS, COARSE), fixed(ROWS, COARSE), field_spec, kern_spec] + const_specs,
        out_specs=fixed(2 * FREQ, FREQ),
        scratch_shapes=[pltpu.VMEM((REACH, 2 * COARSE), F32)],
    )
    spec_grad = sum_blocks(spec_part)
    return call(final_body, f32(ROWS, PERIOD), (spec_grad, block_waves, *waves))


def solution(mesh):
    return jax.shard_map(
        body,
        mesh=mesh,
        in_specs=(
            P(("kern", "noise"), "tile"),
            P("kern", None, None, None),
            P("kern"),
            P(("kern", "noise"), "tile"),
            P("noise", "kern", "tile"),
        ),
        out_specs=P(("kern", "noise"), "tile"),
        check_vma=False,
    )
```

```python
import math

import jax
import jax.numpy as jnp
import numpy as np
from jax import lax
from jax.experimental import pallas as pl
from jax.experimental.pallas import tpu as pltpu
from jax.sharding import PartitionSpec as P

HALO = 16
FREQ = 128
COARSE = 256
PERIOD = 2048
ROWS = 32
REACH = ROWS + 2 * HALO
EDGE = 128
GROUP = 6
PAIRS = GROUP // 2
KERN = 4
SAMPLES = 32
RANK = 16
MIB = 32
BF = jnp.bfloat16
F32 = jnp.float32


def np_split(table):
    table = np.asarray(table, np.float32)
    high = table.astype(jnp.bfloat16)
    low = (table - high.astype(np.float32)).astype(jnp.bfloat16)
    return high, low


def np_waves(ids):
    centred = np.arange(FREQ) - FREQ // 2
    angles = 2.0 * np.pi * ((centred[:, None] * ids[None, :]) % PERIOD) / PERIOD
    return np.cos(angles), np.sin(angles)


def line_tables():
    half = FREQ // 2
    pixels = np.arange(PERIOD)
    angle = lambda f: 2.0 * np.pi * ((f[:, None] * pixels[None, :]) % PERIOD) / PERIOD
    line = np.concatenate([np.cos(angle(np.arange(half + 1))), np.sin(angle(np.arange(1, half)))], 0)
    last = np.sin(angle(np.array([half])))
    unfold = np.zeros((FREQ, 2 * FREQ))
    for j in range(FREQ):
        f = j - half
        unfold[abs(f), j] = 1.0
        if 0 < abs(f) < half:
            unfold[half + abs(f), FREQ + j] = np.sign(f)
    row = np.arange(ROWS) - (ROWS - 1) / 2.0
    fine = np.arange(-half, half + 0.01, 0.25)
    wave = np.exp(2j * np.pi * np.outer(row, fine) / PERIOD)
    basis = np.linalg.svd(np.concatenate([wave.real, wave.imag], 1))[0][:, : RANK - 1]
    basis = np.concatenate([basis, np.zeros((ROWS, FREQ - RANK + 1))], 1)
    freqs = np.arange(FREQ) - half
    coef = np.exp(2j * np.pi * np.outer(freqs, row) / PERIOD) @ basis
    blocks = PERIOD // ROWS
    centre = ROWS * np.arange(blocks) + (ROWS - 1) / 2.0
    phase = np.exp(2j * np.pi * np.outer(freqs, centre) / PERIOD)
    rows = phase[:, :, None] * coef[:, None, :RANK]
    rows[:, :, RANK - 1] = 0.0
    spare = np.zeros_like(rows)
    spare[:, :, RANK - 1] = phase
    rows = rows.reshape(FREQ, blocks * RANK)
    spare = spare.reshape(FREQ, blocks * RANK)
    gather = np.concatenate([rows.real, rows.imag, spare.real, spare.imag], 0)
    return line, last, unfold, basis, np.stack([coef.real, coef.imag]), gather


def tables():
    cos, sin = np_waves(np.arange(PERIOD))
    reach = np.zeros((PERIOD + 2 * HALO, 4 * FREQ))
    reach[HALO:-HALO] = np.concatenate([cos, -sin, sin, cos], 0).T
    ccos, csin = np_waves(np.arange(COARSE) * (PERIOD // COARSE))
    grid = np.block([[ccos, csin], [-csin, ccos]]) / FREQ
    offsets = np.arange(-HALO, HALO + 1)
    taps = np.exp(-(offsets.astype(np.float64) ** 2) / (2.0 * (HALO / 2.0) ** 2))
    taps = taps / taps.sum()
    row_blur = np.zeros((ROWS, REACH))
    for row in range(ROWS):
        row_blur[row, row : row + 2 * HALO + 1] = taps
    shift = np.arange(PERIOD)[:, None] - (PERIOD // COARSE) * np.arange(COARSE)[None, :]
    freqs = np.arange(1, FREQ)
    line = (1.0 + 2.0 * np.cos(2.0 * np.pi * np.outer(np.arange(PERIOD), freqs) / PERIOD).sum(1)) / COARSE
    interp = line[shift % PERIOD]
    padded = np.zeros((PERIOD + 2 * HALO, COARSE))
    padded[HALO:-HALO] = interp
    own = np.zeros((PERIOD, COARSE))
    for index, tap in enumerate(taps):
        own += tap * padded[index : index + PERIOD]
    cross = np.zeros((2, COARSE, 2 * EDGE))
    for column in range(HALO):
        for index, offset in enumerate(offsets):
            if column + offset < 0:
                cross[1, :, column] += taps[index] * interp[PERIOD + column + offset]
            place = PERIOD - 1 - column + offset
            if place >= PERIOD:
                cross[0, :, 2 * EDGE - 1 - column] += taps[index] * interp[place - PERIOD]
    return reach, grid, row_blur, own, cross


LINE, LAST, UNFOLD, BASIS, COEF, GATHER = line_tables()
REACH_WAVES, GRID, ROW_BLUR, OWN, CROSS = tables()
BLOCKS = PERIOD // ROWS
GROUP_BLOCKS = BLOCKS // KERN
WAVE = np.stack(
    [
        np.concatenate([part[:, : 2 * FREQ], part[:, 2 * FREQ :]], 0)
        for part in (REACH_WAVES[first : first + REACH] for first in range(0, PERIOD, ROWS))
    ]
)
WAVE = WAVE.reshape(KERN, GROUP_BLOCKS, 2 * REACH, 2 * FREQ).transpose(1, 0, 2, 3)
WAVE = WAVE.reshape(GROUP_BLOCKS, KERN * 2 * REACH, 2 * FREQ)
GATHER_OWN = GATHER.reshape(4 * FREQ, KERN, GROUP_BLOCKS * RANK).transpose(1, 0, 2)
BLUR = np.kron(np.eye(KERN), ROW_BLUR)


def split(value):
    high = value.astype(BF)
    return high, (value - high.astype(F32)).astype(BF)


NN = (((1,), (0,)), ((), ()))


def dot3(left, right):
    lh, ll = left
    rh, rl = right

    def one(a, b):
        return lax.dot_general(a, b, NN, preferred_element_type=F32)

    return one(lh, rh) + (one(lh, rl) + one(ll, rh))


def dot_exact(left, right):
    high, low = left
    return jnp.dot(high, right, preferred_element_type=F32) + jnp.dot(low, right, preferred_element_type=F32)


def call(body, out_shape, args, place=None, **kw):
    params = pltpu.CompilerParams(vmem_limit_bytes=MIB * 1024 * 1024)
    if place is None:
        return pl.pallas_call(body, out_shape=out_shape, compiler_params=params, **kw)(*args)
    grid_spec = pltpu.PrefetchScalarGridSpec(num_scalar_prefetch=1, **kw)
    return pl.pallas_call(body, out_shape=out_shape, compiler_params=params, grid_spec=grid_spec)(place, *args)


def hbm(*values):
    return tuple(pltpu.with_memory_space_constraint(value, pltpu.HBM) for value in values)


def vmem(*values):
    return tuple(pltpu.with_memory_space_constraint(value, pltpu.VMEM) for value in values)


CHUNK = 512
LANES = 256


def front_body(mask_ref, basis_ref, lh_ref, ll_ref, last_ref, noise_ref, first_ref, second_ref, packed_ref):
    @pl.when(pl.program_id(0) == 0)
    def _():
        transmit = (2.0 * mask_ref[...] - 1.0) * (1.0 / PERIOD)
        rows = dot3(split(basis_ref[...]), split(transmit))
        part = dot3(split(rows), (lh_ref[...], ll_ref[...]))
        row = lax.broadcasted_iota(jnp.int32, (RANK, FREQ), 0)
        lane = lax.broadcasted_iota(jnp.int32, (RANK, FREQ), 1)
        apart = jnp.sum(rows * last_ref[...], 1, keepdims=True)
        apart = jnp.sum(jnp.where(row == lane, apart, 0.0), 0, keepdims=True)
        high, low = split(jnp.where(row == RANK - 1, apart, part))
        packed_ref[:RANK] = high
        packed_ref[RANK:] = low

    for which in range(first_ref.shape[0]):
        rows = slice(which * ROWS, (which + 1) * ROWS)
        first_ref[which, :, :PERIOD] = noise_ref[0, rows]
        first_ref[which, :, PERIOD:] = packed_ref[...]
        second_ref[which] = noise_ref[1, rows]


def spectrum_body(_, got_ref, gh_ref, gl_ref, unfold_ref, coef_ref, out_ref):
    high = got_ref[:, :RANK].reshape(GROUP_BLOCKS * RANK, FREQ)
    low = got_ref[:, RANK:].reshape(GROUP_BLOCKS * RANK, FREQ)
    both = dot3((gh_ref[0], gl_ref[0]), (high, low))
    waves = dot_exact(split(both[: 2 * FREQ]), unfold_ref[...])
    spare_cos, spare_sin = both[2 * FREQ : 3 * FREQ], both[3 * FREQ :]
    coef_re, coef_im = coef_ref[0], coef_ref[1]
    last_cos = jnp.sum(coef_re * spare_cos - coef_im * spare_sin, 1, keepdims=True)
    last_sin = jnp.sum(coef_re * spare_sin + coef_im * spare_cos, 1, keepdims=True)
    first = lax.broadcasted_iota(jnp.int32, (FREQ, FREQ), 1) == 0
    cos_cos, cos_sin = waves[:FREQ, :FREQ], waves[:FREQ, FREQ:]
    sin_cos, sin_sin = waves[FREQ:, :FREQ], waves[FREQ:, FREQ:]
    out_ref[:FREQ] = cos_cos - sin_sin + jnp.where(first, last_sin, 0.0)
    out_ref[FREQ:] = jnp.where(first, last_cos, 0.0) - cos_sin - sin_cos


def field_body(place_ref, weight_ref, s0_ref, s1_ref, s2_ref, s3_ref, kern_ref, *refs):
    wh_ref, wl_ref, gh_ref, gl_ref, blur_ref, field_ref = refs[:6]
    piece_refs, (spec_ref, total_ref, rows_ref) = refs[6 : 6 + KERN], refs[6 + KERN :]
    step = pl.program_id(0)

    @pl.when(step == 0)
    def _():
        spec_ref[...] = (s0_ref[...] + s1_ref[...]) + (s2_ref[...] + s3_ref[...])

    spec_re = spec_ref[:FREQ]
    spec_im = spec_ref[FREQ:]
    near_re, near_im = [], []
    for index in range(2):
        kern_re, kern_im = kern_ref[index, 0], kern_ref[index, 1]
        near_re.append(kern_re * spec_re - kern_im * spec_im)
        near_im.append(kern_re * spec_im + kern_im * spec_re)
    near = jnp.concatenate([jnp.concatenate(near_re, 1), jnp.concatenate(near_im, 1)], 0)
    left = dot3((wh_ref[0], wl_ref[0]), split(near))
    lefts = []
    for index in range(2):
        lanes = slice(index * FREQ, (index + 1) * FREQ)
        for group in range(KERN):
            first = 2 * group * REACH
            re, im = left[first : first + REACH, lanes], left[first + REACH : first + 2 * REACH, lanes]
            lefts.append(jnp.concatenate([re, im], 1))
    field = dot3(split(jnp.concatenate(lefts, 0)), (gh_ref[...], gl_ref[...]))
    field_ref[...] = field
    power = field * field
    power = power[:, :COARSE] + power[:, COARSE:]
    half = KERN * REACH
    total = weight_ref[2 * step] * power[:half] + weight_ref[2 * step + 1] * power[half:]

    @pl.when(step == 0)
    def _():
        total_ref[...] = total

    @pl.when(step > 0)
    def _():
        total_ref[...] += total

    @pl.when(step == pl.num_programs(0) - 1)
    def _():
        rows_ref[...] = dot3(split(blur_ref[...]), split(total_ref[...]))
        for shift, piece_ref in enumerate(piece_refs):
            group = lax.rem(place_ref[0] + shift, KERN)
            piece_ref[...] = rows_ref[pl.ds(pl.multiple_of(group * ROWS, ROWS), ROWS)]


def own_body(r0_ref, r1_ref, r2_ref, r3_ref, oh_ref, ol_ref, out_ref, rows_ref):
    rows = (r0_ref[...] + r1_ref[...]) + (r2_ref[...] + r3_ref[...])
    rows_ref[...] = rows
    out_ref[...] = dot3(split(rows), (oh_ref[...], ol_ref[...]))


def sample_sums(noise_ref, place, acid, sums):
    sum_u, sum_q, sum_qu = sums
    quarter = 0.25 * acid
    base = acid - 2.0
    for index in range(noise_ref.shape[0]):
        noise = noise_ref[(index,) + place].astype(F32)
        u = jnp.tanh(quarter * noise + base)
        q = (1.0 - u * u) * (1.0 + 0.25 * noise)
        sum_u, sum_q, sum_qu = sum_u + u, sum_q + q, sum_qu + q * u
    return sum_u, sum_q, sum_qu


def places(columns):
    width = min(columns, LANES)
    for row in range(0, ROWS, 16):
        for col in range(0, columns, width):
            yield slice(row, row + 16), slice(col, col + width)


def dose_first_body(_, own_ref, other_ref, ch_ref, cl_ref, noise_ref, sums_ref, edge_ref):
    step = pl.program_id(0)
    last = pl.num_programs(0) - 1
    sums_ref[0] = own_ref[...]

    @pl.when(step == 0)
    def _():
        edge_ref[...] = dot3(split(other_ref[...]), (ch_ref[0], cl_ref[0]))
        sums_ref[0, :, :EDGE] += edge_ref[:, :EDGE]

    @pl.when(step == last)
    def _():
        sums_ref[0, :, CHUNK - EDGE :] += edge_ref[:, EDGE:]

    for place in places(CHUNK):
        acid = sums_ref[(0,) + place]
        zero = jnp.zeros(acid.shape, F32)
        for index, value in enumerate(sample_sums(noise_ref, place, acid, (zero, zero, zero))):
            sums_ref[(index + 1,) + place] = value


def acid_grads(sums_ref, target_ref, noise_ref, grad_ref):
    for place in places(grad_ref.shape[1]):
        acid, *sums = [sums_ref[(index,) + place] for index in range(4)]
        sum_u, sum_q, sum_qu = sample_sums(noise_ref, place, acid, sums)
        target = target_ref[place].astype(F32)
        inner = 0.25 - sum_u * (1.0 / SAMPLES) - 0.5 * target
        grad_ref[place] = (1.0 / 16.0) * (sum_q * inner + 1.25 * sum_qu)


def dose_edge_body(_, sums_ref, target_ref, noise_ref, ch_ref, cl_ref, send_ref, grad_ref):
    acid_grads(sums_ref, target_ref, noise_ref, grad_ref)
    part = dot3(split(grad_ref[...]), (ch_ref[0], cl_ref[0]))

    @pl.when(pl.program_id(0) == 0)
    def _():
        send_ref[...] = part

    @pl.when(pl.program_id(0) > 0)
    def _():
        send_ref[...] += part


def dose_body(sums_ref, target_ref, noise_ref, oh_ref, ol_ref, out_ref, grad_ref):
    acid_grads(sums_ref, target_ref, noise_ref, grad_ref)
    part = dot3(split(grad_ref[...]), (oh_ref[...], ol_ref[...]))

    @pl.when(pl.program_id(0) == 0)
    def _():
        out_ref[...] = part

    @pl.when(pl.program_id(0) > 0)
    def _():
        out_ref[...] += part


def back_body(place_ref, weight_ref, p0_ref, p1_ref, p2_ref, p3_ref, field_ref, kern_ref, *refs):
    wh_ref, wl_ref, gh_ref, gl_ref, blur_ref, th_ref, tl_ref, fold_ref, coef_ref = refs[:9]
    out_ref, rows_ref, grad_ref, sum_ref, table, table_sems = refs[9:]
    step = pl.program_id(0)
    fetches = [
        pltpu.make_async_copy(ref, table.at[index], table_sems.at[index])
        for index, ref in enumerate((th_ref, tl_ref))
    ]

    @pl.when(step == 0)
    def _():
        for fetch in fetches:
            fetch.start()
        for shift, piece_ref in enumerate((p0_ref, p1_ref, p2_ref, p3_ref)):
            group = lax.rem(place_ref[0] - shift + KERN, KERN)
            rows_ref[pl.ds(pl.multiple_of(group * ROWS, ROWS), ROWS)] = piece_ref[...]
        part = 2.0 * dot3(split(blur_ref[...]), split(rows_ref[...]))
        grad_ref[:, :COARSE] = part
        grad_ref[:, COARSE:] = part
        sum_ref[...] = jnp.zeros_like(sum_ref)

    grad = grad_ref[...]
    half = KERN * REACH
    pulled = jnp.concatenate(
        [
            field_ref[index * half : (index + 1) * half] * (weight_ref[2 * step + index] * grad)
            for index in range(2)
        ],
        0,
    )
    lefts = dot3(split(pulled), (gh_ref[...], gl_ref[...]))
    stack = []
    for index in range(2):
        column = []
        for group in range(KERN):
            first = index * half + group * REACH
            left = lefts[first : first + REACH]
            column += [left[:, :FREQ], left[:, FREQ:]]
        stack.append(jnp.concatenate(column, 0))
    near = dot3((wh_ref[0], wl_ref[0]), split(jnp.concatenate(stack, 1)))
    sum_re = sum_ref[:FREQ]
    sum_im = sum_ref[FREQ:]
    for index in range(2):
        near_re = near[:FREQ, index * FREQ : (index + 1) * FREQ]
        near_im = near[FREQ:, index * FREQ : (index + 1) * FREQ]
        kern_re, kern_im = kern_ref[index, 0], kern_ref[index, 1]
        sum_re = sum_re + (kern_re * near_re + kern_im * near_im)
        sum_im = sum_im + (kern_re * near_im - kern_im * near_re)
    sum_ref[:FREQ] = sum_re
    sum_ref[FREQ:] = sum_im

    @pl.when(step == pl.num_programs(0) - 1)
    def _():
        grad_re, grad_im = sum_re * (2.0 / PERIOD), sum_im * (2.0 / PERIOD)
        mix = jnp.concatenate(
            [jnp.concatenate([grad_re, -grad_im], 1), jnp.concatenate([-grad_im, -grad_re], 1)], 0
        )
        folded = dot_exact(split(mix), fold_ref[...])
        coef_re, coef_im = coef_ref[0], coef_ref[1]
        by_cos, by_sin = grad_im[:, :1], grad_re[:, :1]
        spare_cos = coef_re * by_cos + coef_im * by_sin
        spare_sin = coef_re * by_sin - coef_im * by_cos
        mixed = jnp.concatenate([folded, spare_cos, spare_sin], 0)
        for fetch in fetches:
            fetch.wait()
        spread = dot3((table[0], table[1]), split(mixed))
        out_ref[...] = spread.reshape(out_ref.shape)


def final_body(got_ref, basis_ref, wh_ref, wl_ref, last_ref, out_ref):
    total = got_ref[0]
    for index in range(1, got_ref.shape[0]):
        total = total + got_ref[index]
    basis = basis_ref[...]
    rows = dot3(split(basis[:, :RANK]), split(total))
    spare = jnp.sum(basis * total[RANK - 1 :], 1, keepdims=True)
    out_ref[...] = dot3(split(rows), (wh_ref[...], wl_ref[...])) + spare * last_ref[...]


def to_const(table):
    return hbm(*(jnp.asarray(part) for part in np_split(table)))


def shifted(values, shifts):
    count = lax.axis_size("kern")
    return [
        lax.ppermute(value, "kern", [(source, (source + shift) % count) for source in range(count)])
        for value, shift in zip(values, shifts)
    ]


def body(mask_values, kernels, weights, target, dose_noise):
    noise_count = lax.axis_size("noise")
    f32 = lambda *shape: jax.ShapeDtypeStruct(shape, F32)
    bf16 = lambda *shape: jax.ShapeDtypeStruct(shape, BF)
    smem = pl.BlockSpec(memory_space=pltpu.SMEM)
    columns = PERIOD // CHUNK
    shifts = range(1, KERN)

    def fixed(*shape):
        return pl.BlockSpec(shape, lambda i, *_: (0,) * len(shape))

    def chunk(rows):
        return pl.BlockSpec((rows, CHUNK), lambda i, *_: (0, i))

    def moved_spec(width):
        return pl.BlockSpec((noise_count // columns, ROWS, width), lambda i: (i, 0, 0))

    moved_first, moved = call(
        front_body,
        (bf16(noise_count, ROWS, PERIOD + FREQ), bf16(noise_count, ROWS, PERIOD)),
        (mask_values, jnp.asarray(BASIS.T[:RANK], F32), *to_const(LINE.T), jnp.asarray(LAST, F32), dose_noise),
        grid=(columns,),
        in_specs=[fixed(ROWS, PERIOD), fixed(RANK, ROWS)]
        + [fixed(PERIOD, FREQ)] * 2
        + [fixed(1, PERIOD), pl.BlockSpec((2, dose_noise.shape[1] // columns, PERIOD), lambda i: (0, i, 0))],
        out_specs=(moved_spec(PERIOD + FREQ), moved_spec(PERIOD)),
        scratch_shapes=[pltpu.VMEM((2 * RANK, FREQ), BF)],
    )
    place = jnp.stack([lax.axis_index(axis).astype(jnp.int32) for axis in ("kern", "noise", "tile")])
    moved_first, place = lax.optimization_barrier((moved_first, place))
    got = lax.all_to_all(moved_first, "noise", 0, 0, tiled=True)
    got, moved, kernels, weights, target, place = lax.optimization_barrier(
        (got, moved, kernels, weights, target, place)
    )
    got_last = lax.all_to_all(moved, "noise", 0, 0, tiled=True)

    def at_place(which, table):
        return [pl.BlockSpec((1,) + table.shape[1:], lambda i, place: (place[which], 0, 0))] * 2

    waves_t = WAVE.transpose(0, 2, 1)
    cross_t = CROSS.transpose(0, 2, 1)
    coef = hbm(jnp.asarray(COEF, F32))
    spec = call(
        spectrum_body,
        f32(2 * FREQ, FREQ),
        (got, *to_const(GATHER_OWN), *hbm(jnp.asarray(UNFOLD, BF)), *coef),
        place=place,
        grid=(1,),
        in_specs=[pl.BlockSpec((noise_count, ROWS, FREQ), lambda i, _: (0, 0, PERIOD // FREQ))]
        + at_place(0, GATHER_OWN)
        + [fixed(*UNFOLD.shape), fixed(*COEF.shape)],
        out_specs=fixed(2 * FREQ, FREQ),
    )
    specs = [spec] + shifted([spec] * len(shifts), shifts)
    pair_spec = pl.BlockSpec((2, 2, FREQ, FREQ), lambda i, *_: (i, 0, 0, 0))
    field_rows = 2 * KERN * REACH
    field_spec = pl.BlockSpec((field_rows, 2 * COARSE), lambda i, *_: (i, 0))
    field, *pieces = call(
        field_body,
        (f32(PAIRS * field_rows, 2 * COARSE),) + (f32(ROWS, COARSE),) * KERN,
        (weights, *specs, *hbm(kernels), *to_const(WAVE), *to_const(GRID), *hbm(jnp.asarray(BLUR, F32))),
        place=place,
        grid=(PAIRS,),
        in_specs=[smem]
        + [fixed(2 * FREQ, FREQ)] * KERN
        + [pair_spec]
        + at_place(1, WAVE)
        + [fixed(*GRID.shape)] * 2
        + [fixed(*BLUR.shape)],
        out_specs=(field_spec,) + (fixed(ROWS, COARSE),) * KERN,
        scratch_shapes=[
            pltpu.VMEM((2 * FREQ, FREQ), F32),
            pltpu.VMEM((KERN * REACH, COARSE), F32),
            pltpu.VMEM((KERN * ROWS, COARSE), F32),
        ],
    )
    pieces = pieces[:1] + shifted(pieces[1:], shifts)
    acid, rows = call(own_body, (f32(ROWS, PERIOD), f32(ROWS, COARSE)), (*pieces, *to_const(OWN.T)))
    swap = [(0, 1), (1, 0)]
    rows_other = lax.ppermute(rows, "tile", swap)
    got_spec = pl.BlockSpec((noise_count, ROWS, CHUNK), lambda i, *_: (0, 0, i))
    sums = call(
        dose_first_body,
        f32(4, ROWS, PERIOD),
        (acid, rows_other, *to_const(CROSS), got),
        place=place,
        grid=(columns,),
        in_specs=[chunk(ROWS), fixed(ROWS, COARSE)] + at_place(2, CROSS) + [got_spec],
        out_specs=pl.BlockSpec((4, ROWS, CHUNK), lambda i, *_: (0, 0, i)),
        scratch_shapes=[pltpu.VMEM((ROWS, 2 * EDGE), F32)],
    )
    far = PERIOD // EDGE - 1
    (target,) = hbm(target)
    (sums,) = vmem(sums)
    send = call(
        dose_edge_body,
        f32(ROWS, COARSE),
        (sums, target, got_last, *to_const(cross_t)),
        place=place,
        grid=(2,),
        in_specs=[
            pl.BlockSpec((4, ROWS, EDGE), lambda i, _: (0, 0, i * far)),
            pl.BlockSpec((ROWS, EDGE), lambda i, _: (0, i * far)),
            pl.BlockSpec((noise_count, ROWS, EDGE), lambda i, _: (0, 0, i * far)),
        ]
        + [pl.BlockSpec((1, EDGE, COARSE), lambda i, place: (place[2], i, 0))] * 2,
        out_specs=fixed(ROWS, COARSE),
        scratch_shapes=[pltpu.VMEM((ROWS, EDGE), F32)],
    )
    grad_other = lax.ppermute(send, "tile", swap)
    grad_own = call(
        dose_body,
        f32(ROWS, COARSE),
        (sums, target, got_last, *to_const(OWN)),
        grid=(columns,),
        in_specs=[pl.BlockSpec((4, ROWS, CHUNK), lambda i: (0, 0, i)), chunk(ROWS), got_spec]
        + [pl.BlockSpec((CHUNK, COARSE), lambda i: (i, 0))] * 2,
        out_specs=fixed(ROWS, COARSE),
        scratch_shapes=[pltpu.VMEM((ROWS, CHUNK), F32)],
    )
    grad = grad_own + grad_other
    grads = [grad] + shifted([grad] * len(shifts), shifts)
    spread = call(
        back_body,
        f32(BLOCKS, RANK, FREQ),
        (
            weights,
            *grads,
            *vmem(field),
            *hbm(kernels),
            *to_const(waves_t),
            *to_const(GRID.T),
            *hbm(jnp.asarray(BLUR.T, F32)),
            *to_const(GATHER.T),
            *hbm(jnp.asarray(UNFOLD.T, BF)),
            *coef,
        ),
        place=place,
        grid=(PAIRS,),
        in_specs=[smem]
        + [fixed(ROWS, COARSE)] * KERN
        + [field_spec, pair_spec]
        + at_place(1, waves_t)
        + [fixed(*GRID.T.shape)] * 2
        + [fixed(*BLUR.T.shape)]
        + [pl.BlockSpec(memory_space=pltpu.HBM)] * 2
        + [fixed(*UNFOLD.T.shape), fixed(*COEF.shape)],
        out_specs=fixed(BLOCKS, RANK, FREQ),
        scratch_shapes=[
            pltpu.VMEM((KERN * ROWS, COARSE), F32),
            pltpu.VMEM((KERN * REACH, 2 * COARSE), F32),
            pltpu.VMEM((2 * FREQ, FREQ), F32),
            pltpu.VMEM((2,) + GATHER.T.shape, BF),
            pltpu.SemaphoreType.DMA((2,)),
        ],
    )
    back = lax.all_to_all(spread, ("kern", "noise"), 0, 0, tiled=True)
    return call(
        final_body,
        f32(ROWS, PERIOD),
        (back, jnp.asarray(BASIS, F32), *to_const(LINE), jnp.asarray(LAST, F32)),
    )


def solution(mesh):
    return jax.shard_map(
        body,
        mesh=mesh,
        in_specs=(
            P(("kern", "noise"), "tile"),
            P("kern", None, None, None),
            P("kern"),
            P(("kern", "noise"), "tile"),
            P("noise", "kern", "tile"),
        ),
        out_specs=P(("kern", "noise"), "tile"),
        check_vma=False,
    )
```

```python
import math

import jax
import jax.numpy as jnp
import numpy as np
from jax import lax
from jax.experimental import pallas as pl
from jax.experimental.pallas import tpu as pltpu
from jax.sharding import PartitionSpec as P

HALO = 16
FREQ = 128
COARSE = 256
PERIOD = 2048
ROWS = 32
REACH = ROWS + 2 * HALO
EDGE = 128
GROUP = 6
PAIRS = GROUP // 2
KERN = 4
SAMPLES = 32
RANK = 16
MIB = 32
BF = jnp.bfloat16
F32 = jnp.float32


def np_split(table):
    table = np.asarray(table, np.float32)
    high = table.astype(jnp.bfloat16)
    low = (table - high.astype(np.float32)).astype(jnp.bfloat16)
    return high, low


def np_waves(ids):
    centred = np.arange(FREQ) - FREQ // 2
    angles = 2.0 * np.pi * ((centred[:, None] * ids[None, :]) % PERIOD) / PERIOD
    return np.cos(angles), np.sin(angles)


def line_tables():
    half = FREQ // 2
    pixels = np.arange(PERIOD)
    angle = lambda f: 2.0 * np.pi * ((f[:, None] * pixels[None, :]) % PERIOD) / PERIOD
    line = np.concatenate([np.cos(angle(np.arange(half + 1))), np.sin(angle(np.arange(1, half)))], 0)
    last = np.sin(angle(np.array([half])))
    unfold = np.zeros((FREQ, 2 * FREQ))
    for j in range(FREQ):
        f = j - half
        unfold[abs(f), j] = 1.0
        if 0 < abs(f) < half:
            unfold[half + abs(f), FREQ + j] = np.sign(f)
    row = np.arange(ROWS) - (ROWS - 1) / 2.0
    fine = np.arange(-half, half + 0.01, 0.25)
    wave = np.exp(2j * np.pi * np.outer(row, fine) / PERIOD)
    basis = np.linalg.svd(np.concatenate([wave.real, wave.imag], 1))[0][:, : RANK - 1]
    basis = np.concatenate([basis, np.zeros((ROWS, FREQ - RANK + 1))], 1)
    freqs = np.arange(FREQ) - half
    coef = np.exp(2j * np.pi * np.outer(freqs, row) / PERIOD) @ basis
    blocks = PERIOD // ROWS
    centre = ROWS * np.arange(blocks) + (ROWS - 1) / 2.0
    phase = np.exp(2j * np.pi * np.outer(freqs, centre) / PERIOD)
    rows = phase[:, :, None] * coef[:, None, :RANK]
    rows[:, :, RANK - 1] = 0.0
    spare = np.zeros_like(rows)
    spare[:, :, RANK - 1] = phase
    rows = rows.reshape(FREQ, blocks * RANK)
    spare = spare.reshape(FREQ, blocks * RANK)
    gather = np.concatenate([rows.real, rows.imag, spare.real, spare.imag], 0)
    return line, last, unfold, basis, np.stack([coef.real, coef.imag]), gather


def tables():
    cos, sin = np_waves(np.arange(PERIOD))
    reach = np.zeros((PERIOD + 2 * HALO, 4 * FREQ))
    reach[HALO:-HALO] = np.concatenate([cos, -sin, sin, cos], 0).T
    ccos, csin = np_waves(np.arange(COARSE) * (PERIOD // COARSE))
    grid = np.block([[ccos, csin], [-csin, ccos]]) / FREQ
    offsets = np.arange(-HALO, HALO + 1)
    taps = np.exp(-(offsets.astype(np.float64) ** 2) / (2.0 * (HALO / 2.0) ** 2))
    taps = taps / taps.sum()
    row_blur = np.zeros((ROWS, REACH))
    for row in range(ROWS):
        row_blur[row, row : row + 2 * HALO + 1] = taps
    shift = np.arange(PERIOD)[:, None] - (PERIOD // COARSE) * np.arange(COARSE)[None, :]
    freqs = np.arange(1, FREQ)
    line = (1.0 + 2.0 * np.cos(2.0 * np.pi * np.outer(np.arange(PERIOD), freqs) / PERIOD).sum(1)) / COARSE
    interp = line[shift % PERIOD]
    padded = np.zeros((PERIOD + 2 * HALO, COARSE))
    padded[HALO:-HALO] = interp
    own = np.zeros((PERIOD, COARSE))
    for index, tap in enumerate(taps):
        own += tap * padded[index : index + PERIOD]
    cross = np.zeros((2, COARSE, 2 * EDGE))
    for column in range(HALO):
        for index, offset in enumerate(offsets):
            if column + offset < 0:
                cross[1, :, column] += taps[index] * interp[PERIOD + column + offset]
            place = PERIOD - 1 - column + offset
            if place >= PERIOD:
                cross[0, :, 2 * EDGE - 1 - column] += taps[index] * interp[place - PERIOD]
    return reach, grid, row_blur, own, cross


LINE, LAST, UNFOLD, BASIS, COEF, GATHER = line_tables()
REACH_WAVES, GRID, ROW_BLUR, OWN, CROSS = tables()
BLOCKS = PERIOD // ROWS
GROUP_BLOCKS = BLOCKS // KERN
WAVE = np.stack(
    [
        np.concatenate([part[:, : 2 * FREQ], part[:, 2 * FREQ :]], 0)
        for part in (REACH_WAVES[first : first + REACH] for first in range(0, PERIOD, ROWS))
    ]
)
WAVE = WAVE.reshape(KERN, GROUP_BLOCKS, 2 * REACH, 2 * FREQ).transpose(1, 0, 2, 3)
WAVE = WAVE.reshape(GROUP_BLOCKS, KERN * 2 * REACH, 2 * FREQ)
LOW = 4
HIGH = RANK - LOW
SPREAD = GATHER.reshape(4 * FREQ, BLOCKS, RANK)
SPREAD = np.concatenate([SPREAD[:, :, : HIGH - 1], SPREAD[:, :, RANK - 1 :], SPREAD[:, :, :LOW]], 2)
SPREAD = SPREAD.reshape(4 * FREQ, BLOCKS * RANK).T
BASIS_BACK = np.concatenate([BASIS[:, : HIGH - 1], np.zeros((ROWS, 1)), BASIS[:, :LOW]], 1)
GATHER_OWN = GATHER.reshape(4 * FREQ, KERN, GROUP_BLOCKS * RANK).transpose(1, 0, 2)
BLUR = np.kron(np.eye(KERN), ROW_BLUR)


def split(value):
    high = value.astype(BF)
    return high, (value - high.astype(F32)).astype(BF)


NN = (((1,), (0,)), ((), ()))


def dot3(left, right):
    lh, ll = left
    rh, rl = right

    def one(a, b):
        return lax.dot_general(a, b, NN, preferred_element_type=F32)

    count = lh.shape[0]
    if count > 64:
        return one(lh, rh) + (one(lh, rl) + one(ll, rh))
    both = one(jnp.concatenate([lh, ll], 0), rh)
    return both[:count] + (one(lh, rl) + both[count:])


def dot_exact(left, right):
    high, low = left
    return jnp.dot(high, right, preferred_element_type=F32) + jnp.dot(low, right, preferred_element_type=F32)


def call(body, out_shape, args, place=None, **kw):
    params = pltpu.CompilerParams(vmem_limit_bytes=MIB * 1024 * 1024)
    if place is None:
        return pl.pallas_call(body, out_shape=out_shape, compiler_params=params, **kw)(*args)
    grid_spec = pltpu.PrefetchScalarGridSpec(num_scalar_prefetch=1, **kw)
    return pl.pallas_call(body, out_shape=out_shape, compiler_params=params, grid_spec=grid_spec)(place, *args)


def hbm(*values):
    return tuple(pltpu.with_memory_space_constraint(value, pltpu.HBM) for value in values)


def vmem(*values):
    return tuple(pltpu.with_memory_space_constraint(value, pltpu.VMEM) for value in values)


CHUNK = 512
LANES = 256


def front_body(mask_ref, basis_ref, lh_ref, ll_ref, last_ref, noise_ref, first_ref, second_ref, packed_ref):
    @pl.when(pl.program_id(0) == 0)
    def _():
        transmit = (2.0 * mask_ref[...] - 1.0) * (1.0 / PERIOD)
        rows = dot3(split(basis_ref[...]), split(transmit))
        part = dot3(split(rows), (lh_ref[...], ll_ref[...]))
        row = lax.broadcasted_iota(jnp.int32, (RANK, FREQ), 0)
        lane = lax.broadcasted_iota(jnp.int32, (RANK, FREQ), 1)
        apart = jnp.sum(rows * last_ref[...], 1, keepdims=True)
        apart = jnp.sum(jnp.where(row == lane, apart, 0.0), 0, keepdims=True)
        high, low = split(jnp.where(row == RANK - 1, apart, part))
        packed_ref[:RANK] = high
        packed_ref[RANK:] = low

    for which in range(first_ref.shape[0]):
        rows = slice(which * ROWS, (which + 1) * ROWS)
        first_ref[which, :, :PERIOD] = noise_ref[0, rows]
        first_ref[which, :, PERIOD:] = packed_ref[...]
        second_ref[which] = noise_ref[1, rows]


def spectrum_body(_, got_ref, gh_ref, gl_ref, unfold_ref, coef_ref, out_ref):
    high = got_ref[:, :RANK].reshape(GROUP_BLOCKS * RANK, FREQ)
    low = got_ref[:, RANK:].reshape(GROUP_BLOCKS * RANK, FREQ)
    both = dot3((gh_ref[0], gl_ref[0]), (high, low))
    waves = dot_exact(split(both[: 2 * FREQ]), unfold_ref[...])
    spare_cos, spare_sin = both[2 * FREQ : 3 * FREQ], both[3 * FREQ :]
    coef_re, coef_im = coef_ref[0], coef_ref[1]
    last_cos = jnp.sum(coef_re * spare_cos - coef_im * spare_sin, 1, keepdims=True)
    last_sin = jnp.sum(coef_re * spare_sin + coef_im * spare_cos, 1, keepdims=True)
    first = lax.broadcasted_iota(jnp.int32, (FREQ, FREQ), 1) == 0
    cos_cos, cos_sin = waves[:FREQ, :FREQ], waves[:FREQ, FREQ:]
    sin_cos, sin_sin = waves[FREQ:, :FREQ], waves[FREQ:, FREQ:]
    out_ref[:FREQ] = cos_cos - sin_sin + jnp.where(first, last_sin, 0.0)
    out_ref[FREQ:] = jnp.where(first, last_cos, 0.0) - cos_sin - sin_cos


def field_body(place_ref, weight_ref, s0_ref, s1_ref, s2_ref, s3_ref, kern_ref, *refs):
    wh_ref, wl_ref, gh_ref, gl_ref, blur_ref, field_ref = refs[:6]
    piece_refs, (spec_ref, total_ref, rows_ref) = refs[6 : 6 + KERN], refs[6 + KERN :]
    step = pl.program_id(0)

    @pl.when(step == 0)
    def _():
        spec_ref[...] = (s0_ref[...] + s1_ref[...]) + (s2_ref[...] + s3_ref[...])

    spec_re = spec_ref[:FREQ]
    spec_im = spec_ref[FREQ:]
    near_re, near_im = [], []
    for index in range(2):
        kern_re, kern_im = kern_ref[index, 0], kern_ref[index, 1]
        near_re.append(kern_re * spec_re - kern_im * spec_im)
        near_im.append(kern_re * spec_im + kern_im * spec_re)
    near = jnp.concatenate([jnp.concatenate(near_re, 1), jnp.concatenate(near_im, 1)], 0)
    left = dot3((wh_ref[0], wl_ref[0]), split(near))
    lefts = []
    for index in range(2):
        lanes = slice(index * FREQ, (index + 1) * FREQ)
        for group in range(KERN):
            first = 2 * group * REACH
            re, im = left[first : first + REACH, lanes], left[first + REACH : first + 2 * REACH, lanes]
            lefts.append(jnp.concatenate([re, im], 1))
    field = dot3(split(jnp.concatenate(lefts, 0)), (gh_ref[...], gl_ref[...]))
    field_ref[...] = field
    power = field * field
    power = power[:, :COARSE] + power[:, COARSE:]
    half = KERN * REACH
    total = weight_ref[2 * step] * power[:half] + weight_ref[2 * step + 1] * power[half:]

    @pl.when(step == 0)
    def _():
        total_ref[...] = total

    @pl.when(step > 0)
    def _():
        total_ref[...] += total

    @pl.when(step == pl.num_programs(0) - 1)
    def _():
        rows_ref[...] = dot3(split(blur_ref[...]), split(total_ref[...]))
        for shift, piece_ref in enumerate(piece_refs):
            group = lax.rem(place_ref[0] + shift, KERN)
            piece_ref[...] = rows_ref[pl.ds(pl.multiple_of(group * ROWS, ROWS), ROWS)]


def sample_sums(noise_ref, place, acid, sums):
    sum_u, sum_q, sum_qu = sums
    quarter = 0.25 * acid
    base = acid - 2.0
    for index in range(noise_ref.shape[0]):
        noise = noise_ref[(index,) + place].astype(F32)
        u = jnp.tanh(quarter * noise + base)
        q = (1.0 - u * u) * (1.0 + 0.25 * noise)
        sum_u, sum_q, sum_qu = sum_u + u, sum_q + q, sum_qu + q * u
    return sum_u, sum_q, sum_qu


def places(columns):
    width = min(columns, LANES)
    for row in range(0, ROWS, 16):
        for col in range(0, columns, width):
            yield slice(row, row + 16), slice(col, col + width)


def dose_first_body(rows_ref, oh_ref, ol_ref, noise_ref, sums_ref):
    sums_ref[0] = dot3(split(rows_ref[...]), (oh_ref[...], ol_ref[...]))
    for place in places(CHUNK):
        acid = sums_ref[(0,) + place]
        zero = jnp.zeros(acid.shape, F32)
        for index, value in enumerate(sample_sums(noise_ref, place, acid, (zero, zero, zero))):
            sums_ref[(index + 1,) + place] = value


def acid_grad(sums, target):
    sum_u, sum_q, sum_qu = sums
    inner = 0.25 - sum_u * (1.0 / SAMPLES) - 0.5 * target.astype(F32)
    return (1.0 / 16.0) * (sum_q * inner + 1.25 * sum_qu)


def dose_edge_body(
    _, acid_ref, other_ref, target_ref, first_ref, second_ref, ch_ref, cl_ref, th_ref, tl_ref, grad_ref, send_ref
):
    halo = dot3(split(other_ref[...]), (ch_ref[0], cl_ref[0]))
    for place in places(EDGE):
        acid = acid_ref[(0,) + place] + halo[place]
        zero = jnp.zeros(acid.shape, F32)
        sums = sample_sums(first_ref, place, acid, (zero, zero, zero))
        sums = sample_sums(second_ref, place, acid, sums)
        grad_ref[place] = acid_grad(sums, target_ref[place])
    part = dot3(split(grad_ref[...]), (th_ref[0], tl_ref[0]))

    @pl.when(pl.program_id(0) == 0)
    def _():
        send_ref[...] = part

    @pl.when(pl.program_id(0) > 0)
    def _():
        send_ref[...] += part


def dose_body(sums_ref, edge_ref, target_ref, noise_ref, oh_ref, ol_ref, out_ref, grad_ref):
    step = pl.program_id(0)
    for place in places(CHUNK):
        acid, *sums = [sums_ref[(index,) + place] for index in range(4)]
        sums = sample_sums(noise_ref, place, acid, sums)
        grad_ref[place] = acid_grad(sums, target_ref[place])

    @pl.when(step == 0)
    def _():
        grad_ref[:, :EDGE] = edge_ref[:, :EDGE]

    @pl.when(step == pl.num_programs(0) - 1)
    def _():
        grad_ref[:, CHUNK - EDGE :] = edge_ref[:, EDGE:]

    part = dot3(split(grad_ref[...]), (oh_ref[...], ol_ref[...]))

    @pl.when(step == 0)
    def _():
        out_ref[...] = part

    @pl.when(step > 0)
    def _():
        out_ref[...] += part


def back_body(place_ref, weight_ref, p0_ref, p1_ref, p2_ref, p3_ref, field_ref, kern_ref, *refs):
    wh_ref, wl_ref, gh_ref, gl_ref, blur_ref, th_ref, tl_ref, fold_ref, coef_ref = refs[:9]
    out_ref, rows_ref, grad_ref, sum_ref, table, table_sems = refs[9:]
    step = pl.program_id(0)
    fetches = [
        pltpu.make_async_copy(ref, table.at[index], table_sems.at[index])
        for index, ref in enumerate((th_ref, tl_ref))
    ]

    @pl.when(step == 0)
    def _():
        for fetch in fetches:
            fetch.start()
        for shift, piece_ref in enumerate((p0_ref, p1_ref, p2_ref, p3_ref)):
            group = lax.rem(place_ref[0] - shift + KERN, KERN)
            rows_ref[pl.ds(pl.multiple_of(group * ROWS, ROWS), ROWS)] = piece_ref[...]
        part = 2.0 * dot3(split(blur_ref[...]), split(rows_ref[...]))
        grad_ref[:, :COARSE] = part
        grad_ref[:, COARSE:] = part
        sum_ref[...] = jnp.zeros_like(sum_ref)

    grad = grad_ref[...]
    half = KERN * REACH
    pulled = jnp.concatenate(
        [
            field_ref[index * half : (index + 1) * half] * (weight_ref[2 * step + index] * grad)
            for index in range(2)
        ],
        0,
    )
    lefts = dot3(split(pulled), (gh_ref[...], gl_ref[...]))
    stack = []
    for index in range(2):
        column = []
        for group in range(KERN):
            first = index * half + group * REACH
            left = lefts[first : first + REACH]
            column += [left[:, :FREQ], left[:, FREQ:]]
        stack.append(jnp.concatenate(column, 0))
    near = dot3((wh_ref[0], wl_ref[0]), split(jnp.concatenate(stack, 1)))
    sum_re = sum_ref[:FREQ]
    sum_im = sum_ref[FREQ:]
    for index in range(2):
        near_re = near[:FREQ, index * FREQ : (index + 1) * FREQ]
        near_im = near[FREQ:, index * FREQ : (index + 1) * FREQ]
        kern_re, kern_im = kern_ref[index, 0], kern_ref[index, 1]
        sum_re = sum_re + (kern_re * near_re + kern_im * near_im)
        sum_im = sum_im + (kern_re * near_im - kern_im * near_re)
    sum_ref[:FREQ] = sum_re
    sum_ref[FREQ:] = sum_im

    @pl.when(step == pl.num_programs(0) - 1)
    def _():
        grad_re, grad_im = sum_re * (2.0 / PERIOD), sum_im * (2.0 / PERIOD)
        mix = jnp.concatenate(
            [jnp.concatenate([grad_re, -grad_im], 1), jnp.concatenate([-grad_im, -grad_re], 1)], 0
        )
        folded = dot_exact(split(mix), fold_ref[...])
        coef_re, coef_im = coef_ref[0], coef_ref[1]
        by_cos, by_sin = grad_im[:, :1], grad_re[:, :1]
        spare_cos = coef_re * by_cos + coef_im * by_sin
        spare_sin = coef_re * by_sin - coef_im * by_cos
        mixed = jnp.concatenate([folded, spare_cos, spare_sin], 0)
        for fetch in fetches:
            fetch.wait()
        high, low = split(dot3((table[0], table[1]), split(mixed)).reshape(out_ref.shape))
        row = lax.broadcasted_iota(jnp.int32, out_ref.shape, 1)
        out_ref[...] = jnp.where(row < HIGH, high.astype(F32), low.astype(F32)).astype(BF)


def final_body(got_ref, back_ref, basis_ref, wh_ref, wl_ref, last_ref, out_ref):
    total = got_ref[0].astype(F32)
    for index in range(1, got_ref.shape[0]):
        total = total + got_ref[index].astype(F32)
    rows = dot3(split(back_ref[...]), split(total))
    spare = jnp.sum(basis_ref[...] * total[HIGH - 1 : HIGH], 1, keepdims=True)
    out_ref[...] = dot3(split(rows), (wh_ref[...], wl_ref[...])) + spare * last_ref[...]


def to_const(table):
    return hbm(*(jnp.asarray(part) for part in np_split(table)))


def shifted(values, shifts):
    count = lax.axis_size("kern")
    return [
        lax.ppermute(value, "kern", [(source, (source + shift) % count) for source in range(count)])
        for value, shift in zip(values, shifts)
    ]


def body(mask_values, kernels, weights, target, dose_noise):
    noise_count = lax.axis_size("noise")
    f32 = lambda *shape: jax.ShapeDtypeStruct(shape, F32)
    bf16 = lambda *shape: jax.ShapeDtypeStruct(shape, BF)
    smem = pl.BlockSpec(memory_space=pltpu.SMEM)
    columns = PERIOD // CHUNK
    shifts = range(1, KERN)

    def fixed(*shape):
        return pl.BlockSpec(shape, lambda i, *_: (0,) * len(shape))

    def chunk(rows):
        return pl.BlockSpec((rows, CHUNK), lambda i, *_: (0, i))

    def moved_spec(width):
        return pl.BlockSpec((noise_count // columns, ROWS, width), lambda i: (i, 0, 0))

    moved_first, moved = call(
        front_body,
        (pltpu.HBM((noise_count, ROWS, PERIOD + FREQ), BF), pltpu.HBM((noise_count, ROWS, PERIOD), BF)),
        hbm(mask_values, jnp.asarray(BASIS.T[:RANK], F32))
        + to_const(LINE.T)
        + hbm(jnp.asarray(LAST, F32), dose_noise),
        grid=(columns,),
        in_specs=[fixed(ROWS, PERIOD), fixed(RANK, ROWS)]
        + [fixed(PERIOD, FREQ)] * 2
        + [fixed(1, PERIOD), pl.BlockSpec((2, dose_noise.shape[1] // columns, PERIOD), lambda i: (0, i, 0))],
        out_specs=(moved_spec(PERIOD + FREQ), moved_spec(PERIOD)),
        scratch_shapes=[pltpu.VMEM((2 * RANK, FREQ), BF)],
    )
    place = jnp.stack([lax.axis_index(axis).astype(jnp.int32) for axis in ("kern", "noise", "tile")])
    moved_first, place = lax.optimization_barrier((moved_first, place))
    got = lax.all_to_all(moved_first, "noise", 0, 0, tiled=True)
    got, moved, kernels, weights, target, place = lax.optimization_barrier(
        (got, moved, kernels, weights, target, place)
    )
    got_last = lax.all_to_all(moved, "noise", 0, 0, tiled=True)

    def at_place(which, table):
        return [pl.BlockSpec((1,) + table.shape[1:], lambda i, place: (place[which], 0, 0))] * 2

    waves_t = WAVE.transpose(0, 2, 1)
    cross_t = CROSS.transpose(0, 2, 1)
    coef = hbm(jnp.asarray(COEF, F32))
    spec = call(
        spectrum_body,
        f32(2 * FREQ, FREQ),
        (got, *to_const(GATHER_OWN), *hbm(jnp.asarray(UNFOLD, BF)), *coef),
        place=place,
        grid=(1,),
        in_specs=[pl.BlockSpec((noise_count, ROWS, FREQ), lambda i, _: (0, 0, PERIOD // FREQ))]
        + at_place(0, GATHER_OWN)
        + [fixed(*UNFOLD.shape), fixed(*COEF.shape)],
        out_specs=fixed(2 * FREQ, FREQ),
    )
    specs = [spec] + shifted([spec] * len(shifts), shifts)
    pair_spec = pl.BlockSpec((2, 2, FREQ, FREQ), lambda i, *_: (i, 0, 0, 0))
    field_rows = 2 * KERN * REACH
    field_spec = pl.BlockSpec((field_rows, 2 * COARSE), lambda i, *_: (i, 0))
    field, *pieces = call(
        field_body,
        (pltpu.HBM((PAIRS * field_rows, 2 * COARSE), F32),) + (f32(ROWS, COARSE),) * KERN,
        (weights, *specs, *hbm(kernels), *to_const(WAVE), *to_const(GRID), *hbm(jnp.asarray(BLUR, F32))),
        place=place,
        grid=(PAIRS,),
        in_specs=[smem]
        + [fixed(2 * FREQ, FREQ)] * KERN
        + [pair_spec]
        + at_place(1, WAVE)
        + [fixed(*GRID.shape)] * 2
        + [fixed(*BLUR.shape)],
        out_specs=(field_spec,) + (fixed(ROWS, COARSE),) * KERN,
        scratch_shapes=[
            pltpu.VMEM((2 * FREQ, FREQ), F32),
            pltpu.VMEM((KERN * REACH, COARSE), F32),
            pltpu.VMEM((KERN * ROWS, COARSE), F32),
        ],
    )
    pieces = pieces[:1] + shifted(pieces[1:], shifts)
    rows = (pieces[0] + pieces[1]) + (pieces[2] + pieces[3])
    swap = [(0, 1), (1, 0)]
    rows_other = lax.ppermute(rows, "tile", swap)
    got_spec = pl.BlockSpec((noise_count, ROWS, CHUNK), lambda i: (0, 0, i))
    sums_spec = pl.BlockSpec((4, ROWS, CHUNK), lambda i: (0, 0, i))
    sums = call(
        dose_first_body,
        f32(4, ROWS, PERIOD),
        (rows, *to_const(OWN.T), got),
        grid=(columns,),
        in_specs=[fixed(ROWS, COARSE)] + [chunk(COARSE)] * 2 + [got_spec],
        out_specs=sums_spec,
    )
    far = PERIOD // EDGE - 1
    (target,) = hbm(target)
    (sums,) = vmem(sums)
    edge_spec = pl.BlockSpec((noise_count, ROWS, EDGE), lambda i, _: (0, 0, i * far))
    edges, send = call(
        dose_edge_body,
        (f32(ROWS, 2 * EDGE), f32(ROWS, COARSE)),
        (sums, rows_other, target, got, got_last, *to_const(CROSS), *to_const(cross_t)),
        place=place,
        grid=(2,),
        in_specs=[
            pl.BlockSpec((1, ROWS, EDGE), lambda i, _: (0, 0, i * far)),
            fixed(ROWS, COARSE),
            pl.BlockSpec((ROWS, EDGE), lambda i, _: (0, i * far)),
            edge_spec,
            edge_spec,
        ]
        + [pl.BlockSpec((1, COARSE, EDGE), lambda i, place: (place[2], 0, i))] * 2
        + [pl.BlockSpec((1, EDGE, COARSE), lambda i, place: (place[2], i, 0))] * 2,
        out_specs=(pl.BlockSpec((ROWS, EDGE), lambda i, _: (0, i)), fixed(ROWS, COARSE)),
    )
    grad_other = lax.ppermute(send, "tile", swap)
    grad_own = call(
        dose_body,
        f32(ROWS, COARSE),
        (sums, edges, target, got_last, *to_const(OWN)),
        grid=(columns,),
        in_specs=[sums_spec, fixed(ROWS, 2 * EDGE), chunk(ROWS), got_spec]
        + [pl.BlockSpec((CHUNK, COARSE), lambda i: (i, 0))] * 2,
        out_specs=fixed(ROWS, COARSE),
        scratch_shapes=[pltpu.VMEM((ROWS, CHUNK), F32)],
    )
    grad = grad_own + grad_other
    grads = [grad] + shifted([grad] * len(shifts), shifts)
    spread = call(
        back_body,
        bf16(BLOCKS, RANK, FREQ),
        (
            weights,
            *grads,
            *hbm(field, kernels),
            *to_const(waves_t),
            *to_const(GRID.T),
            *hbm(jnp.asarray(BLUR.T, F32)),
            *to_const(SPREAD),
            *hbm(jnp.asarray(UNFOLD.T, BF)),
            *coef,
        ),
        place=place,
        grid=(PAIRS,),
        in_specs=[smem]
        + [fixed(ROWS, COARSE)] * KERN
        + [field_spec, pair_spec]
        + at_place(1, waves_t)
        + [fixed(*GRID.T.shape)] * 2
        + [fixed(*BLUR.T.shape)]
        + [pl.BlockSpec(memory_space=pltpu.HBM)] * 2
        + [fixed(*UNFOLD.T.shape), fixed(*COEF.shape)],
        out_specs=fixed(BLOCKS, RANK, FREQ),
        scratch_shapes=[
            pltpu.VMEM((KERN * ROWS, COARSE), F32),
            pltpu.VMEM((KERN * REACH, 2 * COARSE), F32),
            pltpu.VMEM((2 * FREQ, FREQ), F32),
            pltpu.VMEM((2,) + SPREAD.shape, BF),
            pltpu.SemaphoreType.DMA((2,)),
        ],
    )
    back = lax.all_to_all(spread, ("kern", "noise"), 0, 0, tiled=True)
    return call(
        final_body,
        f32(ROWS, PERIOD),
        (back, jnp.asarray(BASIS_BACK, F32), jnp.asarray(BASIS, F32), *(jnp.asarray(t) for t in np_split(LINE)), jnp.asarray(LAST, F32)),
    )


def solution(mesh):
    return jax.shard_map(
        body,
        mesh=mesh,
        in_specs=(
            P(("kern", "noise"), "tile"),
            P("kern", None, None, None),
            P("kern"),
            P(("kern", "noise"), "tile"),
            P("noise", "kern", "tile"),
        ),
        out_specs=P(("kern", "noise"), "tile"),
        check_vma=False,
    )
```

```python
import math

import jax
import jax.numpy as jnp
import numpy as np
from jax import lax
from jax.experimental import pallas as pl
from jax.experimental.pallas import tpu as pltpu
from jax.sharding import PartitionSpec as P

HALO = 16
FREQ = 128
COARSE = 256
PERIOD = 2048
ROWS = 32
REACH = 24
EDGE = 128
GROUP = 6
PAIRS = GROUP // 2
KERN = 4
SAMPLES = 32
RANK = 16
MIB = 32
BF = jnp.bfloat16
F32 = jnp.float32


def np_split(table):
    table = np.asarray(table, np.float32)
    high = table.astype(jnp.bfloat16)
    low = (table - high.astype(np.float32)).astype(jnp.bfloat16)
    return high, low


def np_waves(ids):
    centred = np.arange(FREQ) - FREQ // 2
    angles = 2.0 * np.pi * ((centred[:, None] * ids[None, :]) % PERIOD) / PERIOD
    return np.cos(angles), np.sin(angles)


def line_tables():
    half = FREQ // 2
    pixels = np.arange(PERIOD)
    angle = lambda f: 2.0 * np.pi * ((f[:, None] * pixels[None, :]) % PERIOD) / PERIOD
    line = np.concatenate([np.cos(angle(np.arange(half + 1))), np.sin(angle(np.arange(1, half)))], 0)
    last = np.sin(angle(np.array([half])))
    unfold = np.zeros((FREQ, 2 * FREQ))
    for j in range(FREQ):
        f = j - half
        unfold[abs(f), j] = 1.0
        if 0 < abs(f) < half:
            unfold[half + abs(f), FREQ + j] = np.sign(f)
    row = np.arange(ROWS) - (ROWS - 1) / 2.0
    fine = np.arange(-half, half + 0.01, 0.25)
    wave = np.exp(2j * np.pi * np.outer(row, fine) / PERIOD)
    basis = np.linalg.svd(np.concatenate([wave.real, wave.imag], 1))[0][:, : RANK - 1]
    basis = np.concatenate([basis, np.zeros((ROWS, FREQ - RANK + 1))], 1)
    freqs = np.arange(FREQ) - half
    coef = np.exp(2j * np.pi * np.outer(freqs, row) / PERIOD) @ basis
    blocks = PERIOD // ROWS
    centre = ROWS * np.arange(blocks) + (ROWS - 1) / 2.0
    phase = np.exp(2j * np.pi * np.outer(freqs, centre) / PERIOD)
    rows = phase[:, :, None] * coef[:, None, :RANK]
    rows[:, :, RANK - 1] = 0.0
    spare = np.zeros_like(rows)
    spare[:, :, RANK - 1] = phase
    rows = rows.reshape(FREQ, blocks * RANK)
    spare = spare.reshape(FREQ, blocks * RANK)
    gather = np.concatenate([rows.real, rows.imag, spare.real, spare.imag], 0)
    return line, last, unfold, basis, np.stack([coef.real, coef.imag]), gather


def tables():
    ccos, csin = np_waves(np.arange(COARSE) * (PERIOD // COARSE))
    grid = np.block([[ccos, csin], [-csin, ccos]]) / FREQ
    offsets = np.arange(-HALO, HALO + 1)
    taps = np.exp(-(offsets.astype(np.float64) ** 2) / (2.0 * (HALO / 2.0) ** 2))
    taps = taps / taps.sum()
    nodes = np.cos(np.pi * (np.arange(REACH) + 0.5) / REACH) * (ROWS / 2 + HALO - 0.5) + (ROWS - 1) / 2.0
    freqs = np.arange(1 - FREQ, FREQ)
    at = lambda places: np.exp(2j * np.pi * np.outer(places, freqs) / PERIOD)
    both = lambda value: np.concatenate([value.real, value.imag], 1)
    row_blur = np.zeros((PERIOD // ROWS, ROWS, REACH))
    near = np.arange(-HALO, ROWS + HALO)
    full = np.zeros((ROWS, ROWS + 2 * HALO))
    for row in range(ROWS):
        full[row, row : row + 2 * HALO + 1] = taps
    for block in range(PERIOD // ROWS):
        inside = (near + block * ROWS >= 0) & (near + block * ROWS < PERIOD)
        wanted = both((full * inside) @ at(near))
        row_blur[block] = np.linalg.lstsq(both(at(nodes)).T, wanted.T, rcond=1e-12)[0].T
    places = ROWS * np.arange(PERIOD // ROWS)[:, None] + nodes[None, :]
    angles = 2.0 * np.pi * (places[:, :, None] * (np.arange(FREQ) - FREQ // 2)) / PERIOD
    cos, sin = np.cos(angles), np.sin(angles)
    reach = np.concatenate([np.concatenate([cos, -sin], 2), np.concatenate([sin, cos], 2)], 1)
    shift = np.arange(PERIOD)[:, None] - (PERIOD // COARSE) * np.arange(COARSE)[None, :]
    freqs = np.arange(1, FREQ)
    line = (1.0 + 2.0 * np.cos(2.0 * np.pi * np.outer(np.arange(PERIOD), freqs) / PERIOD).sum(1)) / COARSE
    interp = line[shift % PERIOD]
    padded = np.zeros((PERIOD + 2 * HALO, COARSE))
    padded[HALO:-HALO] = interp
    own = np.zeros((PERIOD, COARSE))
    for index, tap in enumerate(taps):
        own += tap * padded[index : index + PERIOD]
    cross = np.zeros((2, COARSE, 2 * EDGE))
    for column in range(HALO):
        for index, offset in enumerate(offsets):
            if column + offset < 0:
                cross[1, :, column] += taps[index] * interp[PERIOD + column + offset]
            place = PERIOD - 1 - column + offset
            if place >= PERIOD:
                cross[0, :, 2 * EDGE - 1 - column] += taps[index] * interp[place - PERIOD]
    return reach, grid, row_blur, own, cross


LINE, LAST, UNFOLD, BASIS, COEF, GATHER = line_tables()
REACH_WAVES, GRID, ROW_BLUR, OWN, CROSS = tables()
BLOCKS = PERIOD // ROWS
GROUP_BLOCKS = BLOCKS // KERN
WAVE = REACH_WAVES
WAVE = WAVE.reshape(KERN, GROUP_BLOCKS, 2 * REACH, 2 * FREQ).transpose(1, 0, 2, 3)
WAVE = WAVE.reshape(GROUP_BLOCKS, KERN * 2 * REACH, 2 * FREQ)
LOW = 4
HIGH = RANK - LOW
SPREAD = GATHER.reshape(4 * FREQ, BLOCKS, RANK)
SPREAD = np.concatenate([SPREAD[:, :, : HIGH - 1], SPREAD[:, :, RANK - 1 :], SPREAD[:, :, :LOW]], 2)
SPREAD = SPREAD.reshape(4 * FREQ, BLOCKS * RANK).T
BASIS_BACK = np.concatenate([BASIS[:, : HIGH - 1], np.zeros((ROWS, 1)), BASIS[:, :LOW]], 1)
GATHER_OWN = GATHER.reshape(4 * FREQ, KERN, GROUP_BLOCKS * RANK).transpose(1, 0, 2)
BLUR = np.zeros((GROUP_BLOCKS, KERN, ROWS, KERN, REACH))
for group in range(KERN):
    BLUR[:, group, :, group] = ROW_BLUR.reshape(KERN, GROUP_BLOCKS, ROWS, REACH)[group]
BLUR = BLUR.reshape(GROUP_BLOCKS, KERN * ROWS, KERN * REACH)


def split(value):
    high = value.astype(BF)
    return high, (value - high.astype(F32)).astype(BF)


NN = (((1,), (0,)), ((), ()))


def dot3(left, right):
    lh, ll = left
    rh, rl = right

    def one(a, b):
        return lax.dot_general(a, b, NN, preferred_element_type=F32)

    count = lh.shape[0]
    if count > 64:
        return one(jnp.concatenate([lh, ll, lh], 1), jnp.concatenate([rh, rh, rl], 0))
    both = one(jnp.concatenate([lh, ll], 0), rh)
    return both[:count] + (one(lh, rl) + both[count:])


def dot_exact(left, right):
    high, low = left
    return jnp.dot(high, right, preferred_element_type=F32) + jnp.dot(low, right, preferred_element_type=F32)


def call(body, out_shape, args, place=None, **kw):
    params = pltpu.CompilerParams(vmem_limit_bytes=MIB * 1024 * 1024)
    if place is None:
        return pl.pallas_call(body, out_shape=out_shape, compiler_params=params, **kw)(*args)
    grid_spec = pltpu.PrefetchScalarGridSpec(num_scalar_prefetch=1, **kw)
    return pl.pallas_call(body, out_shape=out_shape, compiler_params=params, grid_spec=grid_spec)(place, *args)


def hbm(*values):
    return tuple(pltpu.with_memory_space_constraint(value, pltpu.HBM) for value in values)


def vmem(*values):
    return tuple(pltpu.with_memory_space_constraint(value, pltpu.VMEM) for value in values)


CHUNK = 1024
LANES = 256
PARTS = 4


def front_body(mask_ref, basis_ref, lh_ref, ll_ref, last_ref, noise_ref, first_ref, second_ref, *scratch):
    mask, basis, lh, ll, last, first, second, sems = scratch
    tables = [
        pltpu.make_async_copy(source, target, sems.at[index])
        for index, (source, target) in enumerate(
            zip((mask_ref, basis_ref, lh_ref, ll_ref, last_ref), (mask, basis, lh, ll, last))
        )
    ]
    part = first.shape[0] // PARTS
    loads, stores = [], []
    for index in range(2 * PARTS):
        which, rows = index // PARTS, pl.ds(index % PARTS * part, part)
        held, out_ref = (first, first_ref) if which == 0 else (second, second_ref)
        there = held.at[rows, :, pl.ds(0, PERIOD)] if which == 0 else held.at[rows]
        loads.append(pltpu.make_async_copy(noise_ref.at[which, rows], there, sems.at[5 + index]))
        stores.append(pltpu.make_async_copy(held.at[rows], out_ref.at[rows], sems.at[5 + 2 * PARTS + index]))
    for copy in tables + loads:
        copy.start()
    for copy in tables:
        copy.wait()
    transmit = (2.0 * mask[...] - 1.0) * (1.0 / PERIOD)
    rows = dot3(split(basis[...]), split(transmit))
    line = dot3(split(rows), (lh[...], ll[...]))
    row = lax.broadcasted_iota(jnp.int32, (RANK, FREQ), 0)
    lane = lax.broadcasted_iota(jnp.int32, (RANK, FREQ), 1)
    apart = jnp.sum(rows * last[...], 1, keepdims=True)
    apart = jnp.sum(jnp.where(row == lane, apart, 0.0), 0, keepdims=True)
    packed = jnp.concatenate(split(jnp.where(row == RANK - 1, apart, line)), 0)
    for index in range(first.shape[0]):
        first[index, :, PERIOD:] = packed
    for load, store in zip(loads, stores):
        load.wait()
        store.start()
    for store in stores:
        store.wait()


def spectrum_body(_, got_ref, gh_ref, gl_ref, unfold_ref, coef_ref, out_ref):
    high = got_ref[:, :RANK].reshape(GROUP_BLOCKS * RANK, FREQ)
    low = got_ref[:, RANK:].reshape(GROUP_BLOCKS * RANK, FREQ)
    both = dot3((gh_ref[0], gl_ref[0]), (high, low))
    waves = dot_exact(split(both[: 2 * FREQ]), unfold_ref[...])
    spare_cos, spare_sin = both[2 * FREQ : 3 * FREQ], both[3 * FREQ :]
    coef_re, coef_im = coef_ref[0], coef_ref[1]
    last_cos = jnp.sum(coef_re * spare_cos - coef_im * spare_sin, 1, keepdims=True)
    last_sin = jnp.sum(coef_re * spare_sin + coef_im * spare_cos, 1, keepdims=True)
    first = lax.broadcasted_iota(jnp.int32, (FREQ, FREQ), 1) == 0
    cos_cos, cos_sin = waves[:FREQ, :FREQ], waves[:FREQ, FREQ:]
    sin_cos, sin_sin = waves[FREQ:, :FREQ], waves[FREQ:, FREQ:]
    out_ref[:FREQ] = cos_cos - sin_sin + jnp.where(first, last_sin, 0.0)
    out_ref[FREQ:] = jnp.where(first, last_cos, 0.0) - cos_sin - sin_cos


def field_body(place_ref, weight_ref, *refs):
    ins, outs, scratch = refs[:10], refs[10 : 11 + KERN], refs[11 + KERN :]
    spec_refs, (kern_ref, wh_ref, wl_ref, gh_ref, gl_ref, blur_ref) = ins[:KERN], ins[KERN:]
    field_ref, piece_refs = outs[0], outs[1:]
    specs, kern, wave, grid, blur, field, total_ref, sems = scratch
    block = place_ref[1]
    copies = fetches(
        list(spec_refs) + [kern_ref, wh_ref.at[block], wl_ref.at[block], gh_ref, gl_ref, blur_ref.at[block]],
        [specs.at[index] for index in range(KERN)]
        + [kern, wave.at[0], wave.at[1], grid.at[0], grid.at[1], blur],
        sems,
    )
    for copy in copies[:7]:
        copy.wait()
    spec = (specs[0] + specs[1]) + (specs[2] + specs[3])
    spec_re = spec[:FREQ]
    spec_im = spec[FREQ:]
    half = KERN * REACH
    total, stores = None, []
    for pair in range(PAIRS):
        near_re, near_im = [], []
        for index in (2 * pair, 2 * pair + 1):
            kern_re, kern_im = kern[index, 0], kern[index, 1]
            near_re.append(kern_re * spec_re - kern_im * spec_im)
            near_im.append(kern_re * spec_im + kern_im * spec_re)
        near = jnp.concatenate([jnp.concatenate(near_re, 1), jnp.concatenate(near_im, 1)], 0)
        left = dot3((wave[0], wave[1]), split(near))
        lefts = []
        for index in range(2):
            lanes = slice(index * FREQ, (index + 1) * FREQ)
            for group in range(KERN):
                first = 2 * group * REACH
                re, im = left[first : first + REACH, lanes], left[first + REACH : first + 2 * REACH, lanes]
                lefts.append(jnp.concatenate([re, im], 1))
        if pair == 0:
            for copy in copies[7:9]:
                copy.wait()
        held = field.at[pl.ds(pair * 2 * half, 2 * half)]
        held[...] = dot3(split(jnp.concatenate(lefts, 0)), (grid[0], grid[1]))
        stores.append(pltpu.make_async_copy(held, field_ref.at[pl.ds(pair * 2 * half, 2 * half)], sems.at[10 + pair]))
        stores[-1].start()
        for index in range(2):
            own = held[index * half : (index + 1) * half]
            own = own * own
            own = weight_ref[2 * pair + index] * (own[:, :COARSE] + own[:, COARSE:])
            total = own if total is None else total + own
    copies[9].wait()
    total_ref[...] = dot3(split(blur[...]), split(total))
    for shift, piece_ref in enumerate(piece_refs):
        group = lax.rem(place_ref[0] + shift, KERN)
        piece_ref[...] = total_ref[pl.ds(pl.multiple_of(group * ROWS, ROWS), ROWS)]
    for store in stores:
        store.wait()


def sample_sums(noise_ref, place, acid, sums):
    sum_u, sum_q, sum_qu = sums
    quarter = 0.25 * acid
    base = acid - 2.0
    for index in range(noise_ref.shape[0]):
        noise = noise_ref[(index,) + place].astype(F32)
        u = jnp.tanh(quarter * noise + base)
        q = (1.0 - u * u) * (1.0 + 0.25 * noise)
        sum_u, sum_q, sum_qu = sum_u + u, sum_q + q, sum_qu + q * u
    return sum_u, sum_q, sum_qu


def places(columns):
    width = min(columns, LANES)
    for row in range(0, ROWS, 16):
        for col in range(0, columns, width):
            yield slice(row, row + 16), slice(col, col + width)


def dose_first_body(rows_ref, oh_ref, ol_ref, noise_ref, sums_ref):
    sums_ref[0] = dot3(split(rows_ref[...]), (oh_ref[...], ol_ref[...]))
    for place in places(CHUNK):
        acid = sums_ref[(0,) + place]
        zero = jnp.zeros(acid.shape, F32)
        for index, value in enumerate(sample_sums(noise_ref, place, acid, (zero, zero, zero))):
            sums_ref[(index + 1,) + place] = value


def acid_grad(sums, target):
    sum_u, sum_q, sum_qu = sums
    inner = 0.25 - sum_u * (1.0 / SAMPLES) - 0.5 * target.astype(F32)
    return (1.0 / 16.0) * (sum_q * inner + 1.25 * sum_qu)


def dose_edge_body(
    _, acid_ref, other_ref, target_ref, first_ref, second_ref, ch_ref, cl_ref, th_ref, tl_ref, grad_ref, send_ref
):
    halo = dot3(split(other_ref[...]), (ch_ref[0], cl_ref[0]))
    for place in places(EDGE):
        acid = acid_ref[(0,) + place] + halo[place]
        zero = jnp.zeros(acid.shape, F32)
        sums = sample_sums(first_ref, place, acid, (zero, zero, zero))
        sums = sample_sums(second_ref, place, acid, sums)
        grad_ref[place] = acid_grad(sums, target_ref[place])
    part = dot3(split(grad_ref[...]), (th_ref[0], tl_ref[0]))
    send_ref[...] = jnp.where(pl.program_id(0) == 0, 0.0, send_ref[...]) + part


def dose_body(sums_ref, edge_ref, target_ref, noise_ref, oh_ref, ol_ref, out_ref):
    step = pl.program_id(0)
    last = pl.num_programs(0) - 1
    total = jnp.where(step == 0, 0.0, out_ref[...])
    for col in range(0, CHUNK, LANES):
        lanes = slice(col, col + LANES)
        grads = []
        for row in range(0, ROWS, 16):
            place = (slice(row, row + 16), lanes)
            acid, *sums = [sums_ref[(index,) + place] for index in range(4)]
            grads.append(acid_grad(sample_sums(noise_ref, place, acid, sums), target_ref[place]))
        grad = jnp.concatenate(grads, 0)
        if col == 0:
            grad = jnp.concatenate([jnp.where(step == 0, edge_ref[:, :EDGE], grad[:, :EDGE]), grad[:, EDGE:]], 1)
        if col == CHUNK - LANES:
            here = jnp.where(step == last, edge_ref[:, EDGE:], grad[:, LANES - EDGE :])
            grad = jnp.concatenate([grad[:, : LANES - EDGE], here], 1)
        total = total + dot3(split(grad), (oh_ref[lanes], ol_ref[lanes]))
    out_ref[...] = total


def fetches(sources, targets, sems):
    copies = [
        pltpu.make_async_copy(source, target, sems.at[index])
        for index, (source, target) in enumerate(zip(sources, targets))
    ]
    for copy in copies:
        copy.start()
    return copies


def back_body(place_ref, weight_ref, *refs):
    piece_refs, ins = refs[:KERN], refs[KERN : KERN + 11]
    field_ref, kern_ref, wh_ref, wl_ref, gh_ref, gl_ref, blur_ref, th_ref, tl_ref, fold_ref, coef_ref = ins
    out_ref, rows, blur, grid, field, wave, kern, fold, coef, table, sems = refs[KERN + 11 :]
    block = place_ref[1]
    group = [lax.rem(place_ref[0] - shift + KERN, KERN) * ROWS for shift in range(KERN)]
    size = 2 * KERN * REACH
    pairs = [pl.ds(pair * size, size) for pair in range(PAIRS)]
    copies = fetches(
        list(piece_refs)
        + [blur_ref.at[block], field_ref.at[pairs[0]], gh_ref, gl_ref, wh_ref.at[block], wl_ref.at[block], kern_ref]
        + [field_ref.at[pair] for pair in pairs[1:]]
        + [fold_ref, coef_ref, th_ref, tl_ref],
        [rows.at[pl.ds(pl.multiple_of(first, ROWS), ROWS)] for first in group]
        + [blur, field.at[pairs[0]], grid.at[0], grid.at[1], wave.at[0], wave.at[1], kern]
        + [field.at[pair] for pair in pairs[1:]]
        + [fold, coef, table.at[0], table.at[1]],
        sems,
    )
    for copy in copies[:5]:
        copy.wait()
    part = 2.0 * dot3(split(blur[...]), split(rows[...]))
    grad = jnp.concatenate([part, part], 1)
    half = KERN * REACH
    sum_re = sum_im = None
    for pair in range(PAIRS):
        for copy in copies[5:8] if pair == 0 else copies[10 + pair : 11 + pair]:
            copy.wait()
        pulled = [
            field[index * half : (index + 1) * half] * (weight_ref[index] * grad)
            for index in (2 * pair, 2 * pair + 1)
        ]
        lefts = dot3(split(jnp.concatenate(pulled, 0)), (grid[0], grid[1]))
        stack = []
        for index in range(2):
            column = []
            for which in range(KERN):
                first = index * half + which * REACH
                left = lefts[first : first + REACH]
                column += [left[:, :FREQ], left[:, FREQ:]]
            stack.append(jnp.concatenate(column, 0))
        if pair == 0:
            for copy in copies[8:11]:
                copy.wait()
        near = dot3((wave[0], wave[1]), split(jnp.concatenate(stack, 1)))
        for index in range(2):
            near_re = near[:FREQ, index * FREQ : (index + 1) * FREQ]
            near_im = near[FREQ:, index * FREQ : (index + 1) * FREQ]
            kern_re, kern_im = kern[2 * pair + index, 0], kern[2 * pair + index, 1]
            own_re = kern_re * near_re + kern_im * near_im
            own_im = kern_re * near_im - kern_im * near_re
            sum_re = own_re if sum_re is None else sum_re + own_re
            sum_im = own_im if sum_im is None else sum_im + own_im
    grad_re, grad_im = sum_re * (2.0 / PERIOD), sum_im * (2.0 / PERIOD)
    mix = jnp.concatenate(
        [jnp.concatenate([grad_re, -grad_im], 1), jnp.concatenate([-grad_im, -grad_re], 1)], 0
    )
    for copy in copies[13:]:
        copy.wait()
    folded = dot_exact(split(mix), fold[...])
    coef_re, coef_im = coef[0], coef[1]
    by_cos, by_sin = grad_im[:, :1], grad_re[:, :1]
    spare_cos = coef_re * by_cos + coef_im * by_sin
    spare_sin = coef_re * by_sin - coef_im * by_cos
    mixed = jnp.concatenate([folded, spare_cos, spare_sin], 0)
    high, low = split(dot3((table[0], table[1]), split(mixed)).reshape(out_ref.shape))
    row = lax.broadcasted_iota(jnp.int32, out_ref.shape, 1)
    out_ref[...] = jnp.where(row < HIGH, high.astype(F32), low.astype(F32)).astype(BF)


def final_body(got_ref, back_ref, basis_ref, wh_ref, wl_ref, last_ref, out_ref):
    total = got_ref[0].astype(F32)
    for index in range(1, got_ref.shape[0]):
        total = total + got_ref[index].astype(F32)
    rows = dot3(split(back_ref[...]), split(total))
    spare = jnp.sum(basis_ref[...] * total[HIGH - 1 : HIGH], 1, keepdims=True)
    out_ref[...] = dot3(split(rows), (wh_ref[...], wl_ref[...])) + spare * last_ref[...]


def to_const(table):
    return hbm(*near_const(table))


def near_const(table):
    return tuple(jnp.asarray(part) for part in np_split(table))


def shifted(values, shifts):
    count = lax.axis_size("kern")
    return [
        lax.ppermute(value, "kern", [(source, (source + shift) % count) for source in range(count)])
        for value, shift in zip(values, shifts)
    ]


def body(mask_values, kernels, weights, target, dose_noise):
    noise_count = lax.axis_size("noise")
    f32 = lambda *shape: jax.ShapeDtypeStruct(shape, F32)
    bf16 = lambda *shape: jax.ShapeDtypeStruct(shape, BF)
    smem = pl.BlockSpec(memory_space=pltpu.SMEM)
    columns = PERIOD // CHUNK
    shifts = range(1, KERN)

    def fixed(*shape):
        return pl.BlockSpec(shape, lambda i, *_: (0,) * len(shape))

    def chunk(rows):
        return pl.BlockSpec((rows, CHUNK), lambda i, *_: (0, i))

    def moved_spec(width):
        return pl.BlockSpec((noise_count // columns, ROWS, width), lambda i: (i, 0, 0))

    lines = to_const(LINE.T)
    basis = jnp.asarray(BASIS.T[:RANK], F32)
    last = jnp.asarray(LAST, F32)
    far_noise = dose_noise.reshape(2, noise_count, ROWS, PERIOD)
    anywhere = pl.BlockSpec(memory_space=pltpu.HBM)
    held = (mask_values, basis, *lines, last)
    moved_first, moved = call(
        front_body,
        (pltpu.HBM((noise_count, ROWS, PERIOD + FREQ), BF), pltpu.HBM((noise_count, ROWS, PERIOD), BF)),
        hbm(*held, far_noise),
        in_specs=[anywhere] * 6,
        out_specs=(anywhere, anywhere),
        scratch_shapes=[pltpu.VMEM(value.shape, value.dtype) for value in held]
        + [
            pltpu.VMEM((noise_count, ROWS, PERIOD + FREQ), BF),
            pltpu.VMEM((noise_count, ROWS, PERIOD), BF),
            pltpu.SemaphoreType.DMA((5 + 4 * PARTS,)),
        ],
    )
    place = jnp.stack([lax.axis_index(axis).astype(jnp.int32) for axis in ("kern", "noise", "tile")])
    moved_first, place = lax.optimization_barrier((moved_first, place))
    got = lax.all_to_all(moved_first, "noise", 0, 0, tiled=True)
    got, moved, kernels, weights, target, place = lax.optimization_barrier(
        (got, moved, kernels, weights, target, place)
    )
    got_last = lax.all_to_all(moved, "noise", 0, 0, tiled=True)

    def at_place(which, table):
        return [pl.BlockSpec((1,) + table.shape[1:], lambda i, place: (place[which], 0, 0))] * 2

    waves_t = WAVE.transpose(0, 2, 1)
    cross_t = CROSS.transpose(0, 2, 1)
    coef = hbm(jnp.asarray(COEF, F32))
    spec = call(
        spectrum_body,
        f32(2 * FREQ, FREQ),
        (got, *to_const(GATHER_OWN), jnp.asarray(UNFOLD, BF), jnp.asarray(COEF, F32)),
        place=place,
        grid=(1,),
        in_specs=[pl.BlockSpec((noise_count, ROWS, FREQ), lambda i, _: (0, 0, PERIOD // FREQ))]
        + at_place(0, GATHER_OWN)
        + [fixed(*UNFOLD.shape), fixed(*COEF.shape)],
        out_specs=fixed(2 * FREQ, FREQ),
    )
    specs = [spec] + shifted([spec] * len(shifts), shifts)
    field_rows = 2 * KERN * REACH
    field_shape = (PAIRS * field_rows, 2 * COARSE)
    blur = jnp.asarray(BLUR, F32)
    ins = (*specs, kernels, *to_const(WAVE), *to_const(GRID), blur)
    field, *pieces = call(
        field_body,
        (pltpu.HBM(field_shape, F32),) + (f32(ROWS, COARSE),) * KERN,
        (place, weights, *hbm(*ins)),
        in_specs=[smem] * 2 + [anywhere] * len(ins),
        out_specs=(anywhere,) + (pl.BlockSpec((ROWS, COARSE), lambda: (0, 0)),) * KERN,
        scratch_shapes=[
            pltpu.VMEM((KERN,) + spec.shape, F32),
            pltpu.VMEM(kernels.shape, F32),
            pltpu.VMEM((2,) + WAVE.shape[1:], BF),
            pltpu.VMEM((2,) + GRID.shape, BF),
            pltpu.VMEM(BLUR.shape[1:], F32),
            pltpu.VMEM(field_shape, F32),
            pltpu.VMEM((KERN * ROWS, COARSE), F32),
            pltpu.SemaphoreType.DMA((10 + PAIRS,)),
        ],
    )
    pieces = pieces[:1] + shifted(pieces[1:], shifts)
    rows = (pieces[0] + pieces[1]) + (pieces[2] + pieces[3])
    swap = [(0, 1), (1, 0)]
    rows_other = lax.ppermute(rows, "tile", swap)
    got_spec = pl.BlockSpec((noise_count, ROWS, CHUNK), lambda i: (0, 0, i))
    sums_spec = pl.BlockSpec((4, ROWS, CHUNK), lambda i: (0, 0, i))
    sums = call(
        dose_first_body,
        f32(4, ROWS, PERIOD),
        (rows, *near_const(OWN.T), got),
        grid=(columns,),
        in_specs=[fixed(ROWS, COARSE)] + [chunk(COARSE)] * 2 + [got_spec],
        out_specs=sums_spec,
    )
    far = PERIOD // EDGE - 1
    (target,) = hbm(target)
    (sums,) = vmem(sums)
    edge_spec = pl.BlockSpec((noise_count, ROWS, EDGE), lambda i, _: (0, 0, i * far))
    edges, send = call(
        dose_edge_body,
        (f32(ROWS, 2 * EDGE), f32(ROWS, COARSE)),
        (sums, rows_other, target, got, got_last, *to_const(CROSS), *to_const(cross_t)),
        place=place,
        grid=(2,),
        in_specs=[
            pl.BlockSpec((1, ROWS, EDGE), lambda i, _: (0, 0, i * far)),
            fixed(ROWS, COARSE),
            pl.BlockSpec((ROWS, EDGE), lambda i, _: (0, i * far)),
            edge_spec,
            edge_spec,
        ]
        + [pl.BlockSpec((1, COARSE, EDGE), lambda i, place: (place[2], 0, i))] * 2
        + [pl.BlockSpec((1, EDGE, COARSE), lambda i, place: (place[2], i, 0))] * 2,
        out_specs=(pl.BlockSpec((ROWS, EDGE), lambda i, _: (0, i)), fixed(ROWS, COARSE)),
    )
    grad_other = lax.ppermute(send, "tile", swap)
    grad_own = call(
        dose_body,
        f32(ROWS, COARSE),
        (sums, edges, target, got_last, *to_const(OWN)),
        grid=(columns,),
        in_specs=[sums_spec, fixed(ROWS, 2 * EDGE), chunk(ROWS), got_spec]
        + [pl.BlockSpec((CHUNK, COARSE), lambda i: (i, 0))] * 2,
        out_specs=fixed(ROWS, COARSE),
    )
    grad = grad_own + grad_other
    grads = [grad] + shifted([grad] * len(shifts), shifts)
    blur_t, fold = jnp.asarray(BLUR.transpose(0, 2, 1), F32), jnp.asarray(UNFOLD.T, BF)
    ins = (*grads, field, kernels, *to_const(waves_t), *to_const(GRID.T), blur_t, *to_const(SPREAD), fold, *coef)
    spread = call(
        back_body,
        bf16(BLOCKS, RANK, FREQ),
        (place, weights, *hbm(*ins)),
        in_specs=[smem] * 2 + [anywhere] * len(ins),
        out_specs=pl.BlockSpec((BLOCKS, RANK, FREQ), lambda: (0, 0, 0)),
        scratch_shapes=[
            pltpu.VMEM((KERN * ROWS, COARSE), F32),
            pltpu.VMEM(BLUR.shape[:0:-1], F32),
            pltpu.VMEM((2,) + GRID.T.shape, BF),
            pltpu.VMEM(field_shape, F32),
            pltpu.VMEM((2,) + waves_t.shape[1:], BF),
            pltpu.VMEM(kernels.shape, F32),
            pltpu.VMEM(fold.shape, BF),
            pltpu.VMEM(COEF.shape, F32),
            pltpu.VMEM((2,) + SPREAD.shape, BF),
            pltpu.SemaphoreType.DMA((KERN + 13,)),
        ],
    )
    back = lax.all_to_all(spread, ("kern", "noise"), 0, 0, tiled=True)
    return call(
        final_body,
        f32(ROWS, PERIOD),
        (back, jnp.asarray(BASIS_BACK, F32), jnp.asarray(BASIS, F32), *(jnp.asarray(t) for t in np_split(LINE)), jnp.asarray(LAST, F32)),
    )


def solution(mesh):
    return jax.shard_map(
        body,
        mesh=mesh,
        in_specs=(
            P(("kern", "noise"), "tile"),
            P("kern", None, None, None),
            P("kern"),
            P(("kern", "noise"), "tile"),
            P("noise", "kern", "tile"),
        ),
        out_specs=P(("kern", "noise"), "tile"),
        check_vma=False,
    )
```

```python
import math

import jax
import jax.numpy as jnp
import numpy as np
from jax import lax
from jax.experimental import pallas as pl
from jax.experimental.pallas import tpu as pltpu
from jax.sharding import PartitionSpec as P

HALO = 16
FREQ = 128
COARSE = 256
PERIOD = 2048
ROWS = 32
REACH = 24
EDGE = 128
GROUP = 6
PAIRS = GROUP // 2
KERN = 4
SAMPLES = 32
RANK = 16
MIB = 32
BF = jnp.bfloat16
F32 = jnp.float32


def np_split(table):
    table = np.asarray(table, np.float32)
    high = table.astype(jnp.bfloat16)
    low = (table - high.astype(np.float32)).astype(jnp.bfloat16)
    return high, low


def np_waves(ids):
    centred = np.arange(FREQ) - FREQ // 2
    angles = 2.0 * np.pi * ((centred[:, None] * ids[None, :]) % PERIOD) / PERIOD
    return np.cos(angles), np.sin(angles)


def line_tables():
    half = FREQ // 2
    pixels = np.arange(PERIOD)
    angle = lambda f: 2.0 * np.pi * ((f[:, None] * pixels[None, :]) % PERIOD) / PERIOD
    line = np.concatenate([np.cos(angle(np.arange(half + 1))), np.sin(angle(np.arange(1, half)))], 0)
    last = np.sin(angle(np.array([half])))
    unfold = np.zeros((FREQ, 2 * FREQ))
    for j in range(FREQ):
        f = j - half
        unfold[abs(f), j] = 1.0
        if 0 < abs(f) < half:
            unfold[half + abs(f), FREQ + j] = np.sign(f)
    row = np.arange(ROWS) - (ROWS - 1) / 2.0
    fine = np.arange(-half, half + 0.01, 0.25)
    wave = np.exp(2j * np.pi * np.outer(row, fine) / PERIOD)
    basis = np.linalg.svd(np.concatenate([wave.real, wave.imag], 1))[0][:, : RANK - 1]
    basis = np.concatenate([basis, np.zeros((ROWS, FREQ - RANK + 1))], 1)
    freqs = np.arange(FREQ) - half
    coef = np.exp(2j * np.pi * np.outer(freqs, row) / PERIOD) @ basis
    blocks = PERIOD // ROWS
    centre = ROWS * np.arange(blocks) + (ROWS - 1) / 2.0
    phase = np.exp(2j * np.pi * np.outer(freqs, centre) / PERIOD)
    rows = phase[:, :, None] * coef[:, None, :RANK]
    rows[:, :, RANK - 1] = 0.0
    spare = np.zeros_like(rows)
    spare[:, :, RANK - 1] = phase
    rows = rows.reshape(FREQ, blocks * RANK)
    spare = spare.reshape(FREQ, blocks * RANK)
    gather = np.concatenate([rows.real, rows.imag, spare.real, spare.imag], 0)
    return line, last, unfold, basis, np.stack([coef.real, coef.imag]), gather


def tables():
    ccos, csin = np_waves(np.arange(COARSE) * (PERIOD // COARSE))
    grid = np.block([[ccos, csin], [-csin, ccos]]) / FREQ
    offsets = np.arange(-HALO, HALO + 1)
    taps = np.exp(-(offsets.astype(np.float64) ** 2) / (2.0 * (HALO / 2.0) ** 2))
    taps = taps / taps.sum()
    nodes = np.cos(np.pi * (np.arange(REACH) + 0.5) / REACH) * (ROWS / 2 + HALO - 0.5) + (ROWS - 1) / 2.0
    freqs = np.arange(1 - FREQ, FREQ)
    at = lambda places: np.exp(2j * np.pi * np.outer(places, freqs) / PERIOD)
    both = lambda value: np.concatenate([value.real, value.imag], 1)
    row_blur = np.zeros((PERIOD // ROWS, ROWS, REACH))
    near = np.arange(-HALO, ROWS + HALO)
    full = np.zeros((ROWS, ROWS + 2 * HALO))
    for row in range(ROWS):
        full[row, row : row + 2 * HALO + 1] = taps
    for block in range(PERIOD // ROWS):
        inside = (near + block * ROWS >= 0) & (near + block * ROWS < PERIOD)
        wanted = both((full * inside) @ at(near))
        row_blur[block] = np.linalg.lstsq(both(at(nodes)).T, wanted.T, rcond=1e-12)[0].T
    places = ROWS * np.arange(PERIOD // ROWS)[:, None] + nodes[None, :]
    angles = 2.0 * np.pi * (places[:, :, None] * (np.arange(FREQ) - FREQ // 2)) / PERIOD
    cos, sin = np.cos(angles), np.sin(angles)
    reach = np.concatenate([np.concatenate([cos, -sin], 2), np.concatenate([sin, cos], 2)], 1)
    shift = np.arange(PERIOD)[:, None] - (PERIOD // COARSE) * np.arange(COARSE)[None, :]
    freqs = np.arange(1, FREQ)
    line = (1.0 + 2.0 * np.cos(2.0 * np.pi * np.outer(np.arange(PERIOD), freqs) / PERIOD).sum(1)) / COARSE
    interp = line[shift % PERIOD]
    padded = np.zeros((PERIOD + 2 * HALO, COARSE))
    padded[HALO:-HALO] = interp
    own = np.zeros((PERIOD, COARSE))
    for index, tap in enumerate(taps):
        own += tap * padded[index : index + PERIOD]
    cross = np.zeros((2, COARSE, 2 * EDGE))
    for column in range(HALO):
        for index, offset in enumerate(offsets):
            if column + offset < 0:
                cross[1, :, column] += taps[index] * interp[PERIOD + column + offset]
            place = PERIOD - 1 - column + offset
            if place >= PERIOD:
                cross[0, :, 2 * EDGE - 1 - column] += taps[index] * interp[place - PERIOD]
    return reach, grid, row_blur, own, cross


LINE, LAST, UNFOLD, BASIS, COEF, GATHER = line_tables()
REACH_WAVES, GRID, ROW_BLUR, OWN, CROSS = tables()
BLOCKS = PERIOD // ROWS
GROUP_BLOCKS = BLOCKS // KERN
WAVE = REACH_WAVES
WAVE = WAVE.reshape(KERN, GROUP_BLOCKS, 2 * REACH, 2 * FREQ).transpose(1, 0, 2, 3)
WAVE = WAVE.reshape(GROUP_BLOCKS, KERN * 2 * REACH, 2 * FREQ)
LOW = 4
HIGH = RANK - LOW
SPREAD = GATHER.reshape(4 * FREQ, BLOCKS, RANK)
SPREAD = np.concatenate([SPREAD[:, :, : HIGH - 1], SPREAD[:, :, RANK - 1 :], SPREAD[:, :, :LOW]], 2)
SPREAD = SPREAD.reshape(4 * FREQ, BLOCKS * RANK).T
BASIS_BACK = np.concatenate([BASIS[:, : HIGH - 1], np.zeros((ROWS, 1)), BASIS[:, :LOW]], 1)
GATHER_OWN = GATHER.reshape(4 * FREQ, KERN, GROUP_BLOCKS * RANK).transpose(1, 0, 2)
BLUR = np.zeros((GROUP_BLOCKS, KERN, ROWS, KERN, REACH))
for group in range(KERN):
    BLUR[:, group, :, group] = ROW_BLUR.reshape(KERN, GROUP_BLOCKS, ROWS, REACH)[group]
BLUR = BLUR.reshape(GROUP_BLOCKS, KERN * ROWS, KERN * REACH)


def split(value):
    high = value.astype(BF)
    return high, (value - high.astype(F32)).astype(BF)


NN = (((1,), (0,)), ((), ()))


def dot3(left, right):
    lh, ll = left
    rh, rl = right

    def one(a, b):
        return lax.dot_general(a, b, NN, preferred_element_type=F32)

    count = lh.shape[0]
    if count > 64:
        return one(jnp.concatenate([lh, ll, lh], 1), jnp.concatenate([rh, rh, rl], 0))
    both = one(jnp.concatenate([lh, ll], 0), rh)
    return both[:count] + (one(lh, rl) + both[count:])


def dot_exact(left, right):
    high, low = left
    return jnp.dot(high, right, preferred_element_type=F32) + jnp.dot(low, right, preferred_element_type=F32)


def call(body, out_shape, args, place=None, **kw):
    params = pltpu.CompilerParams(vmem_limit_bytes=MIB * 1024 * 1024)
    if place is None:
        return pl.pallas_call(body, out_shape=out_shape, compiler_params=params, **kw)(*args)
    grid_spec = pltpu.PrefetchScalarGridSpec(num_scalar_prefetch=1, **kw)
    return pl.pallas_call(body, out_shape=out_shape, compiler_params=params, grid_spec=grid_spec)(place, *args)


def hbm(*values):
    return tuple(pltpu.with_memory_space_constraint(value, pltpu.HBM) for value in values)


def vmem(*values):
    return tuple(pltpu.with_memory_space_constraint(value, pltpu.VMEM) for value in values)


CHUNK = 1024
LANES = 256
PARTS = 4


def fetches(sources, targets, sems):
    copies = [
        pltpu.make_async_copy(source, target, sems.at[index])
        for index, (source, target) in enumerate(zip(sources, targets))
    ]
    for copy in copies:
        copy.start()
    return copies


def front_body(mask_ref, basis_ref, lh_ref, ll_ref, last_ref, noise_ref, first_ref, second_ref, *scratch):
    mask, basis, lh, ll, last, first, second, sems = scratch
    tables = [
        pltpu.make_async_copy(source, target, sems.at[index])
        for index, (source, target) in enumerate(
            zip((mask_ref, basis_ref, lh_ref, ll_ref, last_ref), (mask, basis, lh, ll, last))
        )
    ]
    part = first.shape[0] // PARTS
    loads, stores = [], []
    for index in range(2 * PARTS):
        which, rows = index // PARTS, pl.ds(index % PARTS * part, part)
        held, out_ref = (first, first_ref) if which == 0 else (second, second_ref)
        there = held.at[rows, :, pl.ds(0, PERIOD)] if which == 0 else held.at[rows]
        loads.append(pltpu.make_async_copy(noise_ref.at[which, rows], there, sems.at[5 + index]))
        stores.append(pltpu.make_async_copy(held.at[rows], out_ref.at[rows], sems.at[5 + 2 * PARTS + index]))
    for copy in tables + loads:
        copy.start()
    for copy in tables:
        copy.wait()
    transmit = (2.0 * mask[...] - 1.0) * (1.0 / PERIOD)
    rows = dot3(split(basis[...]), split(transmit))
    line = dot3(split(rows), (lh[...], ll[...]))
    row = lax.broadcasted_iota(jnp.int32, (RANK, FREQ), 0)
    lane = lax.broadcasted_iota(jnp.int32, (RANK, FREQ), 1)
    apart = jnp.sum(rows * last[...], 1, keepdims=True)
    apart = jnp.sum(jnp.where(row == lane, apart, 0.0), 0, keepdims=True)
    packed = jnp.concatenate(split(jnp.where(row == RANK - 1, apart, line)), 0)
    for index in range(first.shape[0]):
        first[index, :, PERIOD:] = packed
    for load, store in zip(loads, stores):
        load.wait()
        store.start()
    for store in stores:
        store.wait()


def spectrum_body(_, got_ref, gh_ref, gl_ref, unfold_ref, coef_ref, out_ref):
    high = got_ref[:, :RANK].reshape(GROUP_BLOCKS * RANK, FREQ)
    low = got_ref[:, RANK:].reshape(GROUP_BLOCKS * RANK, FREQ)
    both = dot3((gh_ref[0], gl_ref[0]), (high, low))
    waves = dot_exact(split(both[: 2 * FREQ]), unfold_ref[...])
    spare_cos, spare_sin = both[2 * FREQ : 3 * FREQ], both[3 * FREQ :]
    coef_re, coef_im = coef_ref[0], coef_ref[1]
    last_cos = jnp.sum(coef_re * spare_cos - coef_im * spare_sin, 1, keepdims=True)
    last_sin = jnp.sum(coef_re * spare_sin + coef_im * spare_cos, 1, keepdims=True)
    first = lax.broadcasted_iota(jnp.int32, (FREQ, FREQ), 1) == 0
    cos_cos, cos_sin = waves[:FREQ, :FREQ], waves[:FREQ, FREQ:]
    sin_cos, sin_sin = waves[FREQ:, :FREQ], waves[FREQ:, FREQ:]
    out_ref[:FREQ] = cos_cos - sin_sin + jnp.where(first, last_sin, 0.0)
    out_ref[FREQ:] = jnp.where(first, last_cos, 0.0) - cos_sin - sin_cos


def field_body(place_ref, weight_ref, *refs):
    ins, outs, scratch = refs[:10], refs[10 : 11 + KERN], refs[11 + KERN :]
    spec_refs, (kern_ref, wh_ref, wl_ref, gh_ref, gl_ref, blur_ref) = ins[:KERN], ins[KERN:]
    field_ref, piece_refs = outs[0], outs[1:]
    specs, kern, wave, grid, blur, field, total_ref, sems = scratch
    block = place_ref[1]
    copies = fetches(
        list(spec_refs) + [kern_ref, wh_ref.at[block], wl_ref.at[block], gh_ref, gl_ref, blur_ref.at[block]],
        [specs.at[index] for index in range(KERN)]
        + [kern, wave.at[0], wave.at[1], grid.at[0], grid.at[1], blur],
        sems,
    )
    for copy in copies[:7]:
        copy.wait()
    spec = (specs[0] + specs[1]) + (specs[2] + specs[3])
    spec_re = spec[:FREQ]
    spec_im = spec[FREQ:]
    half = KERN * REACH
    total, stores = None, []
    for pair in range(PAIRS):
        near_re, near_im = [], []
        for index in (2 * pair, 2 * pair + 1):
            kern_re, kern_im = kern[index, 0], kern[index, 1]
            near_re.append(kern_re * spec_re - kern_im * spec_im)
            near_im.append(kern_re * spec_im + kern_im * spec_re)
        near = jnp.concatenate([jnp.concatenate(near_re, 1), jnp.concatenate(near_im, 1)], 0)
        left = dot3((wave[0], wave[1]), split(near))
        lefts = []
        for index in range(2):
            lanes = slice(index * FREQ, (index + 1) * FREQ)
            for group in range(KERN):
                first = 2 * group * REACH
                re, im = left[first : first + REACH, lanes], left[first + REACH : first + 2 * REACH, lanes]
                lefts.append(jnp.concatenate([re, im], 1))
        if pair == 0:
            for copy in copies[7:9]:
                copy.wait()
        held = field.at[pl.ds(pair * 2 * half, 2 * half)]
        held[...] = dot3(split(jnp.concatenate(lefts, 0)), (grid[0], grid[1]))
        stores.append(pltpu.make_async_copy(held, field_ref.at[pl.ds(pair * 2 * half, 2 * half)], sems.at[10 + pair]))
        stores[-1].start()
        for index in range(2):
            own = held[index * half : (index + 1) * half]
            own = own * own
            own = weight_ref[2 * pair + index] * (own[:, :COARSE] + own[:, COARSE:])
            total = own if total is None else total + own
    copies[9].wait()
    total_ref[...] = dot3(split(blur[...]), split(total))
    for shift, piece_ref in enumerate(piece_refs):
        group = jnp.bitwise_xor(place_ref[0], shift)
        piece_ref[...] = total_ref[pl.ds(pl.multiple_of(group * ROWS, ROWS), ROWS)]
    for store in stores:
        store.wait()


def sample_sums(noise_ref, place, acid, sums):
    sum_u, sum_q, sum_qu = sums
    quarter = 0.25 * acid
    base = acid - 2.0
    for index in range(noise_ref.shape[0]):
        noise = noise_ref[(index,) + place].astype(F32)
        u = jnp.tanh(quarter * noise + base)
        q = (1.0 - u * u) * (1.0 + 0.25 * noise)
        sum_u, sum_q, sum_qu = sum_u + u, sum_q + q, sum_qu + q * u
    return sum_u, sum_q, sum_qu


def places(columns):
    width = min(columns, LANES)
    for row in range(0, ROWS, 16):
        for col in range(0, columns, width):
            yield slice(row, row + 16), slice(col, col + width)


def dose_first_body(rows_ref, oh_ref, ol_ref, noise_ref, sums_ref):
    sums_ref[0] = dot3(split(rows_ref[...]), (oh_ref[...], ol_ref[...]))
    for place in places(CHUNK):
        acid = sums_ref[(0,) + place]
        zero = jnp.zeros(acid.shape, F32)
        for index, value in enumerate(sample_sums(noise_ref, place, acid, (zero, zero, zero))):
            sums_ref[(index + 1,) + place] = value


def acid_grad(sums, target):
    sum_u, sum_q, sum_qu = sums
    inner = 0.25 - sum_u * (1.0 / SAMPLES) - 0.5 * target.astype(F32)
    return (1.0 / 16.0) * (sum_q * inner + 1.25 * sum_qu)


def dose_edge_body(place_ref, sums_ref, other_ref, *refs):
    ins, (grad_ref, send_ref), (held, target, cross, cross_t, sems) = refs[:7], refs[7:9], refs[9:]
    target_ref, first_ref, second_ref, ch_ref, cl_ref, th_ref, tl_ref = ins
    tile = place_ref[2]
    sides = [pl.ds(0, EDGE), pl.ds(PERIOD - EDGE, EDGE)]
    copies = fetches(
        [ch_ref.at[tile], cl_ref.at[tile]]
        + [ref.at[:, :, side] for side in sides for ref in (first_ref, second_ref)]
        + [target_ref.at[:, side] for side in sides]
        + [th_ref.at[tile], tl_ref.at[tile]],
        [cross.at[0], cross.at[1]]
        + [held.at[index] for index in range(4)]
        + [target.at[index] for index in range(2)]
        + [cross_t.at[0], cross_t.at[1]],
        sems,
    )
    for copy in copies[:2]:
        copy.wait()
    halo = dot3(split(other_ref[...]), (cross[0], cross[1]))
    for copy in copies[2:8]:
        copy.wait()
    grads = []
    for side in range(2):
        columns = []
        for row, lanes in places(EDGE):
            place = (row, lanes)
            there = slice(side * (PERIOD - EDGE), side * (PERIOD - EDGE) + EDGE)
            acid = sums_ref[0, row, there] + halo[row, side * EDGE : (side + 1) * EDGE]
            zero = jnp.zeros(acid.shape, F32)
            sums = sample_sums(held.at[2 * side], place, acid, (zero, zero, zero))
            sums = sample_sums(held.at[2 * side + 1], place, acid, sums)
            columns.append(acid_grad(sums, target[(side,) + place]))
        grads.append(jnp.concatenate(columns, 0))
    grad = jnp.concatenate(grads, 1)
    grad_ref[...] = grad
    for copy in copies[8:]:
        copy.wait()
    send_ref[...] = dot3(split(grad), (cross_t[0], cross_t[1]))


def dose_body(place_ref, sums_ref, edge_ref, target_ref, noise_ref, oh_ref, ol_ref, *refs):
    step = pl.program_id(0)
    last = pl.num_programs(0) - 1
    ins, out_ref, outs, sems = refs[:11], refs[11], refs[12:20], refs[20]
    field_ref, kern_ref, wh_ref, wl_ref, gh_ref, gl_ref, blur_ref, th_ref, tl_ref, fold_ref, coef_ref = ins
    field, kern, wave, grid, blur, table, fold, coef = outs
    block = place_ref[1]
    copies = [
        pltpu.make_async_copy(source, held, sems.at[index])
        for index, (source, held) in enumerate(
            zip(
                [field_ref, kern_ref, wh_ref.at[block], wl_ref.at[block], gh_ref, gl_ref]
                + [blur_ref.at[block], th_ref, tl_ref, fold_ref, coef_ref],
                [field, kern, wave.at[0], wave.at[1], grid.at[0], grid.at[1]]
                + [blur, table.at[0], table.at[1], fold, coef],
            )
        )
    ]

    @pl.when(step == 0)
    def _():
        for copy in copies:
            copy.start()

    total = jnp.where(step == 0, 0.0, out_ref[...])
    for col in range(0, CHUNK, LANES):
        lanes = slice(col, col + LANES)
        grads = []
        for row in range(0, ROWS, 16):
            place = (slice(row, row + 16), lanes)
            acid, *sums = [sums_ref[(index,) + place] for index in range(4)]
            grads.append(acid_grad(sample_sums(noise_ref, place, acid, sums), target_ref[place]))
        grad = jnp.concatenate(grads, 0)
        if col == 0:
            grad = jnp.concatenate([jnp.where(step == 0, edge_ref[:, :EDGE], grad[:, :EDGE]), grad[:, EDGE:]], 1)
        if col == CHUNK - LANES:
            here = jnp.where(step == last, edge_ref[:, EDGE:], grad[:, LANES - EDGE :])
            grad = jnp.concatenate([grad[:, : LANES - EDGE], here], 1)
        total = total + dot3(split(grad), (oh_ref[lanes], ol_ref[lanes]))
    out_ref[...] = total

    @pl.when(step == last)
    def _():
        for copy in copies:
            copy.wait()


def back_body(place_ref, weight_ref, *refs):
    piece_refs, (field, kern, wave, grid, blur, table, fold, coef) = refs[:KERN], refs[KERN : KERN + 8]
    out_ref, rows = refs[KERN + 8 :]
    for shift, piece_ref in enumerate(piece_refs):
        first = jnp.bitwise_xor(place_ref[0], shift) * ROWS
        rows[pl.ds(pl.multiple_of(first, ROWS), ROWS)] = piece_ref[...]
    part = 2.0 * dot3(split(blur[...]), split(rows[...]))
    grad = jnp.concatenate([part, part], 1)
    half = KERN * REACH
    sum_re = sum_im = None
    for pair in range(PAIRS):
        pulled = [
            field[index * half : (index + 1) * half] * (weight_ref[index] * grad)
            for index in (2 * pair, 2 * pair + 1)
        ]
        lefts = dot3(split(jnp.concatenate(pulled, 0)), (grid[0], grid[1]))
        stack = []
        for index in range(2):
            column = []
            for which in range(KERN):
                first = index * half + which * REACH
                left = lefts[first : first + REACH]
                column += [left[:, :FREQ], left[:, FREQ:]]
            stack.append(jnp.concatenate(column, 0))
        near = dot3((wave[0], wave[1]), split(jnp.concatenate(stack, 1)))
        for index in range(2):
            near_re = near[:FREQ, index * FREQ : (index + 1) * FREQ]
            near_im = near[FREQ:, index * FREQ : (index + 1) * FREQ]
            kern_re, kern_im = kern[2 * pair + index, 0], kern[2 * pair + index, 1]
            own_re = kern_re * near_re + kern_im * near_im
            own_im = kern_re * near_im - kern_im * near_re
            sum_re = own_re if sum_re is None else sum_re + own_re
            sum_im = own_im if sum_im is None else sum_im + own_im
    grad_re, grad_im = sum_re * (2.0 / PERIOD), sum_im * (2.0 / PERIOD)
    mix = jnp.concatenate(
        [jnp.concatenate([grad_re, -grad_im], 1), jnp.concatenate([-grad_im, -grad_re], 1)], 0
    )
    folded = dot_exact(split(mix), fold[...])
    coef_re, coef_im = coef[0], coef[1]
    by_cos, by_sin = grad_im[:, :1], grad_re[:, :1]
    spare_cos = coef_re * by_cos + coef_im * by_sin
    spare_sin = coef_re * by_sin - coef_im * by_cos
    mixed = jnp.concatenate([folded, spare_cos, spare_sin], 0)
    high, low = split(dot3((table[0], table[1]), split(mixed)).reshape(out_ref.shape))
    row = lax.broadcasted_iota(jnp.int32, out_ref.shape, 1)
    out_ref[...] = jnp.where(row < HIGH, high.astype(F32), low.astype(F32)).astype(BF)


def final_body(got_ref, back_ref, basis_ref, wh_ref, wl_ref, last_ref, out_ref):
    total = got_ref[0].astype(F32)
    for index in range(1, got_ref.shape[0]):
        total = total + got_ref[index].astype(F32)
    rows = dot3(split(back_ref[...]), split(total))
    spare = jnp.sum(basis_ref[...] * total[HIGH - 1 : HIGH], 1, keepdims=True)
    out_ref[...] = dot3(split(rows), (wh_ref[...], wl_ref[...])) + spare * last_ref[...]


def to_const(table):
    return hbm(*near_const(table))


def near_const(table):
    return tuple(jnp.asarray(part) for part in np_split(table))


def shifted(values, shifts):
    count = lax.axis_size("kern")
    return [
        lax.ppermute(value, "kern", [(source, source ^ shift) for source in range(count)])
        for value, shift in zip(values, shifts)
    ]


def body(mask_values, kernels, weights, target, dose_noise):
    noise_count = lax.axis_size("noise")
    f32 = lambda *shape: jax.ShapeDtypeStruct(shape, F32)
    bf16 = lambda *shape: jax.ShapeDtypeStruct(shape, BF)
    smem = pl.BlockSpec(memory_space=pltpu.SMEM)
    columns = PERIOD // CHUNK
    shifts = range(1, KERN)

    def fixed(*shape):
        return pl.BlockSpec(shape, lambda i, *_: (0,) * len(shape))

    def chunk(rows):
        return pl.BlockSpec((rows, CHUNK), lambda i, *_: (0, i))

    def moved_spec(width):
        return pl.BlockSpec((noise_count // columns, ROWS, width), lambda i: (i, 0, 0))

    lines = to_const(LINE.T)
    basis = jnp.asarray(BASIS.T[:RANK], F32)
    last = jnp.asarray(LAST, F32)
    far_noise = dose_noise.reshape(2, noise_count, ROWS, PERIOD)
    anywhere = pl.BlockSpec(memory_space=pltpu.HBM)
    held = (mask_values, basis, *lines, last)
    moved_first, moved = call(
        front_body,
        (pltpu.HBM((noise_count, ROWS, PERIOD + FREQ), BF), pltpu.HBM((noise_count, ROWS, PERIOD), BF)),
        hbm(*held, far_noise),
        in_specs=[anywhere] * 6,
        out_specs=(anywhere, anywhere),
        scratch_shapes=[pltpu.VMEM(value.shape, value.dtype) for value in held]
        + [
            pltpu.VMEM((noise_count, ROWS, PERIOD + FREQ), BF),
            pltpu.VMEM((noise_count, ROWS, PERIOD), BF),
            pltpu.SemaphoreType.DMA((5 + 4 * PARTS,)),
        ],
    )
    place = jnp.stack([lax.axis_index(axis).astype(jnp.int32) for axis in ("kern", "noise", "tile")])
    moved_first, place = lax.optimization_barrier((moved_first, place))
    got = lax.all_to_all(moved_first, "noise", 0, 0, tiled=True)
    got, moved, kernels, weights, target, place = lax.optimization_barrier(
        (got, moved, kernels, weights, target, place)
    )
    got_last = lax.all_to_all(moved, "noise", 0, 0, tiled=True)

    def at_place(which, table):
        return [pl.BlockSpec((1,) + table.shape[1:], lambda i, place: (place[which], 0, 0))] * 2

    waves_t = WAVE.transpose(0, 2, 1)
    cross_t = CROSS.transpose(0, 2, 1)
    coef = hbm(jnp.asarray(COEF, F32))
    spec = call(
        spectrum_body,
        f32(2 * FREQ, FREQ),
        (got, *near_const(GATHER_OWN), jnp.asarray(UNFOLD, BF), jnp.asarray(COEF, F32)),
        place=place,
        grid=(1,),
        in_specs=[pl.BlockSpec((noise_count, ROWS, FREQ), lambda i, _: (0, 0, PERIOD // FREQ))]
        + at_place(0, GATHER_OWN)
        + [fixed(*UNFOLD.shape), fixed(*COEF.shape)],
        out_specs=fixed(2 * FREQ, FREQ),
    )
    specs = [spec] + shifted([spec] * len(shifts), shifts)
    field_rows = 2 * KERN * REACH
    field_shape = (PAIRS * field_rows, 2 * COARSE)
    blur = jnp.asarray(BLUR, F32)
    ins = (*specs, kernels, *to_const(WAVE), *to_const(GRID), blur)
    field, *pieces = call(
        field_body,
        (pltpu.HBM(field_shape, F32),) + (f32(ROWS, COARSE),) * KERN,
        (place, weights, *hbm(*ins)),
        in_specs=[smem] * 2 + [anywhere] * len(ins),
        out_specs=(anywhere,) + (pl.BlockSpec((ROWS, COARSE), lambda: (0, 0)),) * KERN,
        scratch_shapes=[
            pltpu.VMEM((KERN,) + spec.shape, F32),
            pltpu.VMEM(kernels.shape, F32),
            pltpu.VMEM((2,) + WAVE.shape[1:], BF),
            pltpu.VMEM((2,) + GRID.shape, BF),
            pltpu.VMEM(BLUR.shape[1:], F32),
            pltpu.VMEM(field_shape, F32),
            pltpu.VMEM((KERN * ROWS, COARSE), F32),
            pltpu.SemaphoreType.DMA((10 + PAIRS,)),
        ],
    )
    pieces = pieces[:1] + shifted(pieces[1:], shifts)
    rows = (pieces[0] + pieces[1]) + (pieces[2] + pieces[3])
    swap = [(0, 1), (1, 0)]
    rows_other = lax.ppermute(rows, "tile", swap)
    got_spec = pl.BlockSpec((noise_count, ROWS, CHUNK), lambda i: (0, 0, i))
    sums_spec = pl.BlockSpec((4, ROWS, CHUNK), lambda i: (0, 0, i))
    sums = call(
        dose_first_body,
        f32(4, ROWS, PERIOD),
        (rows, *near_const(OWN.T), got),
        grid=(columns,),
        in_specs=[fixed(ROWS, COARSE)] + [chunk(COARSE)] * 2 + [got_spec],
        out_specs=sums_spec,
    )
    (target,) = hbm(target)
    (sums,) = vmem(sums)
    inside = pl.BlockSpec(memory_space=pltpu.VMEM)
    piece_spec = pl.BlockSpec((ROWS, COARSE), lambda: (0, 0))
    edges, send = call(
        dose_edge_body,
        (f32(ROWS, 2 * EDGE), f32(ROWS, COARSE)),
        (place, sums, rows_other, target, got, got_last, *to_const(CROSS), *to_const(cross_t)),
        in_specs=[smem, inside, piece_spec, anywhere]
        + [pl.BlockSpec(memory_space=pl.ANY)] * 2
        + [anywhere] * 4,
        out_specs=(piece_spec, piece_spec),
        scratch_shapes=[
            pltpu.VMEM((4, noise_count, ROWS, EDGE), BF),
            pltpu.VMEM((2, ROWS, EDGE), BF),
            pltpu.VMEM((2,) + CROSS.shape[1:], BF),
            pltpu.VMEM((2,) + cross_t.shape[1:], BF),
            pltpu.SemaphoreType.DMA((10,)),
        ],
    )
    grad_other = lax.ppermute(send, "tile", swap)
    blur_t, fold = jnp.asarray(BLUR.transpose(0, 2, 1), F32), jnp.asarray(UNFOLD.T, BF)
    ins = (field, kernels, *to_const(waves_t), *to_const(GRID.T), blur_t, *to_const(SPREAD), fold, *coef)
    held = [
        (field_shape, F32),
        (kernels.shape, F32),
        ((2,) + waves_t.shape[1:], BF),
        ((2,) + GRID.T.shape, BF),
        (BLUR.shape[:0:-1], F32),
        ((2,) + SPREAD.shape, BF),
        (fold.shape, BF),
        (COEF.shape, F32),
    ]
    grad_own, *staged = call(
        dose_body,
        (f32(ROWS, COARSE),) + tuple(pltpu.VMEM(shape, dtype) for shape, dtype in held),
        (place, sums, edges, target, got_last, *to_const(OWN), *hbm(*ins)),
        grid=(columns,),
        in_specs=[smem, sums_spec, fixed(ROWS, 2 * EDGE), chunk(ROWS), got_spec]
        + [pl.BlockSpec((CHUNK, COARSE), lambda i: (i, 0))] * 2
        + [anywhere] * len(ins),
        out_specs=(fixed(ROWS, COARSE),) + (inside,) * len(held),
        scratch_shapes=[pltpu.SemaphoreType.DMA((len(ins),))],
    )
    grad = grad_own + grad_other
    grads = [grad] + shifted([grad] * len(shifts), shifts)
    spread = call(
        back_body,
        bf16(BLOCKS, RANK, FREQ),
        (place, weights, *grads, *vmem(*staged)),
        in_specs=[smem] * 2 + [piece_spec] * KERN + [inside] * len(held),
        out_specs=pl.BlockSpec((BLOCKS, RANK, FREQ), lambda: (0, 0, 0)),
        scratch_shapes=[pltpu.VMEM((KERN * ROWS, COARSE), F32)],
    )
    back = lax.all_to_all(spread, ("kern", "noise"), 0, 0, tiled=True)
    return call(
        final_body,
        f32(ROWS, PERIOD),
        (back, jnp.asarray(BASIS_BACK, F32), jnp.asarray(BASIS, F32), *(jnp.asarray(t) for t in np_split(LINE)), jnp.asarray(LAST, F32)),
    )


def solution(mesh):
    return jax.shard_map(
        body,
        mesh=mesh,
        in_specs=(
            P(("kern", "noise"), "tile"),
            P("kern", None, None, None),
            P("kern"),
            P(("kern", "noise"), "tile"),
            P("noise", "kern", "tile"),
        ),
        out_specs=P(("kern", "noise"), "tile"),
        check_vma=False,
    )
```

```python
import math

import jax
import jax.numpy as jnp
import numpy as np
from jax import lax
from jax.experimental import pallas as pl
from jax.experimental.pallas import tpu as pltpu
from jax.sharding import PartitionSpec as P

HALO = 16
FREQ = 128
COARSE = 256
PERIOD = 2048
ROWS = 32
REACH = 24
EDGE = 128
GROUP = 6
PAIRS = GROUP // 2
KERN = 4
SAMPLES = 32
RANK = 16
MIB = 32
BF = jnp.bfloat16
F32 = jnp.float32


def np_split(table):
    table = np.asarray(table, np.float32)
    high = table.astype(jnp.bfloat16)
    low = (table - high.astype(np.float32)).astype(jnp.bfloat16)
    return high, low


def np_waves(ids):
    centred = np.arange(FREQ) - FREQ // 2
    angles = 2.0 * np.pi * ((centred[:, None] * ids[None, :]) % PERIOD) / PERIOD
    return np.cos(angles), np.sin(angles)


def line_tables():
    half = FREQ // 2
    pixels = np.arange(PERIOD)
    angle = lambda f: 2.0 * np.pi * ((f[:, None] * pixels[None, :]) % PERIOD) / PERIOD
    line = np.concatenate([np.cos(angle(np.arange(half + 1))), np.sin(angle(np.arange(1, half)))], 0)
    last = np.sin(angle(np.array([half])))
    unfold = np.zeros((FREQ, 2 * FREQ))
    for j in range(FREQ):
        f = j - half
        unfold[abs(f), j] = 1.0
        if 0 < abs(f) < half:
            unfold[half + abs(f), FREQ + j] = np.sign(f)
    row = np.arange(ROWS) - (ROWS - 1) / 2.0
    fine = np.arange(-half, half + 0.01, 0.25)
    wave = np.exp(2j * np.pi * np.outer(row, fine) / PERIOD)
    basis = np.linalg.svd(np.concatenate([wave.real, wave.imag], 1))[0][:, : RANK - 1]
    basis = np.concatenate([basis, np.zeros((ROWS, FREQ - RANK + 1))], 1)
    freqs = np.arange(FREQ) - half
    coef = np.exp(2j * np.pi * np.outer(freqs, row) / PERIOD) @ basis
    blocks = PERIOD // ROWS
    centre = ROWS * np.arange(blocks) + (ROWS - 1) / 2.0
    phase = np.exp(2j * np.pi * np.outer(freqs, centre) / PERIOD)
    rows = phase[:, :, None] * coef[:, None, :RANK]
    rows[:, :, RANK - 1] = 0.0
    spare = np.zeros_like(rows)
    spare[:, :, RANK - 1] = phase
    rows = rows.reshape(FREQ, blocks * RANK)
    spare = spare.reshape(FREQ, blocks * RANK)
    gather = np.concatenate([rows.real, rows.imag, spare.real, spare.imag], 0)
    return line, last, unfold, basis, np.stack([coef.real, coef.imag]), gather


def tables():
    ccos, csin = np_waves(np.arange(COARSE) * (PERIOD // COARSE))
    grid = np.block([[ccos, csin], [-csin, ccos]]) / FREQ
    offsets = np.arange(-HALO, HALO + 1)
    taps = np.exp(-(offsets.astype(np.float64) ** 2) / (2.0 * (HALO / 2.0) ** 2))
    taps = taps / taps.sum()
    nodes = np.cos(np.pi * (np.arange(REACH) + 0.5) / REACH) * (ROWS / 2 + HALO - 0.5) + (ROWS - 1) / 2.0
    freqs = np.arange(1 - FREQ, FREQ)
    at = lambda places: np.exp(2j * np.pi * np.outer(places, freqs) / PERIOD)
    both = lambda value: np.concatenate([value.real, value.imag], 1)
    row_blur = np.zeros((PERIOD // ROWS, ROWS, REACH))
    near = np.arange(-HALO, ROWS + HALO)
    full = np.zeros((ROWS, ROWS + 2 * HALO))
    for row in range(ROWS):
        full[row, row : row + 2 * HALO + 1] = taps
    for block in range(PERIOD // ROWS):
        inside = (near + block * ROWS >= 0) & (near + block * ROWS < PERIOD)
        wanted = both((full * inside) @ at(near))
        row_blur[block] = np.linalg.lstsq(both(at(nodes)).T, wanted.T, rcond=1e-12)[0].T
    places = ROWS * np.arange(PERIOD // ROWS)[:, None] + nodes[None, :]
    angles = 2.0 * np.pi * (places[:, :, None] * (np.arange(FREQ) - FREQ // 2)) / PERIOD
    cos, sin = np.cos(angles), np.sin(angles)
    reach = np.concatenate([np.concatenate([cos, -sin], 2), np.concatenate([sin, cos], 2)], 1)
    shift = np.arange(PERIOD)[:, None] - (PERIOD // COARSE) * np.arange(COARSE)[None, :]
    freqs = np.arange(1, FREQ)
    line = (1.0 + 2.0 * np.cos(2.0 * np.pi * np.outer(np.arange(PERIOD), freqs) / PERIOD).sum(1)) / COARSE
    interp = line[shift % PERIOD]
    padded = np.zeros((PERIOD + 2 * HALO, COARSE))
    padded[HALO:-HALO] = interp
    own = np.zeros((PERIOD, COARSE))
    for index, tap in enumerate(taps):
        own += tap * padded[index : index + PERIOD]
    cross = np.zeros((2, COARSE, 2 * EDGE))
    for column in range(HALO):
        for index, offset in enumerate(offsets):
            if column + offset < 0:
                cross[1, :, column] += taps[index] * interp[PERIOD + column + offset]
            place = PERIOD - 1 - column + offset
            if place >= PERIOD:
                cross[0, :, 2 * EDGE - 1 - column] += taps[index] * interp[place - PERIOD]
    return reach, grid, row_blur, own, cross


LINE, LAST, UNFOLD, BASIS, COEF, GATHER = line_tables()
REACH_WAVES, GRID, ROW_BLUR, OWN, CROSS = tables()
BLOCKS = PERIOD // ROWS
GROUP_BLOCKS = BLOCKS // KERN
WAVE = REACH_WAVES
WAVE = WAVE.reshape(KERN, GROUP_BLOCKS, 2 * REACH, 2 * FREQ).transpose(1, 0, 2, 3)
WAVE = WAVE.reshape(GROUP_BLOCKS, KERN * 2 * REACH, 2 * FREQ)
LOW = 4
HIGH = RANK - LOW - 1
SPREAD = GATHER.reshape(4 * FREQ, BLOCKS, RANK)
SPARE = SPREAD[:, :, RANK - 1 :]
SPREAD = np.concatenate([SPREAD[:, :, : HIGH - 1], SPARE, SPREAD[:, :, :LOW], SPARE], 2)
SPREAD = SPREAD.reshape(4 * FREQ, BLOCKS * RANK).T
BASIS_BACK = np.zeros((ROWS, RANK))
BASIS_BACK[:, : HIGH - 1] = BASIS[:, : HIGH - 1]
BASIS_BACK[:, HIGH : HIGH + LOW] = BASIS[:, :LOW]
GATHER_OWN = GATHER.reshape(4 * FREQ, KERN, GROUP_BLOCKS * RANK).transpose(1, 0, 2)
BLUR = np.zeros((GROUP_BLOCKS, KERN, ROWS, KERN, REACH))
for group in range(KERN):
    BLUR[:, group, :, group] = ROW_BLUR.reshape(KERN, GROUP_BLOCKS, ROWS, REACH)[group]
BLUR = BLUR.reshape(GROUP_BLOCKS, KERN * ROWS, KERN * REACH)


def split(value):
    high = value.astype(BF)
    return high, (value - high.astype(F32)).astype(BF)


NN = (((1,), (0,)), ((), ()))


def dot3(left, right):
    lh, ll = left
    rh, rl = right

    def one(a, b):
        return lax.dot_general(a, b, NN, preferred_element_type=F32)

    count = lh.shape[0]
    if count > 64:
        return one(jnp.concatenate([lh, ll, lh], 1), jnp.concatenate([rh, rh, rl], 0))
    both = one(jnp.concatenate([lh, ll], 0), rh)
    return both[:count] + (one(lh, rl) + both[count:])


def dot_exact(left, right):
    high, low = left
    return jnp.dot(high, right, preferred_element_type=F32) + jnp.dot(low, right, preferred_element_type=F32)


def call(body, out_shape, args, place=None, **kw):
    params = pltpu.CompilerParams(vmem_limit_bytes=MIB * 1024 * 1024)
    if place is None:
        return pl.pallas_call(body, out_shape=out_shape, compiler_params=params, **kw)(*args)
    grid_spec = pltpu.PrefetchScalarGridSpec(num_scalar_prefetch=1, **kw)
    return pl.pallas_call(body, out_shape=out_shape, compiler_params=params, grid_spec=grid_spec)(place, *args)


def hbm(*values):
    return tuple(pltpu.with_memory_space_constraint(value, pltpu.HBM) for value in values)


def vmem(*values):
    return tuple(pltpu.with_memory_space_constraint(value, pltpu.VMEM) for value in values)


CHUNK = 512
LANES = 256
PARTS = 4


def fetches(sources, targets, sems):
    copies = [
        pltpu.make_async_copy(source, target, sems.at[index])
        for index, (source, target) in enumerate(zip(sources, targets))
    ]
    for copy in copies:
        copy.start()
    return copies


def front_body(mask_ref, basis_ref, lh_ref, ll_ref, last_ref, noise_ref, first_ref, second_ref, *scratch):
    mask, basis, lh, ll, last, first, second, sems = scratch
    tables = [
        pltpu.make_async_copy(source, target, sems.at[index])
        for index, (source, target) in enumerate(
            zip((mask_ref, basis_ref, lh_ref, ll_ref, last_ref), (mask, basis, lh, ll, last))
        )
    ]
    part = first.shape[0] // PARTS
    loads, stores = [], []
    for index in range(2 * PARTS):
        which, rows = index // PARTS, pl.ds(index % PARTS * part, part)
        held, out_ref = (first, first_ref) if which == 0 else (second, second_ref)
        there = held.at[rows, :, pl.ds(0, PERIOD)] if which == 0 else held.at[rows]
        loads.append(pltpu.make_async_copy(noise_ref.at[which, rows], there, sems.at[5 + index]))
        stores.append(pltpu.make_async_copy(held.at[rows], out_ref.at[rows], sems.at[5 + 2 * PARTS + index]))
    for copy in tables + loads:
        copy.start()
    for copy in tables:
        copy.wait()
    transmit = (2.0 * mask[...] - 1.0) * (1.0 / PERIOD)
    rows = dot3(split(basis[...]), split(transmit))
    line = dot3(split(rows), (lh[...], ll[...]))
    row = lax.broadcasted_iota(jnp.int32, (RANK, FREQ), 0)
    lane = lax.broadcasted_iota(jnp.int32, (RANK, FREQ), 1)
    apart = jnp.sum(rows * last[...], 1, keepdims=True)
    apart = jnp.sum(jnp.where(row == lane, apart, 0.0), 0, keepdims=True)
    packed = jnp.concatenate(split(jnp.where(row == RANK - 1, apart, line)), 0)
    for index in range(first.shape[0]):
        first[index, :, PERIOD:] = packed
    for load, store in zip(loads, stores):
        load.wait()
        store.start()
    for store in stores:
        store.wait()


def spectrum_body(_, got_ref, gh_ref, gl_ref, unfold_ref, coef_ref, out_ref):
    high = got_ref[:, :RANK].reshape(GROUP_BLOCKS * RANK, FREQ)
    low = got_ref[:, RANK:].reshape(GROUP_BLOCKS * RANK, FREQ)
    both = dot3((gh_ref[0], gl_ref[0]), (high, low))
    waves = dot_exact(split(both[: 2 * FREQ]), unfold_ref[...])
    spare_cos, spare_sin = both[2 * FREQ : 3 * FREQ], both[3 * FREQ :]
    coef_re, coef_im = coef_ref[0], coef_ref[1]
    last_cos = jnp.sum(coef_re * spare_cos - coef_im * spare_sin, 1, keepdims=True)
    last_sin = jnp.sum(coef_re * spare_sin + coef_im * spare_cos, 1, keepdims=True)
    first = lax.broadcasted_iota(jnp.int32, (FREQ, FREQ), 1) == 0
    cos_cos, cos_sin = waves[:FREQ, :FREQ], waves[:FREQ, FREQ:]
    sin_cos, sin_sin = waves[FREQ:, :FREQ], waves[FREQ:, FREQ:]
    out_ref[:FREQ] = cos_cos - sin_sin + jnp.where(first, last_sin, 0.0)
    out_ref[FREQ:] = jnp.where(first, last_cos, 0.0) - cos_sin - sin_cos


def field_body(place_ref, weight_ref, *refs):
    ins, outs, scratch = refs[:10], refs[10 : 11 + KERN], refs[11 + KERN :]
    spec_refs, (kern_ref, wh_ref, wl_ref, gh_ref, gl_ref, blur_ref) = ins[:KERN], ins[KERN:]
    field_ref, piece_refs = outs[0], outs[1:]
    specs, kern, wave, grid, blur, field, total_ref, sems = scratch
    block = place_ref[1]
    copies = fetches(
        list(spec_refs) + [kern_ref, wh_ref.at[block], wl_ref.at[block], gh_ref, gl_ref, blur_ref.at[block]],
        [specs.at[index] for index in range(KERN)]
        + [kern, wave.at[0], wave.at[1], grid.at[0], grid.at[1], blur],
        sems,
    )
    for copy in copies[:7]:
        copy.wait()
    spec = (specs[0] + specs[1]) + (specs[2] + specs[3])
    spec_re = spec[:FREQ]
    spec_im = spec[FREQ:]
    half = KERN * REACH
    total, stores = None, []
    for pair in range(PAIRS):
        near_re, near_im = [], []
        for index in (2 * pair, 2 * pair + 1):
            kern_re, kern_im = kern[index, 0], kern[index, 1]
            near_re.append(kern_re * spec_re - kern_im * spec_im)
            near_im.append(kern_re * spec_im + kern_im * spec_re)
        near = jnp.concatenate([jnp.concatenate(near_re, 1), jnp.concatenate(near_im, 1)], 0)
        left = dot3((wave[0], wave[1]), split(near))
        lefts = []
        for index in range(2):
            lanes = slice(index * FREQ, (index + 1) * FREQ)
            for group in range(KERN):
                first = 2 * group * REACH
                re, im = left[first : first + REACH, lanes], left[first + REACH : first + 2 * REACH, lanes]
                lefts.append(jnp.concatenate([re, im], 1))
        if pair == 0:
            for copy in copies[7:9]:
                copy.wait()
        held = field.at[pl.ds(pair * 2 * half, 2 * half)]
        held[...] = dot3(split(jnp.concatenate(lefts, 0)), (grid[0], grid[1]))
        stores.append(pltpu.make_async_copy(held, field_ref.at[pl.ds(pair * 2 * half, 2 * half)], sems.at[10 + pair]))
        stores[-1].start()
        for index in range(2):
            own = held[index * half : (index + 1) * half]
            own = own * own
            own = weight_ref[2 * pair + index] * (own[:, :COARSE] + own[:, COARSE:])
            total = own if total is None else total + own
    copies[9].wait()
    total_ref[...] = dot3(split(blur[...]), split(total))
    for shift, piece_ref in enumerate(piece_refs):
        group = jnp.bitwise_xor(place_ref[0], shift)
        piece_ref[...] = total_ref[pl.ds(pl.multiple_of(group * ROWS, ROWS), ROWS)]
    for store in stores:
        store.wait()


def sample_sums(noise_ref, place, acid, sums):
    sum_u, sum_q, sum_qu = sums
    quarter = 0.25 * acid
    base = acid - 2.0
    for index in range(noise_ref.shape[0]):
        noise = noise_ref[(index,) + place].astype(F32)
        u = jnp.tanh(quarter * noise + base)
        q = (1.0 - u * u) * (1.0 + 0.25 * noise)
        sum_u, sum_q, sum_qu = sum_u + u, sum_q + q, sum_qu + q * u
    return sum_u, sum_q, sum_qu


def places(columns):
    width = min(columns, LANES)
    for row in range(0, ROWS, 16):
        for col in range(0, columns, width):
            yield slice(row, row + 16), slice(col, col + width)


def dose_first_body(rows_ref, oh_ref, ol_ref, noise_ref, sums_ref):
    sums_ref[0] = dot3(split(rows_ref[...]), (oh_ref[...], ol_ref[...]))
    for place in places(PERIOD):
        acid = sums_ref[(0,) + place]
        zero = jnp.zeros(acid.shape, F32)
        for index, value in enumerate(sample_sums(noise_ref, place, acid, (zero, zero, zero))):
            sums_ref[(index + 1,) + place] = value


def acid_grad(sums, target):
    sum_u, sum_q, sum_qu = sums
    inner = 0.25 - sum_u * (1.0 / SAMPLES) - 0.5 * target.astype(F32)
    return (1.0 / 16.0) * (sum_q * inner + 1.25 * sum_qu)


def dose_edge_body(place_ref, sums_ref, other_ref, *refs):
    ins, (grad_ref, send_ref), (held, target, cross, cross_t, sems) = refs[:7], refs[7:9], refs[9:]
    target_ref, first_ref, second_ref, ch_ref, cl_ref, th_ref, tl_ref = ins
    tile = place_ref[2]
    sides = [pl.ds(0, EDGE), pl.ds(PERIOD - EDGE, EDGE)]
    copies = fetches(
        [ch_ref.at[tile], cl_ref.at[tile]]
        + [ref.at[:, :, side] for side in sides for ref in (first_ref, second_ref)]
        + [target_ref.at[:, side] for side in sides]
        + [th_ref.at[tile], tl_ref.at[tile]],
        [cross.at[0], cross.at[1]]
        + [held.at[index] for index in range(4)]
        + [target.at[index] for index in range(2)]
        + [cross_t.at[0], cross_t.at[1]],
        sems,
    )
    for copy in copies[:2]:
        copy.wait()
    halo = dot3(split(other_ref[...]), (cross[0], cross[1]))
    for copy in copies[2:8]:
        copy.wait()
    grads = []
    for side in range(2):
        columns = []
        for row, lanes in places(EDGE):
            place = (row, lanes)
            there = slice(side * (PERIOD - EDGE), side * (PERIOD - EDGE) + EDGE)
            acid = sums_ref[0, row, there] + halo[row, side * EDGE : (side + 1) * EDGE]
            zero = jnp.zeros(acid.shape, F32)
            sums = sample_sums(held.at[2 * side], place, acid, (zero, zero, zero))
            sums = sample_sums(held.at[2 * side + 1], place, acid, sums)
            columns.append(acid_grad(sums, target[(side,) + place]))
        grads.append(jnp.concatenate(columns, 0))
    grad = jnp.concatenate(grads, 1)
    grad_ref[...] = grad
    for copy in copies[8:]:
        copy.wait()
    send_ref[...] = dot3(split(grad), (cross_t[0], cross_t[1]))


def dose_body(place_ref, sums_ref, edge_ref, target_ref, noise_ref, oh_ref, ol_ref, *refs):
    ins, out_ref, outs, (target, noise, own, sems) = refs[:11], refs[11], refs[12:20], refs[20:]
    field_ref, kern_ref, wh_ref, wl_ref, gh_ref, gl_ref, blur_ref, th_ref, tl_ref, fold_ref, coef_ref = ins
    field, kern, wave, grid, blur, table, fold, coef = outs
    block = place_ref[1]
    chunks = [pl.ds(first, CHUNK) for first in range(0, PERIOD, CHUNK)]
    copies = fetches(
        [target_ref]
        + [ref for part in chunks for ref in (noise_ref.at[:, :, part], oh_ref.at[part], ol_ref.at[part])]
        + [field_ref, kern_ref, wh_ref.at[block], wl_ref.at[block], gh_ref, gl_ref]
        + [blur_ref.at[block], th_ref, tl_ref, fold_ref, coef_ref],
        [target]
        + [
            ref
            for index, part in enumerate(chunks)
            for ref in (noise.at[index], own.at[0, part], own.at[1, part])
        ]
        + [field, kern, wave.at[0], wave.at[1], grid.at[0], grid.at[1]]
        + [blur, table.at[0], table.at[1], fold, coef],
        sems,
    )
    copies[0].wait()
    total = None
    for index in range(len(chunks)):
        for copy in copies[1 + 3 * index : 4 + 3 * index]:
            copy.wait()
        for col in range(0, CHUNK, LANES):
            first = index * CHUNK + col
            grads = []
            for row in range(0, ROWS, 16):
                place = (slice(row, row + 16), slice(first, first + LANES))
                acid, *sums = [sums_ref[(which,) + place] for which in range(4)]
                here = (slice(row, row + 16), slice(col, col + LANES))
                grads.append(acid_grad(sample_sums(noise.at[index], here, acid, sums), target[place]))
            grad = jnp.concatenate(grads, 0)
            if first == 0:
                grad = jnp.concatenate([edge_ref[:, :EDGE], grad[:, EDGE:]], 1)
            if first == PERIOD - LANES:
                grad = jnp.concatenate([grad[:, : LANES - EDGE], edge_ref[:, EDGE:]], 1)
            lines = slice(first, first + LANES)
            part = dot3(split(grad), (own[0, lines], own[1, lines]))
            total = part if total is None else total + part
    out_ref[...] = total
    for copy in copies[1 + 3 * len(chunks) :]:
        copy.wait()


def back_body(place_ref, weight_ref, *refs):
    piece_refs, (field, kern, wave, grid, blur, table, fold, coef) = refs[:KERN], refs[KERN : KERN + 8]
    out_ref, rows = refs[KERN + 8 :]
    for shift, piece_ref in enumerate(piece_refs):
        first = jnp.bitwise_xor(place_ref[0], shift) * ROWS
        rows[pl.ds(pl.multiple_of(first, ROWS), ROWS)] = piece_ref[...]
    part = 2.0 * dot3(split(blur[...]), split(rows[...]))
    grad = jnp.concatenate([part, part], 1)
    half = KERN * REACH
    sum_re = sum_im = None
    for pair in range(PAIRS):
        pulled = [
            field[index * half : (index + 1) * half] * (weight_ref[index] * grad)
            for index in (2 * pair, 2 * pair + 1)
        ]
        lefts = dot3(split(jnp.concatenate(pulled, 0)), (grid[0], grid[1]))
        stack = []
        for index in range(2):
            column = []
            for which in range(KERN):
                first = index * half + which * REACH
                left = lefts[first : first + REACH]
                column += [left[:, :FREQ], left[:, FREQ:]]
            stack.append(jnp.concatenate(column, 0))
        near = dot3((wave[0], wave[1]), split(jnp.concatenate(stack, 1)))
        for index in range(2):
            near_re = near[:FREQ, index * FREQ : (index + 1) * FREQ]
            near_im = near[FREQ:, index * FREQ : (index + 1) * FREQ]
            kern_re, kern_im = kern[2 * pair + index, 0], kern[2 * pair + index, 1]
            own_re = kern_re * near_re + kern_im * near_im
            own_im = kern_re * near_im - kern_im * near_re
            sum_re = own_re if sum_re is None else sum_re + own_re
            sum_im = own_im if sum_im is None else sum_im + own_im
    grad_re, grad_im = sum_re * (2.0 / PERIOD), sum_im * (2.0 / PERIOD)
    mix = jnp.concatenate(
        [jnp.concatenate([grad_re, -grad_im], 1), jnp.concatenate([-grad_im, -grad_re], 1)], 0
    )
    folded = dot_exact(split(mix), fold[...])
    coef_re, coef_im = coef[0], coef[1]
    by_cos, by_sin = grad_im[:, :1], grad_re[:, :1]
    spare_cos = coef_re * by_cos + coef_im * by_sin
    spare_sin = coef_re * by_sin - coef_im * by_cos
    mixed = jnp.concatenate([folded, spare_cos, spare_sin], 0)
    high, low = split(dot3((table[0], table[1]), split(mixed)).reshape(out_ref.shape))
    row = lax.broadcasted_iota(jnp.int32, out_ref.shape, 1)
    out_ref[...] = jnp.where(row < HIGH, high.astype(F32), low.astype(F32)).astype(BF)


def final_body(got_ref, back_ref, basis_ref, wh_ref, wl_ref, last_ref, out_ref):
    total = got_ref[0].astype(F32)
    for index in range(1, got_ref.shape[0]):
        total = total + got_ref[index].astype(F32)
    rows = dot3(split(back_ref[...]), split(total))
    spare = jnp.sum(basis_ref[...] * (total[HIGH - 1 : HIGH] + total[RANK - 1 :]), 1, keepdims=True)
    out_ref[...] = dot3(split(rows), (wh_ref[...], wl_ref[...])) + spare * last_ref[...]


def to_const(table):
    return hbm(*near_const(table))


def near_const(table):
    return tuple(jnp.asarray(part) for part in np_split(table))


def shifted(values, shifts):
    count = lax.axis_size("kern")
    return [
        lax.ppermute(value, "kern", [(source, source ^ shift) for source in range(count)])
        for value, shift in zip(values, shifts)
    ]


def body(mask_values, kernels, weights, target, dose_noise):
    noise_count = lax.axis_size("noise")
    f32 = lambda *shape: jax.ShapeDtypeStruct(shape, F32)
    bf16 = lambda *shape: jax.ShapeDtypeStruct(shape, BF)
    smem = pl.BlockSpec(memory_space=pltpu.SMEM)
    columns = PERIOD // CHUNK
    shifts = range(1, KERN)

    def fixed(*shape):
        return pl.BlockSpec(shape, lambda i, *_: (0,) * len(shape))

    def chunk(rows):
        return pl.BlockSpec((rows, CHUNK), lambda i, *_: (0, i))

    def moved_spec(width):
        return pl.BlockSpec((noise_count // columns, ROWS, width), lambda i: (i, 0, 0))

    lines = to_const(LINE.T)
    basis = jnp.asarray(BASIS.T[:RANK], F32)
    last = jnp.asarray(LAST, F32)
    far_noise = dose_noise.reshape(2, noise_count, ROWS, PERIOD)
    anywhere = pl.BlockSpec(memory_space=pltpu.HBM)
    held = (mask_values, basis, *lines, last)
    moved_first, moved = call(
        front_body,
        (pltpu.HBM((noise_count, ROWS, PERIOD + FREQ), BF), pltpu.HBM((noise_count, ROWS, PERIOD), BF)),
        hbm(*held, far_noise),
        in_specs=[anywhere] * 6,
        out_specs=(anywhere, anywhere),
        scratch_shapes=[pltpu.VMEM(value.shape, value.dtype) for value in held]
        + [
            pltpu.VMEM((noise_count, ROWS, PERIOD + FREQ), BF),
            pltpu.VMEM((noise_count, ROWS, PERIOD), BF),
            pltpu.SemaphoreType.DMA((5 + 4 * PARTS,)),
        ],
    )
    place = jnp.stack([lax.axis_index(axis).astype(jnp.int32) for axis in ("kern", "noise", "tile")])
    moved_first, place = lax.optimization_barrier((moved_first, place))
    got = lax.all_to_all(moved_first, "noise", 0, 0, tiled=True)
    got, moved, kernels, weights, target, place = lax.optimization_barrier(
        (got, moved, kernels, weights, target, place)
    )
    got_last = lax.all_to_all(moved, "noise", 0, 0, tiled=True)

    def at_place(which, table):
        return [pl.BlockSpec((1,) + table.shape[1:], lambda i, place: (place[which], 0, 0))] * 2

    waves_t = WAVE.transpose(0, 2, 1)
    cross_t = CROSS.transpose(0, 2, 1)
    coef = hbm(jnp.asarray(COEF, F32))
    spec = call(
        spectrum_body,
        f32(2 * FREQ, FREQ),
        (got, *near_const(GATHER_OWN), jnp.asarray(UNFOLD, BF), jnp.asarray(COEF, F32)),
        place=place,
        grid=(1,),
        in_specs=[pl.BlockSpec((noise_count, ROWS, FREQ), lambda i, _: (0, 0, PERIOD // FREQ))]
        + at_place(0, GATHER_OWN)
        + [fixed(*UNFOLD.shape), fixed(*COEF.shape)],
        out_specs=fixed(2 * FREQ, FREQ),
    )
    specs = [spec] + shifted([spec] * len(shifts), shifts)
    field_rows = 2 * KERN * REACH
    field_shape = (PAIRS * field_rows, 2 * COARSE)
    blur = jnp.asarray(BLUR, F32)
    ins = (*specs, kernels, *to_const(WAVE), *to_const(GRID), blur)
    field, *pieces = call(
        field_body,
        (pltpu.HBM(field_shape, F32),) + (f32(ROWS, COARSE),) * KERN,
        (place, weights, *hbm(*ins)),
        in_specs=[smem] * 2 + [anywhere] * len(ins),
        out_specs=(anywhere,) + (pl.BlockSpec((ROWS, COARSE), lambda: (0, 0)),) * KERN,
        scratch_shapes=[
            pltpu.VMEM((KERN,) + spec.shape, F32),
            pltpu.VMEM(kernels.shape, F32),
            pltpu.VMEM((2,) + WAVE.shape[1:], BF),
            pltpu.VMEM((2,) + GRID.shape, BF),
            pltpu.VMEM(BLUR.shape[1:], F32),
            pltpu.VMEM(field_shape, F32),
            pltpu.VMEM((KERN * ROWS, COARSE), F32),
            pltpu.SemaphoreType.DMA((10 + PAIRS,)),
        ],
    )
    pieces = pieces[:1] + shifted(pieces[1:], shifts)
    rows = (pieces[0] + pieces[1]) + (pieces[2] + pieces[3])
    swap = [(0, 1), (1, 0)]
    rows_other = lax.ppermute(rows, "tile", swap)
    sums = call(
        dose_first_body,
        f32(4, ROWS, PERIOD),
        (rows, *near_const(OWN.T), got),
        grid=(1,),
        in_specs=[fixed(ROWS, COARSE)] + [fixed(COARSE, PERIOD)] * 2 + [fixed(noise_count, ROWS, PERIOD)],
        out_specs=pl.BlockSpec((4, ROWS, PERIOD), lambda i: (0, 0, 0)),
    )
    (target,) = hbm(target)
    (sums,) = vmem(sums)
    inside = pl.BlockSpec(memory_space=pltpu.VMEM)
    piece_spec = pl.BlockSpec((ROWS, COARSE), lambda: (0, 0))
    edges, send = call(
        dose_edge_body,
        (f32(ROWS, 2 * EDGE), f32(ROWS, COARSE)),
        (place, sums, rows_other, target, got, got_last, *to_const(CROSS), *to_const(cross_t)),
        in_specs=[smem, inside, piece_spec, anywhere]
        + [pl.BlockSpec(memory_space=pl.ANY)] * 2
        + [anywhere] * 4,
        out_specs=(piece_spec, piece_spec),
        scratch_shapes=[
            pltpu.VMEM((4, noise_count, ROWS, EDGE), BF),
            pltpu.VMEM((2, ROWS, EDGE), BF),
            pltpu.VMEM((2,) + CROSS.shape[1:], BF),
            pltpu.VMEM((2,) + cross_t.shape[1:], BF),
            pltpu.SemaphoreType.DMA((10,)),
        ],
    )
    grad_other = lax.ppermute(send, "tile", swap)
    blur_t, fold = jnp.asarray(BLUR.transpose(0, 2, 1), F32), jnp.asarray(UNFOLD.T, BF)
    ins = (field, kernels, *to_const(waves_t), *to_const(GRID.T), blur_t, *to_const(SPREAD), fold, *coef)
    held = [
        (field_shape, F32),
        (kernels.shape, F32),
        ((2,) + waves_t.shape[1:], BF),
        ((2,) + GRID.T.shape, BF),
        (BLUR.shape[:0:-1], F32),
        ((2,) + SPREAD.shape, BF),
        (fold.shape, BF),
        (COEF.shape, F32),
    ]
    grad_own, *staged = call(
        dose_body,
        (f32(ROWS, COARSE),) + tuple(pltpu.VMEM(shape, dtype) for shape, dtype in held),
        (place, sums, edges, target, got_last, *to_const(OWN), *hbm(*ins)),
        in_specs=[smem, inside, piece_spec, anywhere, pl.BlockSpec(memory_space=pl.ANY)]
        + [anywhere] * (2 + len(ins)),
        out_specs=(piece_spec,) + (inside,) * len(held),
        scratch_shapes=[
            pltpu.VMEM((ROWS, PERIOD), BF),
            pltpu.VMEM((columns, noise_count, ROWS, CHUNK), BF),
            pltpu.VMEM((2,) + OWN.shape, BF),
            pltpu.SemaphoreType.DMA((1 + 3 * columns + len(ins),)),
        ],
    )
    grad = grad_own + grad_other
    grads = [grad] + shifted([grad] * len(shifts), shifts)
    spread = call(
        back_body,
        bf16(BLOCKS, RANK, FREQ),
        (place, weights, *grads, *vmem(*staged)),
        in_specs=[smem] * 2 + [piece_spec] * KERN + [inside] * len(held),
        out_specs=pl.BlockSpec((BLOCKS, RANK, FREQ), lambda: (0, 0, 0)),
        scratch_shapes=[pltpu.VMEM((KERN * ROWS, COARSE), F32)],
    )
    back = lax.all_to_all(spread, ("kern", "noise"), 0, 0, tiled=True)
    return call(
        final_body,
        f32(ROWS, PERIOD),
        (back, jnp.asarray(BASIS_BACK, F32), jnp.asarray(BASIS, F32), *(jnp.asarray(t) for t in np_split(LINE)), jnp.asarray(LAST, F32)),
    )


def solution(mesh):
    return jax.shard_map(
        body,
        mesh=mesh,
        in_specs=(
            P(("kern", "noise"), "tile"),
            P("kern", None, None, None),
            P("kern"),
            P(("kern", "noise"), "tile"),
            P("noise", "kern", "tile"),
        ),
        out_specs=P(("kern", "noise"), "tile"),
        check_vma=False,
    )
```

```python
import math

import jax
import jax.numpy as jnp
import numpy as np
from jax import lax
from jax.experimental import pallas as pl
from jax.experimental.pallas import tpu as pltpu
from jax.sharding import PartitionSpec as P

HALO = 16
FREQ = 128
COARSE = 256
PERIOD = 2048
ROWS = 32
REACH = 24
EDGE = 128
GROUP = 6
PAIRS = GROUP // 2
KERN = 4
SAMPLES = 32
RANK = 16
MIB = 32
BF = jnp.bfloat16
F32 = jnp.float32


def np_split(table):
    table = np.asarray(table, np.float32)
    high = table.astype(jnp.bfloat16)
    low = (table - high.astype(np.float32)).astype(jnp.bfloat16)
    return high, low


def np_waves(ids):
    centred = np.arange(FREQ) - FREQ // 2
    angles = 2.0 * np.pi * ((centred[:, None] * ids[None, :]) % PERIOD) / PERIOD
    return np.cos(angles), np.sin(angles)


def line_tables():
    half = FREQ // 2
    pixels = np.arange(PERIOD)
    angle = lambda f: 2.0 * np.pi * ((f[:, None] * pixels[None, :]) % PERIOD) / PERIOD
    line = np.concatenate([np.cos(angle(np.arange(half + 1))), np.sin(angle(np.arange(1, half)))], 0)
    last = np.sin(angle(np.array([half])))
    unfold = np.zeros((FREQ, 2 * FREQ))
    for j in range(FREQ):
        f = j - half
        unfold[abs(f), j] = 1.0
        if 0 < abs(f) < half:
            unfold[half + abs(f), FREQ + j] = np.sign(f)
    row = np.arange(ROWS) - (ROWS - 1) / 2.0
    fine = np.arange(-half, half + 0.01, 0.25)
    wave = np.exp(2j * np.pi * np.outer(row, fine) / PERIOD)
    basis = np.linalg.svd(np.concatenate([wave.real, wave.imag], 1))[0][:, : RANK - 1]
    basis = np.concatenate([basis, np.zeros((ROWS, FREQ - RANK + 1))], 1)
    freqs = np.arange(FREQ) - half
    coef = np.exp(2j * np.pi * np.outer(freqs, row) / PERIOD) @ basis
    blocks = PERIOD // ROWS
    centre = ROWS * np.arange(blocks) + (ROWS - 1) / 2.0
    phase = np.exp(2j * np.pi * np.outer(freqs, centre) / PERIOD)
    rows = phase[:, :, None] * coef[:, None, :RANK]
    rows[:, :, RANK - 1] = 0.0
    spare = np.zeros_like(rows)
    spare[:, :, RANK - 1] = phase
    rows = rows.reshape(FREQ, blocks * RANK)
    spare = spare.reshape(FREQ, blocks * RANK)
    gather = np.concatenate([rows.real, rows.imag, spare.real, spare.imag], 0)
    return line, last, unfold, basis, np.stack([coef.real, coef.imag]), gather


def tables():
    ccos, csin = np_waves(np.arange(COARSE) * (PERIOD // COARSE))
    grid = np.block([[ccos, csin], [-csin, ccos]]) / FREQ
    offsets = np.arange(-HALO, HALO + 1)
    taps = np.exp(-(offsets.astype(np.float64) ** 2) / (2.0 * (HALO / 2.0) ** 2))
    taps = taps / taps.sum()
    nodes = np.cos(np.pi * (np.arange(REACH) + 0.5) / REACH) * (ROWS / 2 + HALO - 0.5) + (ROWS - 1) / 2.0
    freqs = np.arange(1 - FREQ, FREQ)
    at = lambda places: np.exp(2j * np.pi * np.outer(places, freqs) / PERIOD)
    both = lambda value: np.concatenate([value.real, value.imag], 1)
    row_blur = np.zeros((PERIOD // ROWS, ROWS, REACH))
    near = np.arange(-HALO, ROWS + HALO)
    full = np.zeros((ROWS, ROWS + 2 * HALO))
    for row in range(ROWS):
        full[row, row : row + 2 * HALO + 1] = taps
    for block in range(PERIOD // ROWS):
        inside = (near + block * ROWS >= 0) & (near + block * ROWS < PERIOD)
        wanted = both((full * inside) @ at(near))
        row_blur[block] = np.linalg.lstsq(both(at(nodes)).T, wanted.T, rcond=1e-12)[0].T
    places = ROWS * np.arange(PERIOD // ROWS)[:, None] + nodes[None, :]
    angles = 2.0 * np.pi * (places[:, :, None] * (np.arange(FREQ) - FREQ // 2)) / PERIOD
    cos, sin = np.cos(angles), np.sin(angles)
    reach = np.concatenate([np.concatenate([cos, -sin], 2), np.concatenate([sin, cos], 2)], 1)
    shift = np.arange(PERIOD)[:, None] - (PERIOD // COARSE) * np.arange(COARSE)[None, :]
    freqs = np.arange(1, FREQ)
    line = (1.0 + 2.0 * np.cos(2.0 * np.pi * np.outer(np.arange(PERIOD), freqs) / PERIOD).sum(1)) / COARSE
    interp = line[shift % PERIOD]
    padded = np.zeros((PERIOD + 2 * HALO, COARSE))
    padded[HALO:-HALO] = interp
    own = np.zeros((PERIOD, COARSE))
    for index, tap in enumerate(taps):
        own += tap * padded[index : index + PERIOD]
    cross = np.zeros((2, COARSE, 2 * EDGE))
    for column in range(HALO):
        for index, offset in enumerate(offsets):
            if column + offset < 0:
                cross[1, :, column] += taps[index] * interp[PERIOD + column + offset]
            place = PERIOD - 1 - column + offset
            if place >= PERIOD:
                cross[0, :, 2 * EDGE - 1 - column] += taps[index] * interp[place - PERIOD]
    return reach, grid, row_blur, own, cross


LINE, LAST, UNFOLD, BASIS, COEF, GATHER = line_tables()
REACH_WAVES, GRID, ROW_BLUR, OWN, CROSS = tables()
BLOCKS = PERIOD // ROWS
GROUP_BLOCKS = BLOCKS // KERN
WAVE = REACH_WAVES
WAVE = WAVE.reshape(KERN, GROUP_BLOCKS, 2 * REACH, 2 * FREQ).transpose(1, 0, 2, 3)
WAVE = WAVE.reshape(GROUP_BLOCKS, KERN * 2 * REACH, 2 * FREQ)
LOW = 4
HIGH = RANK - LOW - 1
SPREAD = GATHER.reshape(4 * FREQ, BLOCKS, RANK)
SPARE = SPREAD[:, :, RANK - 1 :]
SPREAD = np.concatenate([SPREAD[:, :, : HIGH - 1], SPARE, SPREAD[:, :, :LOW], SPARE], 2)
SPREAD = SPREAD.reshape(4 * FREQ, BLOCKS * RANK).T
BASIS_BACK = np.zeros((ROWS, RANK))
BASIS_BACK[:, : HIGH - 1] = BASIS[:, : HIGH - 1]
BASIS_BACK[:, HIGH : HIGH + LOW] = BASIS[:, :LOW]
GATHER_OWN = GATHER.reshape(4 * FREQ, KERN, GROUP_BLOCKS * RANK).transpose(1, 0, 2)
BLUR = np.zeros((GROUP_BLOCKS, KERN, ROWS, KERN, REACH))
for group in range(KERN):
    BLUR[:, group, :, group] = ROW_BLUR.reshape(KERN, GROUP_BLOCKS, ROWS, REACH)[group]
BLUR = BLUR.reshape(GROUP_BLOCKS, KERN * ROWS, KERN * REACH)


def split(value):
    high = value.astype(BF)
    return high, (value - high.astype(F32)).astype(BF)


NN = (((1,), (0,)), ((), ()))


def dot3(left, right):
    lh, ll = left
    rh, rl = right

    def one(a, b):
        return lax.dot_general(a, b, NN, preferred_element_type=F32)

    count = lh.shape[0]
    if count > 64:
        return one(jnp.concatenate([lh, ll, lh], 1), jnp.concatenate([rh, rh, rl], 0))
    both = one(jnp.concatenate([lh, ll], 0), rh)
    return both[:count] + (one(lh, rl) + both[count:])


def dot_exact(left, right):
    high, low = left
    return jnp.dot(high, right, preferred_element_type=F32) + jnp.dot(low, right, preferred_element_type=F32)


def call(body, out_shape, args, place=None, **kw):
    params = pltpu.CompilerParams(vmem_limit_bytes=MIB * 1024 * 1024)
    if place is None:
        return pl.pallas_call(body, out_shape=out_shape, compiler_params=params, **kw)(*args)
    grid_spec = pltpu.PrefetchScalarGridSpec(num_scalar_prefetch=1, **kw)
    return pl.pallas_call(body, out_shape=out_shape, compiler_params=params, grid_spec=grid_spec)(place, *args)


def hbm(*values):
    return tuple(pltpu.with_memory_space_constraint(value, pltpu.HBM) for value in values)


def vmem(*values):
    return tuple(pltpu.with_memory_space_constraint(value, pltpu.VMEM) for value in values)


CHUNK = 512
LANES = 256
PARTS = 4


def fetches(sources, targets, sems):
    copies = [
        pltpu.make_async_copy(source, target, sems.at[index])
        for index, (source, target) in enumerate(zip(sources, targets))
    ]
    for copy in copies:
        copy.start()
    return copies


def front_body(mask_ref, basis_ref, lh_ref, ll_ref, last_ref, noise_ref, first, second_ref, *scratch):
    mask, basis, lh, ll, last, second, sems = scratch
    tables = [
        pltpu.make_async_copy(source, target, sems.at[index])
        for index, (source, target) in enumerate(
            zip((mask_ref, basis_ref, lh_ref, ll_ref, last_ref), (mask, basis, lh, ll, last))
        )
    ]
    part = first.shape[0] // PARTS
    loads, stores = [], []
    for index in range(2 * PARTS):
        which, rows = index // PARTS, pl.ds(index % PARTS * part, part)
        there = first.at[rows, :, pl.ds(0, PERIOD)] if which == 0 else second.at[rows]
        loads.append(pltpu.make_async_copy(noise_ref.at[which, rows], there, sems.at[5 + index]))
        if which == 1:
            stores.append(pltpu.make_async_copy(there, second_ref.at[rows], sems.at[5 + PARTS + index]))
    for copy in tables + loads:
        copy.start()
    for copy in tables:
        copy.wait()
    transmit = (2.0 * mask[...] - 1.0) * (1.0 / PERIOD)
    rows = dot3(split(basis[...]), split(transmit))
    line = dot3(split(rows), (lh[...], ll[...]))
    row = lax.broadcasted_iota(jnp.int32, (RANK, FREQ), 0)
    lane = lax.broadcasted_iota(jnp.int32, (RANK, FREQ), 1)
    apart = jnp.sum(rows * last[...], 1, keepdims=True)
    apart = jnp.sum(jnp.where(row == lane, apart, 0.0), 0, keepdims=True)
    packed = jnp.concatenate(split(jnp.where(row == RANK - 1, apart, line)), 0)
    for index in range(first.shape[0]):
        first[index, :, PERIOD:] = packed
    for load, store in zip(loads[PARTS:], stores):
        load.wait()
        store.start()
    for load in loads[:PARTS]:
        load.wait()
    for store in stores:
        store.wait()


def spectrum_body(_, got_ref, gh_ref, gl_ref, unfold_ref, coef_ref, out_ref):
    high = got_ref[:, :RANK].reshape(GROUP_BLOCKS * RANK, FREQ)
    low = got_ref[:, RANK:].reshape(GROUP_BLOCKS * RANK, FREQ)
    both = dot3((gh_ref[0], gl_ref[0]), (high, low))
    waves = dot_exact(split(both[: 2 * FREQ]), unfold_ref[...])
    spare_cos, spare_sin = both[2 * FREQ : 3 * FREQ], both[3 * FREQ :]
    coef_re, coef_im = coef_ref[0], coef_ref[1]
    last_cos = jnp.sum(coef_re * spare_cos - coef_im * spare_sin, 1, keepdims=True)
    last_sin = jnp.sum(coef_re * spare_sin + coef_im * spare_cos, 1, keepdims=True)
    first = lax.broadcasted_iota(jnp.int32, (FREQ, FREQ), 1) == 0
    cos_cos, cos_sin = waves[:FREQ, :FREQ], waves[:FREQ, FREQ:]
    sin_cos, sin_sin = waves[FREQ:, :FREQ], waves[FREQ:, FREQ:]
    out_ref[:FREQ] = cos_cos - sin_sin + jnp.where(first, last_sin, 0.0)
    out_ref[FREQ:] = jnp.where(first, last_cos, 0.0) - cos_sin - sin_cos


def field_body(place_ref, weight_ref, *refs):
    ins, outs, scratch = refs[:10], refs[10 : 11 + KERN], refs[11 + KERN :]
    spec_refs, (kern_ref, wh_ref, wl_ref, gh_ref, gl_ref, blur_ref) = ins[:KERN], ins[KERN:]
    field_ref, piece_refs = outs[0], outs[1:]
    specs, kern, wave, grid, blur, field, total_ref, sems = scratch
    block = place_ref[1]
    copies = fetches(
        list(spec_refs) + [kern_ref, wh_ref.at[block], wl_ref.at[block], gh_ref, gl_ref, blur_ref.at[block]],
        [specs.at[index] for index in range(KERN)]
        + [kern, wave.at[0], wave.at[1], grid.at[0], grid.at[1], blur],
        sems,
    )
    for copy in copies[:7]:
        copy.wait()
    spec = (specs[0] + specs[1]) + (specs[2] + specs[3])
    spec_re = spec[:FREQ]
    spec_im = spec[FREQ:]
    half = KERN * REACH
    total, stores = None, []
    for pair in range(PAIRS):
        near_re, near_im = [], []
        for index in (2 * pair, 2 * pair + 1):
            kern_re, kern_im = kern[index, 0], kern[index, 1]
            near_re.append(kern_re * spec_re - kern_im * spec_im)
            near_im.append(kern_re * spec_im + kern_im * spec_re)
        near = jnp.concatenate([jnp.concatenate(near_re, 1), jnp.concatenate(near_im, 1)], 0)
        left = dot3((wave[0], wave[1]), split(near))
        lefts = []
        for index in range(2):
            lanes = slice(index * FREQ, (index + 1) * FREQ)
            for group in range(KERN):
                first = 2 * group * REACH
                re, im = left[first : first + REACH, lanes], left[first + REACH : first + 2 * REACH, lanes]
                lefts.append(jnp.concatenate([re, im], 1))
        if pair == 0:
            for copy in copies[7:9]:
                copy.wait()
        held = field.at[pl.ds(pair * 2 * half, 2 * half)]
        held[...] = dot3(split(jnp.concatenate(lefts, 0)), (grid[0], grid[1]))
        stores.append(pltpu.make_async_copy(held, field_ref.at[pl.ds(pair * 2 * half, 2 * half)], sems.at[10 + pair]))
        stores[-1].start()
        for index in range(2):
            own = held[index * half : (index + 1) * half]
            own = own * own
            own = weight_ref[2 * pair + index] * (own[:, :COARSE] + own[:, COARSE:])
            total = own if total is None else total + own
    copies[9].wait()
    total_ref[...] = dot3(split(blur[...]), split(total))
    for shift, piece_ref in enumerate(piece_refs):
        group = jnp.bitwise_xor(place_ref[0], shift)
        piece_ref[...] = total_ref[pl.ds(pl.multiple_of(group * ROWS, ROWS), ROWS)]
    for store in stores:
        store.wait()


def sample_sums(noise_ref, place, acid, sums):
    sum_u, sum_q, sum_qu = sums
    quarter = 0.25 * acid
    base = acid - 2.0
    for index in range(noise_ref.shape[0]):
        noise = noise_ref[(index,) + place].astype(F32)
        u = jnp.tanh(quarter * noise + base)
        q = (1.0 - u * u) * (1.0 + 0.25 * noise)
        sum_u, sum_q, sum_qu = sum_u + u, sum_q + q, sum_qu + q * u
    return sum_u, sum_q, sum_qu


def places(columns):
    width = min(columns, LANES)
    for row in range(0, ROWS, 16):
        for col in range(0, columns, width):
            yield slice(row, row + 16), slice(col, col + width)


def dose_first_body(rows_ref, oh_ref, ol_ref, noise_ref, sums_ref):
    sums_ref[0] = dot3(split(rows_ref[...]), (oh_ref[...], ol_ref[...]))
    for place in places(PERIOD):
        acid = sums_ref[(0,) + place]
        zero = jnp.zeros(acid.shape, F32)
        for index, value in enumerate(sample_sums(noise_ref, place, acid, (zero, zero, zero))):
            sums_ref[(index + 1,) + place] = value


def acid_grad(sums, target):
    sum_u, sum_q, sum_qu = sums
    inner = 0.25 - sum_u * (1.0 / SAMPLES) - 0.5 * target.astype(F32)
    return (1.0 / 16.0) * (sum_q * inner + 1.25 * sum_qu)


def dose_edge_body(place_ref, sums_ref, other_ref, *refs):
    ins, (grad_ref, send_ref), (held, target, cross, cross_t, sems) = refs[:7], refs[7:9], refs[9:]
    target_ref, first_ref, second_ref, ch_ref, cl_ref, th_ref, tl_ref = ins
    tile = place_ref[2]
    sides = [pl.ds(0, EDGE), pl.ds(PERIOD - EDGE, EDGE)]
    copies = fetches(
        [ch_ref.at[tile], cl_ref.at[tile]]
        + [ref.at[:, :, side] for side in sides for ref in (first_ref, second_ref)]
        + [target_ref.at[:, side] for side in sides]
        + [th_ref.at[tile], tl_ref.at[tile]],
        [cross.at[0], cross.at[1]]
        + [held.at[index] for index in range(4)]
        + [target.at[index] for index in range(2)]
        + [cross_t.at[0], cross_t.at[1]],
        sems,
    )
    for copy in copies[:2]:
        copy.wait()
    halo = dot3(split(other_ref[...]), (cross[0], cross[1]))
    for copy in copies[2:8]:
        copy.wait()
    grads = []
    for side in range(2):
        columns = []
        for row, lanes in places(EDGE):
            place = (row, lanes)
            there = slice(side * (PERIOD - EDGE), side * (PERIOD - EDGE) + EDGE)
            acid = sums_ref[0, row, there] + halo[row, side * EDGE : (side + 1) * EDGE]
            zero = jnp.zeros(acid.shape, F32)
            sums = sample_sums(held.at[2 * side], place, acid, (zero, zero, zero))
            sums = sample_sums(held.at[2 * side + 1], place, acid, sums)
            columns.append(acid_grad(sums, target[(side,) + place]))
        grads.append(jnp.concatenate(columns, 0))
    grad = jnp.concatenate(grads, 1)
    grad_ref[...] = grad
    for copy in copies[8:]:
        copy.wait()
    send_ref[...] = dot3(split(grad), (cross_t[0], cross_t[1]))


def dose_body(place_ref, sums_ref, edge_ref, target_ref, noise_ref, oh_ref, ol_ref, *refs):
    ins, out_ref, outs, (target, noise, own, sems) = refs[:11], refs[11], refs[12:20], refs[20:]
    field_ref, kern_ref, wh_ref, wl_ref, gh_ref, gl_ref, blur_ref, th_ref, tl_ref, fold_ref, coef_ref = ins
    field, kern, wave, grid, blur, table, fold, coef = outs
    block = place_ref[1]
    chunks = [pl.ds(first, CHUNK) for first in range(0, PERIOD, CHUNK)]
    copies = fetches(
        [target_ref]
        + [ref for part in chunks for ref in (noise_ref.at[:, :, part], oh_ref.at[part], ol_ref.at[part])]
        + [field_ref, kern_ref, wh_ref.at[block], wl_ref.at[block], gh_ref, gl_ref]
        + [blur_ref.at[block], th_ref, tl_ref, fold_ref, coef_ref],
        [target]
        + [
            ref
            for index, part in enumerate(chunks)
            for ref in (noise.at[index], own.at[0, part], own.at[1, part])
        ]
        + [field, kern, wave.at[0], wave.at[1], grid.at[0], grid.at[1]]
        + [blur, table.at[0], table.at[1], fold, coef],
        sems,
    )
    copies[0].wait()
    total = None
    for index in range(len(chunks)):
        for copy in copies[1 + 3 * index : 4 + 3 * index]:
            copy.wait()
        for col in range(0, CHUNK, LANES):
            first = index * CHUNK + col
            grads = []
            for row in range(0, ROWS, 16):
                place = (slice(row, row + 16), slice(first, first + LANES))
                acid, *sums = [sums_ref[(which,) + place] for which in range(4)]
                here = (slice(row, row + 16), slice(col, col + LANES))
                grads.append(acid_grad(sample_sums(noise.at[index], here, acid, sums), target[place]))
            grad = jnp.concatenate(grads, 0)
            if first == 0:
                grad = jnp.concatenate([edge_ref[:, :EDGE], grad[:, EDGE:]], 1)
            if first == PERIOD - LANES:
                grad = jnp.concatenate([grad[:, : LANES - EDGE], edge_ref[:, EDGE:]], 1)
            lines = slice(first, first + LANES)
            part = dot3(split(grad), (own[0, lines], own[1, lines]))
            total = part if total is None else total + part
    out_ref[...] = total
    for copy in copies[1 + 3 * len(chunks) :]:
        copy.wait()


def back_body(place_ref, weight_ref, *refs):
    piece_refs, (field, kern, wave, grid, blur, table, fold, coef) = refs[:KERN], refs[KERN : KERN + 8]
    out_ref, rows = refs[KERN + 8 :]
    for shift, piece_ref in enumerate(piece_refs):
        first = jnp.bitwise_xor(place_ref[0], shift) * ROWS
        rows[pl.ds(pl.multiple_of(first, ROWS), ROWS)] = piece_ref[...]
    part = 2.0 * dot3(split(blur[...]), split(rows[...]))
    grad = jnp.concatenate([part, part], 1)
    half = KERN * REACH
    sum_re = sum_im = None
    for pair in range(PAIRS):
        pulled = [
            field[index * half : (index + 1) * half] * (weight_ref[index] * grad)
            for index in (2 * pair, 2 * pair + 1)
        ]
        lefts = dot3(split(jnp.concatenate(pulled, 0)), (grid[0], grid[1]))
        stack = []
        for index in range(2):
            column = []
            for which in range(KERN):
                first = index * half + which * REACH
                left = lefts[first : first + REACH]
                column += [left[:, :FREQ], left[:, FREQ:]]
            stack.append(jnp.concatenate(column, 0))
        near = dot3((wave[0], wave[1]), split(jnp.concatenate(stack, 1)))
        for index in range(2):
            near_re = near[:FREQ, index * FREQ : (index + 1) * FREQ]
            near_im = near[FREQ:, index * FREQ : (index + 1) * FREQ]
            kern_re, kern_im = kern[2 * pair + index, 0], kern[2 * pair + index, 1]
            own_re = kern_re * near_re + kern_im * near_im
            own_im = kern_re * near_im - kern_im * near_re
            sum_re = own_re if sum_re is None else sum_re + own_re
            sum_im = own_im if sum_im is None else sum_im + own_im
    grad_re, grad_im = sum_re * (2.0 / PERIOD), sum_im * (2.0 / PERIOD)
    mix = jnp.concatenate(
        [jnp.concatenate([grad_re, -grad_im], 1), jnp.concatenate([-grad_im, -grad_re], 1)], 0
    )
    folded = dot_exact(split(mix), fold[...])
    coef_re, coef_im = coef[0], coef[1]
    by_cos, by_sin = grad_im[:, :1], grad_re[:, :1]
    spare_cos = coef_re * by_cos + coef_im * by_sin
    spare_sin = coef_re * by_sin - coef_im * by_cos
    mixed = jnp.concatenate([folded, spare_cos, spare_sin], 0)
    high, low = split(dot3((table[0], table[1]), split(mixed)).reshape(out_ref.shape))
    row = lax.broadcasted_iota(jnp.int32, out_ref.shape, 1)
    out_ref[...] = jnp.where(row < HIGH, high.astype(F32), low.astype(F32)).astype(BF)


def final_body(got_ref, back_ref, basis_ref, wh_ref, wl_ref, last_ref, out_ref):
    total = got_ref[0].astype(F32)
    for index in range(1, got_ref.shape[0]):
        total = total + got_ref[index].astype(F32)
    rows = dot3(split(back_ref[...]), split(total))
    spare = jnp.sum(basis_ref[...] * (total[HIGH - 1 : HIGH] + total[RANK - 1 :]), 1, keepdims=True)
    out_ref[...] = dot3(split(rows), (wh_ref[...], wl_ref[...])) + spare * last_ref[...]


def to_const(table):
    return hbm(*near_const(table))


def near_const(table):
    return tuple(jnp.asarray(part) for part in np_split(table))


def shifted(values, shifts):
    count = lax.axis_size("kern")
    return [
        lax.ppermute(value, "kern", [(source, source ^ shift) for source in range(count)])
        for value, shift in zip(values, shifts)
    ]


def body(mask_values, kernels, weights, target, dose_noise):
    noise_count = lax.axis_size("noise")
    f32 = lambda *shape: jax.ShapeDtypeStruct(shape, F32)
    bf16 = lambda *shape: jax.ShapeDtypeStruct(shape, BF)
    smem = pl.BlockSpec(memory_space=pltpu.SMEM)
    columns = PERIOD // CHUNK
    shifts = range(1, KERN)

    def fixed(*shape):
        return pl.BlockSpec(shape, lambda i, *_: (0,) * len(shape))

    def chunk(rows):
        return pl.BlockSpec((rows, CHUNK), lambda i, *_: (0, i))

    def moved_spec(width):
        return pl.BlockSpec((noise_count // columns, ROWS, width), lambda i: (i, 0, 0))

    lines = to_const(LINE.T)
    basis = jnp.asarray(BASIS.T[:RANK], F32)
    last = jnp.asarray(LAST, F32)
    far_noise = dose_noise.reshape(2, noise_count, ROWS, PERIOD)
    anywhere = pl.BlockSpec(memory_space=pltpu.HBM)
    held = (mask_values, basis, *lines, last)
    moved_first, moved = call(
        front_body,
        (pltpu.VMEM((noise_count, ROWS, PERIOD + FREQ), BF), pltpu.HBM((noise_count, ROWS, PERIOD), BF)),
        hbm(*held, far_noise),
        in_specs=[anywhere] * 6,
        out_specs=(pl.BlockSpec(memory_space=pltpu.VMEM), anywhere),
        scratch_shapes=[pltpu.VMEM(value.shape, value.dtype) for value in held]
        + [
            pltpu.VMEM((noise_count, ROWS, PERIOD), BF),
            pltpu.SemaphoreType.DMA((5 + 3 * PARTS,)),
        ],
    )
    place = jnp.stack([lax.axis_index(axis).astype(jnp.int32) for axis in ("kern", "noise", "tile")])
    moved_first, place = lax.optimization_barrier((moved_first, place))
    got = lax.all_to_all(moved_first, "noise", 0, 0, tiled=True)
    got, moved, kernels, weights, target, place = lax.optimization_barrier(
        (got, moved, kernels, weights, target, place)
    )
    got_last = lax.all_to_all(moved, "noise", 0, 0, tiled=True)

    def at_place(which, table):
        return [pl.BlockSpec((1,) + table.shape[1:], lambda i, place: (place[which], 0, 0))] * 2

    waves_t = WAVE.transpose(0, 2, 1)
    cross_t = CROSS.transpose(0, 2, 1)
    coef = hbm(jnp.asarray(COEF, F32))
    spec = call(
        spectrum_body,
        f32(2 * FREQ, FREQ),
        (got, *near_const(GATHER_OWN), jnp.asarray(UNFOLD, BF), jnp.asarray(COEF, F32)),
        place=place,
        grid=(1,),
        in_specs=[pl.BlockSpec((noise_count, ROWS, FREQ), lambda i, _: (0, 0, PERIOD // FREQ))]
        + at_place(0, GATHER_OWN)
        + [fixed(*UNFOLD.shape), fixed(*COEF.shape)],
        out_specs=fixed(2 * FREQ, FREQ),
    )
    specs = [spec] + shifted([spec] * len(shifts), shifts)
    field_rows = 2 * KERN * REACH
    field_shape = (PAIRS * field_rows, 2 * COARSE)
    blur = jnp.asarray(BLUR, F32)
    ins = (*specs, kernels, *to_const(WAVE), *to_const(GRID), blur)
    field, *pieces = call(
        field_body,
        (pltpu.HBM(field_shape, F32),) + (f32(ROWS, COARSE),) * KERN,
        (place, weights, *hbm(*ins)),
        in_specs=[smem] * 2 + [anywhere] * len(ins),
        out_specs=(anywhere,) + (pl.BlockSpec((ROWS, COARSE), lambda: (0, 0)),) * KERN,
        scratch_shapes=[
            pltpu.VMEM((KERN,) + spec.shape, F32),
            pltpu.VMEM(kernels.shape, F32),
            pltpu.VMEM((2,) + WAVE.shape[1:], BF),
            pltpu.VMEM((2,) + GRID.shape, BF),
            pltpu.VMEM(BLUR.shape[1:], F32),
            pltpu.VMEM(field_shape, F32),
            pltpu.VMEM((KERN * ROWS, COARSE), F32),
            pltpu.SemaphoreType.DMA((10 + PAIRS,)),
        ],
    )
    pieces = pieces[:1] + shifted(pieces[1:], shifts)
    rows = (pieces[0] + pieces[1]) + (pieces[2] + pieces[3])
    swap = [(0, 1), (1, 0)]
    rows_other = lax.ppermute(rows, "tile", swap)
    sums = call(
        dose_first_body,
        f32(4, ROWS, PERIOD),
        (rows, *near_const(OWN.T), got),
        grid=(1,),
        in_specs=[fixed(ROWS, COARSE)] + [fixed(COARSE, PERIOD)] * 2 + [fixed(noise_count, ROWS, PERIOD)],
        out_specs=pl.BlockSpec((4, ROWS, PERIOD), lambda i: (0, 0, 0)),
    )
    (target,) = hbm(target)
    (sums,) = vmem(sums)
    inside = pl.BlockSpec(memory_space=pltpu.VMEM)
    piece_spec = pl.BlockSpec((ROWS, COARSE), lambda: (0, 0))
    edges, send = call(
        dose_edge_body,
        (f32(ROWS, 2 * EDGE), f32(ROWS, COARSE)),
        (place, sums, rows_other, target, got, got_last, *to_const(CROSS), *to_const(cross_t)),
        in_specs=[smem, inside, piece_spec, anywhere]
        + [pl.BlockSpec(memory_space=pl.ANY)] * 2
        + [anywhere] * 4,
        out_specs=(piece_spec, piece_spec),
        scratch_shapes=[
            pltpu.VMEM((4, noise_count, ROWS, EDGE), BF),
            pltpu.VMEM((2, ROWS, EDGE), BF),
            pltpu.VMEM((2,) + CROSS.shape[1:], BF),
            pltpu.VMEM((2,) + cross_t.shape[1:], BF),
            pltpu.SemaphoreType.DMA((10,)),
        ],
    )
    grad_other = lax.ppermute(send, "tile", swap)
    blur_t, fold = jnp.asarray(BLUR.transpose(0, 2, 1), F32), jnp.asarray(UNFOLD.T, BF)
    ins = (field, kernels, *to_const(waves_t), *to_const(GRID.T), blur_t, *to_const(SPREAD), fold, *coef)
    held = [
        (field_shape, F32),
        (kernels.shape, F32),
        ((2,) + waves_t.shape[1:], BF),
        ((2,) + GRID.T.shape, BF),
        (BLUR.shape[:0:-1], F32),
        ((2,) + SPREAD.shape, BF),
        (fold.shape, BF),
        (COEF.shape, F32),
    ]
    grad_own, *staged = call(
        dose_body,
        (f32(ROWS, COARSE),) + tuple(pltpu.VMEM(shape, dtype) for shape, dtype in held),
        (place, sums, edges, target, got_last, *to_const(OWN), *hbm(*ins)),
        in_specs=[smem, inside, piece_spec, anywhere, pl.BlockSpec(memory_space=pl.ANY)]
        + [anywhere] * (2 + len(ins)),
        out_specs=(piece_spec,) + (inside,) * len(held),
        scratch_shapes=[
            pltpu.VMEM((ROWS, PERIOD), BF),
            pltpu.VMEM((columns, noise_count, ROWS, CHUNK), BF),
            pltpu.VMEM((2,) + OWN.shape, BF),
            pltpu.SemaphoreType.DMA((1 + 3 * columns + len(ins),)),
        ],
    )
    grad = grad_own + grad_other
    grads = [grad] + shifted([grad] * len(shifts), shifts)
    spread = call(
        back_body,
        bf16(BLOCKS, RANK, FREQ),
        (place, weights, *grads, *vmem(*staged)),
        in_specs=[smem] * 2 + [piece_spec] * KERN + [inside] * len(held),
        out_specs=pl.BlockSpec((BLOCKS, RANK, FREQ), lambda: (0, 0, 0)),
        scratch_shapes=[pltpu.VMEM((KERN * ROWS, COARSE), F32)],
    )
    back = lax.all_to_all(spread, ("kern", "noise"), 0, 0, tiled=True)
    return call(
        final_body,
        f32(ROWS, PERIOD),
        (back, jnp.asarray(BASIS_BACK, F32), jnp.asarray(BASIS, F32), *(jnp.asarray(t) for t in np_split(LINE)), jnp.asarray(LAST, F32)),
    )


def solution(mesh):
    return jax.shard_map(
        body,
        mesh=mesh,
        in_specs=(
            P(("kern", "noise"), "tile"),
            P("kern", None, None, None),
            P("kern"),
            P(("kern", "noise"), "tile"),
            P("noise", "kern", "tile"),
        ),
        out_specs=P(("kern", "noise"), "tile"),
        check_vma=False,
    )
```

```python
import math

import jax
import jax.numpy as jnp
import numpy as np
from jax import lax
from jax.experimental import pallas as pl
from jax.experimental.pallas import tpu as pltpu
from jax.sharding import PartitionSpec as P

HALO = 16
FREQ = 128
COARSE = 256
PERIOD = 2048
ROWS = 32
REACH = 24
EDGE = 128
GROUP = 6
PAIRS = GROUP // 2
KERN = 4
SAMPLES = 32
RANK = 16
MIB = 32
BF = jnp.bfloat16
F32 = jnp.float32


def np_split(table):
    table = np.asarray(table, np.float32)
    high = table.astype(jnp.bfloat16)
    low = (table - high.astype(np.float32)).astype(jnp.bfloat16)
    return high, low


def np_waves(ids):
    centred = np.arange(FREQ) - FREQ // 2
    angles = 2.0 * np.pi * ((centred[:, None] * ids[None, :]) % PERIOD) / PERIOD
    return np.cos(angles), np.sin(angles)


def line_tables():
    half = FREQ // 2
    pixels = np.arange(PERIOD)
    angle = lambda f: 2.0 * np.pi * ((f[:, None] * pixels[None, :]) % PERIOD) / PERIOD
    line = np.concatenate([np.cos(angle(np.arange(half + 1))), np.sin(angle(np.arange(1, half)))], 0)
    last = np.sin(angle(np.array([half])))
    unfold = np.zeros((FREQ, 2 * FREQ))
    for j in range(FREQ):
        f = j - half
        unfold[abs(f), j] = 1.0
        if 0 < abs(f) < half:
            unfold[half + abs(f), FREQ + j] = np.sign(f)
    row = np.arange(ROWS) - (ROWS - 1) / 2.0
    fine = np.arange(-half, half + 0.01, 0.25)
    wave = np.exp(2j * np.pi * np.outer(row, fine) / PERIOD)
    basis = np.linalg.svd(np.concatenate([wave.real, wave.imag], 1))[0][:, : RANK - 1]
    basis = np.concatenate([basis, np.zeros((ROWS, FREQ - RANK + 1))], 1)
    freqs = np.arange(FREQ) - half
    coef = np.exp(2j * np.pi * np.outer(freqs, row) / PERIOD) @ basis
    blocks = PERIOD // ROWS
    centre = ROWS * np.arange(blocks) + (ROWS - 1) / 2.0
    phase = np.exp(2j * np.pi * np.outer(freqs, centre) / PERIOD)
    rows = phase[:, :, None] * coef[:, None, :RANK]
    rows[:, :, RANK - 1] = 0.0
    spare = np.zeros_like(rows)
    spare[:, :, RANK - 1] = phase
    rows = rows.reshape(FREQ, blocks * RANK)
    spare = spare.reshape(FREQ, blocks * RANK)
    gather = np.concatenate([rows.real, rows.imag, spare.real, spare.imag], 0)
    return line, last, unfold, basis, np.stack([coef.real, coef.imag]), gather


def tables():
    ccos, csin = np_waves(np.arange(COARSE) * (PERIOD // COARSE))
    grid = np.block([[ccos, csin], [-csin, ccos]]) / FREQ
    offsets = np.arange(-HALO, HALO + 1)
    taps = np.exp(-(offsets.astype(np.float64) ** 2) / (2.0 * (HALO / 2.0) ** 2))
    taps = taps / taps.sum()
    nodes = np.cos(np.pi * (np.arange(REACH) + 0.5) / REACH) * (ROWS / 2 + HALO - 0.5) + (ROWS - 1) / 2.0
    freqs = np.arange(1 - FREQ, FREQ)
    at = lambda places: np.exp(2j * np.pi * np.outer(places, freqs) / PERIOD)
    both = lambda value: np.concatenate([value.real, value.imag], 1)
    row_blur = np.zeros((PERIOD // ROWS, ROWS, REACH))
    near = np.arange(-HALO, ROWS + HALO)
    full = np.zeros((ROWS, ROWS + 2 * HALO))
    for row in range(ROWS):
        full[row, row : row + 2 * HALO + 1] = taps
    for block in range(PERIOD // ROWS):
        inside = (near + block * ROWS >= 0) & (near + block * ROWS < PERIOD)
        wanted = both((full * inside) @ at(near))
        row_blur[block] = np.linalg.lstsq(both(at(nodes)).T, wanted.T, rcond=1e-12)[0].T
    places = ROWS * np.arange(PERIOD // ROWS)[:, None] + nodes[None, :]
    angles = 2.0 * np.pi * (places[:, :, None] * (np.arange(FREQ) - FREQ // 2)) / PERIOD
    cos, sin = np.cos(angles), np.sin(angles)
    reach = np.concatenate([np.concatenate([cos, -sin], 2), np.concatenate([sin, cos], 2)], 1)
    shift = np.arange(PERIOD)[:, None] - (PERIOD // COARSE) * np.arange(COARSE)[None, :]
    freqs = np.arange(1, FREQ)
    line = (1.0 + 2.0 * np.cos(2.0 * np.pi * np.outer(np.arange(PERIOD), freqs) / PERIOD).sum(1)) / COARSE
    interp = line[shift % PERIOD]
    padded = np.zeros((PERIOD + 2 * HALO, COARSE))
    padded[HALO:-HALO] = interp
    own = np.zeros((PERIOD, COARSE))
    for index, tap in enumerate(taps):
        own += tap * padded[index : index + PERIOD]
    cross = np.zeros((2, COARSE, 2 * EDGE))
    for column in range(HALO):
        for index, offset in enumerate(offsets):
            if column + offset < 0:
                cross[1, :, column] += taps[index] * interp[PERIOD + column + offset]
            place = PERIOD - 1 - column + offset
            if place >= PERIOD:
                cross[0, :, 2 * EDGE - 1 - column] += taps[index] * interp[place - PERIOD]
    return reach, grid, row_blur, own, cross


LINE, LAST, UNFOLD, BASIS, COEF, GATHER = line_tables()
REACH_WAVES, GRID, ROW_BLUR, OWN, CROSS = tables()
BLOCKS = PERIOD // ROWS
GROUP_BLOCKS = BLOCKS // KERN
WAVE = REACH_WAVES
WAVE = WAVE.reshape(KERN, GROUP_BLOCKS, 2 * REACH, 2 * FREQ).transpose(1, 0, 2, 3)
WAVE = WAVE.reshape(GROUP_BLOCKS, KERN * 2 * REACH, 2 * FREQ)
LOW = 4
HIGH = RANK - LOW - 1
SPREAD = GATHER.reshape(4 * FREQ, BLOCKS, RANK)
SPARE = SPREAD[:, :, RANK - 1 :]
SPREAD = np.concatenate([SPREAD[:, :, : HIGH - 1], SPARE, SPREAD[:, :, :LOW], SPARE], 2)
SPREAD = SPREAD.reshape(4 * FREQ, BLOCKS * RANK).T
BASIS_BACK = np.zeros((ROWS, RANK))
BASIS_BACK[:, : HIGH - 1] = BASIS[:, : HIGH - 1]
BASIS_BACK[:, HIGH : HIGH + LOW] = BASIS[:, :LOW]
GATHER_OWN = GATHER.reshape(4 * FREQ, KERN, GROUP_BLOCKS * RANK).transpose(1, 0, 2)
BLUR = np.zeros((GROUP_BLOCKS, KERN, ROWS, KERN, REACH))
for group in range(KERN):
    BLUR[:, group, :, group] = ROW_BLUR.reshape(KERN, GROUP_BLOCKS, ROWS, REACH)[group]
BLUR = BLUR.reshape(GROUP_BLOCKS, KERN * ROWS, KERN * REACH)


def split(value):
    high = value.astype(BF)
    return high, (value - high.astype(F32)).astype(BF)


NN = (((1,), (0,)), ((), ()))


def dot3(left, right):
    lh, ll = left
    rh, rl = right

    def one(a, b):
        return lax.dot_general(a, b, NN, preferred_element_type=F32)

    count = lh.shape[0]
    if count > 64:
        return one(jnp.concatenate([lh, ll, lh], 1), jnp.concatenate([rh, rh, rl], 0))
    both = one(jnp.concatenate([lh, ll], 0), rh)
    return both[:count] + (one(lh, rl) + both[count:])


def dot_exact(left, right):
    high, low = left
    return jnp.dot(high, right, preferred_element_type=F32) + jnp.dot(low, right, preferred_element_type=F32)


def call(body, out_shape, args, place=None, **kw):
    params = pltpu.CompilerParams(vmem_limit_bytes=MIB * 1024 * 1024)
    if place is None:
        return pl.pallas_call(body, out_shape=out_shape, compiler_params=params, **kw)(*args)
    grid_spec = pltpu.PrefetchScalarGridSpec(num_scalar_prefetch=1, **kw)
    return pl.pallas_call(body, out_shape=out_shape, compiler_params=params, grid_spec=grid_spec)(place, *args)


def hbm(*values):
    return tuple(pltpu.with_memory_space_constraint(value, pltpu.HBM) for value in values)


def vmem(*values):
    return tuple(pltpu.with_memory_space_constraint(value, pltpu.VMEM) for value in values)


CHUNK = 512
LANES = 256
PARTS = 4


def fetches(sources, targets, sems):
    copies = [
        pltpu.make_async_copy(source, target, sems.at[index])
        for index, (source, target) in enumerate(zip(sources, targets))
    ]
    for copy in copies:
        copy.start()
    return copies


def front_body(mask_ref, basis_ref, lh_ref, ll_ref, last_ref, noise_ref, first, second_ref, *scratch):
    mask, basis, lh, ll, last, second, sems = scratch
    tables = [
        pltpu.make_async_copy(source, target, sems.at[index])
        for index, (source, target) in enumerate(
            zip((mask_ref, basis_ref, lh_ref, ll_ref, last_ref), (mask, basis, lh, ll, last))
        )
    ]
    part = first.shape[0] // PARTS
    loads, stores = [], []
    for index in range(2 * PARTS):
        which, rows = index // PARTS, pl.ds(index % PARTS * part, part)
        there = first.at[rows, :, pl.ds(0, PERIOD)] if which == 0 else second.at[rows]
        loads.append(pltpu.make_async_copy(noise_ref.at[which, rows], there, sems.at[5 + index]))
        if which == 1:
            stores.append(pltpu.make_async_copy(there, second_ref.at[rows], sems.at[5 + PARTS + index]))
    for copy in tables + loads[PARTS:] + loads[:PARTS]:
        copy.start()
    for copy in tables:
        copy.wait()
    transmit = (2.0 * mask[...] - 1.0) * (1.0 / PERIOD)
    rows = dot3(split(basis[...]), split(transmit))
    line = dot3(split(rows), (lh[...], ll[...]))
    row = lax.broadcasted_iota(jnp.int32, (RANK, FREQ), 0)
    lane = lax.broadcasted_iota(jnp.int32, (RANK, FREQ), 1)
    apart = jnp.sum(rows * last[...], 1, keepdims=True)
    apart = jnp.sum(jnp.where(row == lane, apart, 0.0), 0, keepdims=True)
    packed = jnp.concatenate(split(jnp.where(row == RANK - 1, apart, line)), 0)
    for index in range(first.shape[0]):
        first[index, :, PERIOD:] = packed
    for load, store in zip(loads[PARTS:], stores):
        load.wait()
        store.start()
    for load in loads[:PARTS]:
        load.wait()
    for store in stores:
        store.wait()


def spectrum_body(_, got_ref, gh_ref, gl_ref, unfold_ref, coef_ref, out_ref):
    high = got_ref[:, :RANK].reshape(GROUP_BLOCKS * RANK, FREQ)
    low = got_ref[:, RANK:].reshape(GROUP_BLOCKS * RANK, FREQ)
    both = dot3((gh_ref[0], gl_ref[0]), (high, low))
    waves = dot_exact(split(both[: 2 * FREQ]), unfold_ref[...])
    spare_cos, spare_sin = both[2 * FREQ : 3 * FREQ], both[3 * FREQ :]
    coef_re, coef_im = coef_ref[0], coef_ref[1]
    last_cos = jnp.sum(coef_re * spare_cos - coef_im * spare_sin, 1, keepdims=True)
    last_sin = jnp.sum(coef_re * spare_sin + coef_im * spare_cos, 1, keepdims=True)
    first = lax.broadcasted_iota(jnp.int32, (FREQ, FREQ), 1) == 0
    cos_cos, cos_sin = waves[:FREQ, :FREQ], waves[:FREQ, FREQ:]
    sin_cos, sin_sin = waves[FREQ:, :FREQ], waves[FREQ:, FREQ:]
    out_ref[:FREQ] = cos_cos - sin_sin + jnp.where(first, last_sin, 0.0)
    out_ref[FREQ:] = jnp.where(first, last_cos, 0.0) - cos_sin - sin_cos


def field_body(place_ref, weight_ref, *refs):
    ins, outs, scratch = refs[:10], refs[10 : 11 + KERN], refs[11 + KERN :]
    spec_refs, (kern_ref, wh_ref, wl_ref, gh_ref, gl_ref, blur_ref) = ins[:KERN], ins[KERN:]
    field_ref, piece_refs = outs[0], outs[1:]
    specs, kern, wave, grid, blur, field, total_ref, sems = scratch
    block = place_ref[1]
    copies = fetches(
        list(spec_refs) + [kern_ref, wh_ref.at[block], wl_ref.at[block], gh_ref, gl_ref, blur_ref.at[block]],
        [specs.at[index] for index in range(KERN)]
        + [kern, wave.at[0], wave.at[1], grid.at[0], grid.at[1], blur],
        sems,
    )
    for copy in copies[:7]:
        copy.wait()
    spec = (specs[0] + specs[1]) + (specs[2] + specs[3])
    spec_re = spec[:FREQ]
    spec_im = spec[FREQ:]
    half = KERN * REACH
    total, stores = None, []
    for pair in range(PAIRS):
        near_re, near_im = [], []
        for index in (2 * pair, 2 * pair + 1):
            kern_re, kern_im = kern[index, 0], kern[index, 1]
            near_re.append(kern_re * spec_re - kern_im * spec_im)
            near_im.append(kern_re * spec_im + kern_im * spec_re)
        near = jnp.concatenate([jnp.concatenate(near_re, 1), jnp.concatenate(near_im, 1)], 0)
        left = dot3((wave[0], wave[1]), split(near))
        lefts = []
        for index in range(2):
            lanes = slice(index * FREQ, (index + 1) * FREQ)
            for group in range(KERN):
                first = 2 * group * REACH
                re, im = left[first : first + REACH, lanes], left[first + REACH : first + 2 * REACH, lanes]
                lefts.append(jnp.concatenate([re, im], 1))
        if pair == 0:
            for copy in copies[7:9]:
                copy.wait()
        held = field.at[pl.ds(pair * 2 * half, 2 * half)]
        held[...] = dot3(split(jnp.concatenate(lefts, 0)), (grid[0], grid[1]))
        stores.append(pltpu.make_async_copy(held, field_ref.at[pl.ds(pair * 2 * half, 2 * half)], sems.at[10 + pair]))
        stores[-1].start()
        for index in range(2):
            own = held[index * half : (index + 1) * half]
            own = own * own
            own = weight_ref[2 * pair + index] * (own[:, :COARSE] + own[:, COARSE:])
            total = own if total is None else total + own
    copies[9].wait()
    total_ref[...] = dot3(split(blur[...]), split(total))
    for shift, piece_ref in enumerate(piece_refs):
        group = jnp.bitwise_xor(place_ref[0], shift)
        piece_ref[...] = total_ref[pl.ds(pl.multiple_of(group * ROWS, ROWS), ROWS)]
    for store in stores:
        store.wait()


def sample_sums(noise_ref, place, acid, sums):
    sum_u, sum_q, sum_qu = sums
    quarter = 0.25 * acid
    base = acid - 2.0
    for index in range(noise_ref.shape[0]):
        noise = noise_ref[(index,) + place].astype(F32)
        u = jnp.tanh(quarter * noise + base)
        q = (1.0 - u * u) * (1.0 + 0.25 * noise)
        sum_u, sum_q, sum_qu = sum_u + u, sum_q + q, sum_qu + q * u
    return sum_u, sum_q, sum_qu


def places(columns):
    width = min(columns, LANES)
    for row in range(0, ROWS, 16):
        for col in range(0, columns, width):
            yield slice(row, row + 16), slice(col, col + width)


def dose_first_body(rows_ref, oh_ref, ol_ref, noise_ref, sums_ref):
    sums_ref[0] = dot3(split(rows_ref[...]), (oh_ref[...], ol_ref[...]))
    for place in places(PERIOD):
        acid = sums_ref[(0,) + place]
        zero = jnp.zeros(acid.shape, F32)
        for index, value in enumerate(sample_sums(noise_ref, place, acid, (zero, zero, zero))):
            sums_ref[(index + 1,) + place] = value


def acid_grad(sums, target):
    sum_u, sum_q, sum_qu = sums
    inner = 0.25 - sum_u * (1.0 / SAMPLES) - 0.5 * target.astype(F32)
    return (1.0 / 16.0) * (sum_q * inner + 1.25 * sum_qu)


def dose_edge_body(place_ref, sums_ref, other_ref, *refs):
    ins, (grad_ref, send_ref), (held, target, cross, cross_t, sems) = refs[:7], refs[7:9], refs[9:]
    target_ref, first_ref, second_ref, ch_ref, cl_ref, th_ref, tl_ref = ins
    tile = place_ref[2]
    sides = [pl.ds(0, EDGE), pl.ds(PERIOD - EDGE, EDGE)]
    copies = fetches(
        [ch_ref.at[tile], cl_ref.at[tile]]
        + [ref.at[:, :, side] for side in sides for ref in (first_ref, second_ref)]
        + [target_ref.at[:, side] for side in sides]
        + [th_ref.at[tile], tl_ref.at[tile]],
        [cross.at[0], cross.at[1]]
        + [held.at[index] for index in range(4)]
        + [target.at[index] for index in range(2)]
        + [cross_t.at[0], cross_t.at[1]],
        sems,
    )
    for copy in copies[:2]:
        copy.wait()
    halo = dot3(split(other_ref[...]), (cross[0], cross[1]))
    for copy in copies[2:8]:
        copy.wait()
    grads = []
    for side in range(2):
        columns = []
        for row, lanes in places(EDGE):
            place = (row, lanes)
            there = slice(side * (PERIOD - EDGE), side * (PERIOD - EDGE) + EDGE)
            acid = sums_ref[0, row, there] + halo[row, side * EDGE : (side + 1) * EDGE]
            zero = jnp.zeros(acid.shape, F32)
            sums = sample_sums(held.at[2 * side], place, acid, (zero, zero, zero))
            sums = sample_sums(held.at[2 * side + 1], place, acid, sums)
            columns.append(acid_grad(sums, target[(side,) + place]))
        grads.append(jnp.concatenate(columns, 0))
    grad = jnp.concatenate(grads, 1)
    grad_ref[...] = grad
    for copy in copies[8:]:
        copy.wait()
    send_ref[...] = dot3(split(grad), (cross_t[0], cross_t[1]))


def dose_body(place_ref, sums_ref, edge_ref, target_ref, noise_ref, oh_ref, ol_ref, *refs):
    ins, out_ref, outs, (target, noise, own, sems) = refs[:11], refs[11], refs[12:20], refs[20:]
    field_ref, kern_ref, wh_ref, wl_ref, gh_ref, gl_ref, blur_ref, th_ref, tl_ref, fold_ref, coef_ref = ins
    field, kern, wave, grid, blur, table, fold, coef = outs
    block = place_ref[1]
    chunks = [pl.ds(first, CHUNK) for first in range(0, PERIOD, CHUNK)]
    copies = fetches(
        [target_ref]
        + [ref for part in chunks for ref in (noise_ref.at[:, :, part], oh_ref.at[part], ol_ref.at[part])]
        + [field_ref, kern_ref, wh_ref.at[block], wl_ref.at[block], gh_ref, gl_ref]
        + [blur_ref.at[block], th_ref, tl_ref, fold_ref, coef_ref],
        [target]
        + [
            ref
            for index, part in enumerate(chunks)
            for ref in (noise.at[index], own.at[0, part], own.at[1, part])
        ]
        + [field, kern, wave.at[0], wave.at[1], grid.at[0], grid.at[1]]
        + [blur, table.at[0], table.at[1], fold, coef],
        sems,
    )
    copies[0].wait()
    total = None
    for index in range(len(chunks)):
        for copy in copies[1 + 3 * index : 4 + 3 * index]:
            copy.wait()
        for col in range(0, CHUNK, LANES):
            first = index * CHUNK + col
            grads = []
            for row in range(0, ROWS, 16):
                place = (slice(row, row + 16), slice(first, first + LANES))
                acid, *sums = [sums_ref[(which,) + place] for which in range(4)]
                here = (slice(row, row + 16), slice(col, col + LANES))
                grads.append(acid_grad(sample_sums(noise.at[index], here, acid, sums), target[place]))
            grad = jnp.concatenate(grads, 0)
            if first == 0:
                grad = jnp.concatenate([edge_ref[:, :EDGE], grad[:, EDGE:]], 1)
            if first == PERIOD - LANES:
                grad = jnp.concatenate([grad[:, : LANES - EDGE], edge_ref[:, EDGE:]], 1)
            lines = slice(first, first + LANES)
            part = dot3(split(grad), (own[0, lines], own[1, lines]))
            total = part if total is None else total + part
    out_ref[...] = total
    for copy in copies[1 + 3 * len(chunks) :]:
        copy.wait()


def back_body(place_ref, weight_ref, *refs):
    piece_refs, (field, kern, wave, grid, blur, table, fold, coef) = refs[:KERN], refs[KERN : KERN + 8]
    out_ref, rows = refs[KERN + 8 :]
    for shift, piece_ref in enumerate(piece_refs):
        first = jnp.bitwise_xor(place_ref[0], shift) * ROWS
        rows[pl.ds(pl.multiple_of(first, ROWS), ROWS)] = piece_ref[...]
    part = 2.0 * dot3(split(blur[...]), split(rows[...]))
    grad = jnp.concatenate([part, part], 1)
    half = KERN * REACH
    sum_re = sum_im = None
    for pair in range(PAIRS):
        pulled = [
            field[index * half : (index + 1) * half] * (weight_ref[index] * grad)
            for index in (2 * pair, 2 * pair + 1)
        ]
        lefts = dot3(split(jnp.concatenate(pulled, 0)), (grid[0], grid[1]))
        stack = []
        for index in range(2):
            column = []
            for which in range(KERN):
                first = index * half + which * REACH
                left = lefts[first : first + REACH]
                column += [left[:, :FREQ], left[:, FREQ:]]
            stack.append(jnp.concatenate(column, 0))
        near = dot3((wave[0], wave[1]), split(jnp.concatenate(stack, 1)))
        for index in range(2):
            near_re = near[:FREQ, index * FREQ : (index + 1) * FREQ]
            near_im = near[FREQ:, index * FREQ : (index + 1) * FREQ]
            kern_re, kern_im = kern[2 * pair + index, 0], kern[2 * pair + index, 1]
            own_re = kern_re * near_re + kern_im * near_im
            own_im = kern_re * near_im - kern_im * near_re
            sum_re = own_re if sum_re is None else sum_re + own_re
            sum_im = own_im if sum_im is None else sum_im + own_im
    grad_re, grad_im = sum_re * (2.0 / PERIOD), sum_im * (2.0 / PERIOD)
    mix = jnp.concatenate(
        [jnp.concatenate([grad_re, -grad_im], 1), jnp.concatenate([-grad_im, -grad_re], 1)], 0
    )
    folded = dot_exact(split(mix), fold[...])
    coef_re, coef_im = coef[0], coef[1]
    by_cos, by_sin = grad_im[:, :1], grad_re[:, :1]
    spare_cos = coef_re * by_cos + coef_im * by_sin
    spare_sin = coef_re * by_sin - coef_im * by_cos
    mixed = jnp.concatenate([folded, spare_cos, spare_sin], 0)
    high, low = split(dot3((table[0], table[1]), split(mixed)).reshape(out_ref.shape))
    row = lax.broadcasted_iota(jnp.int32, out_ref.shape, 1)
    out_ref[...] = jnp.where(row < HIGH, high.astype(F32), low.astype(F32)).astype(BF)


def final_body(got_ref, back_ref, basis_ref, wh_ref, wl_ref, last_ref, out_ref):
    total = got_ref[0].astype(F32)
    for index in range(1, got_ref.shape[0]):
        total = total + got_ref[index].astype(F32)
    rows = dot3(split(back_ref[...]), split(total))
    spare = jnp.sum(basis_ref[...] * (total[HIGH - 1 : HIGH] + total[RANK - 1 :]), 1, keepdims=True)
    out_ref[...] = dot3(split(rows), (wh_ref[...], wl_ref[...])) + spare * last_ref[...]


def to_const(table):
    return hbm(*near_const(table))


def near_const(table):
    return tuple(jnp.asarray(part) for part in np_split(table))


def shifted(values, shifts):
    count = lax.axis_size("kern")
    return [
        lax.ppermute(value, "kern", [(source, source ^ shift) for source in range(count)])
        for value, shift in zip(values, shifts)
    ]


def body(mask_values, kernels, weights, target, dose_noise):
    noise_count = lax.axis_size("noise")
    f32 = lambda *shape: jax.ShapeDtypeStruct(shape, F32)
    bf16 = lambda *shape: jax.ShapeDtypeStruct(shape, BF)
    smem = pl.BlockSpec(memory_space=pltpu.SMEM)
    columns = PERIOD // CHUNK
    shifts = range(1, KERN)

    def fixed(*shape):
        return pl.BlockSpec(shape, lambda i, *_: (0,) * len(shape))

    def chunk(rows):
        return pl.BlockSpec((rows, CHUNK), lambda i, *_: (0, i))

    def moved_spec(width):
        return pl.BlockSpec((noise_count // columns, ROWS, width), lambda i: (i, 0, 0))

    lines = to_const(LINE.T)
    basis = jnp.asarray(BASIS.T[:RANK], F32)
    last = jnp.asarray(LAST, F32)
    far_noise = dose_noise.reshape(2, noise_count, ROWS, PERIOD)
    anywhere = pl.BlockSpec(memory_space=pltpu.HBM)
    held = (mask_values, basis, *lines, last)
    moved_first, moved = call(
        front_body,
        (pltpu.VMEM((noise_count, ROWS, PERIOD + FREQ), BF), pltpu.HBM((noise_count, ROWS, PERIOD), BF)),
        hbm(*held, far_noise),
        in_specs=[anywhere] * 6,
        out_specs=(pl.BlockSpec(memory_space=pltpu.VMEM), anywhere),
        scratch_shapes=[pltpu.VMEM(value.shape, value.dtype) for value in held]
        + [
            pltpu.VMEM((noise_count, ROWS, PERIOD), BF),
            pltpu.SemaphoreType.DMA((5 + 3 * PARTS,)),
        ],
    )
    place = jnp.stack([lax.axis_index(axis).astype(jnp.int32) for axis in ("kern", "noise", "tile")])
    moved_first, place = lax.optimization_barrier((moved_first, place))
    got = lax.all_to_all(moved_first, "noise", 0, 0, tiled=True)
    got, moved, kernels, weights, target, place = lax.optimization_barrier(
        (got, moved, kernels, weights, target, place)
    )
    got_last = lax.all_to_all(moved, "noise", 0, 0, tiled=True)

    def at_place(which, table):
        return [pl.BlockSpec((1,) + table.shape[1:], lambda i, place: (place[which], 0, 0))] * 2

    waves_t = WAVE.transpose(0, 2, 1)
    cross_t = CROSS.transpose(0, 2, 1)
    coef = hbm(jnp.asarray(COEF, F32))
    spec = call(
        spectrum_body,
        f32(2 * FREQ, FREQ),
        (got, *near_const(GATHER_OWN), jnp.asarray(UNFOLD, BF), jnp.asarray(COEF, F32)),
        place=place,
        grid=(1,),
        in_specs=[pl.BlockSpec((noise_count, ROWS, FREQ), lambda i, _: (0, 0, PERIOD // FREQ))]
        + at_place(0, GATHER_OWN)
        + [fixed(*UNFOLD.shape), fixed(*COEF.shape)],
        out_specs=fixed(2 * FREQ, FREQ),
    )
    specs = [spec] + shifted([spec] * len(shifts), shifts)
    field_rows = 2 * KERN * REACH
    field_shape = (PAIRS * field_rows, 2 * COARSE)
    blur = jnp.asarray(BLUR, F32)
    ins = (*specs, kernels, *to_const(WAVE), *to_const(GRID), blur)
    field, *pieces = call(
        field_body,
        (pltpu.HBM(field_shape, F32),) + (f32(ROWS, COARSE),) * KERN,
        (place, weights, *hbm(*ins)),
        in_specs=[smem] * 2 + [anywhere] * len(ins),
        out_specs=(anywhere,) + (pl.BlockSpec((ROWS, COARSE), lambda: (0, 0)),) * KERN,
        scratch_shapes=[
            pltpu.VMEM((KERN,) + spec.shape, F32),
            pltpu.VMEM(kernels.shape, F32),
            pltpu.VMEM((2,) + WAVE.shape[1:], BF),
            pltpu.VMEM((2,) + GRID.shape, BF),
            pltpu.VMEM(BLUR.shape[1:], F32),
            pltpu.VMEM(field_shape, F32),
            pltpu.VMEM((KERN * ROWS, COARSE), F32),
            pltpu.SemaphoreType.DMA((10 + PAIRS,)),
        ],
    )
    pieces = pieces[:1] + shifted(pieces[1:], shifts)
    rows = (pieces[0] + pieces[1]) + (pieces[2] + pieces[3])
    swap = [(0, 1), (1, 0)]
    rows_other = lax.ppermute(rows, "tile", swap)
    sums = call(
        dose_first_body,
        f32(4, ROWS, PERIOD),
        (rows, *near_const(OWN.T), got),
        grid=(1,),
        in_specs=[fixed(ROWS, COARSE)] + [fixed(COARSE, PERIOD)] * 2 + [fixed(noise_count, ROWS, PERIOD)],
        out_specs=pl.BlockSpec((4, ROWS, PERIOD), lambda i: (0, 0, 0)),
    )
    (target,) = hbm(target)
    (sums,) = vmem(sums)
    inside = pl.BlockSpec(memory_space=pltpu.VMEM)
    piece_spec = pl.BlockSpec((ROWS, COARSE), lambda: (0, 0))
    edges, send = call(
        dose_edge_body,
        (f32(ROWS, 2 * EDGE), f32(ROWS, COARSE)),
        (place, sums, rows_other, target, got, got_last, *to_const(CROSS), *to_const(cross_t)),
        in_specs=[smem, inside, piece_spec, anywhere]
        + [pl.BlockSpec(memory_space=pl.ANY)] * 2
        + [anywhere] * 4,
        out_specs=(piece_spec, piece_spec),
        scratch_shapes=[
            pltpu.VMEM((4, noise_count, ROWS, EDGE), BF),
            pltpu.VMEM((2, ROWS, EDGE), BF),
            pltpu.VMEM((2,) + CROSS.shape[1:], BF),
            pltpu.VMEM((2,) + cross_t.shape[1:], BF),
            pltpu.SemaphoreType.DMA((10,)),
        ],
    )
    grad_other = lax.ppermute(send, "tile", swap)
    blur_t, fold = jnp.asarray(BLUR.transpose(0, 2, 1), F32), jnp.asarray(UNFOLD.T, BF)
    ins = (field, kernels, *to_const(waves_t), *to_const(GRID.T), blur_t, *to_const(SPREAD), fold, *coef)
    held = [
        (field_shape, F32),
        (kernels.shape, F32),
        ((2,) + waves_t.shape[1:], BF),
        ((2,) + GRID.T.shape, BF),
        (BLUR.shape[:0:-1], F32),
        ((2,) + SPREAD.shape, BF),
        (fold.shape, BF),
        (COEF.shape, F32),
    ]
    grad_own, *staged = call(
        dose_body,
        (f32(ROWS, COARSE),) + tuple(pltpu.VMEM(shape, dtype) for shape, dtype in held),
        (place, sums, edges, target, got_last, *to_const(OWN), *hbm(*ins)),
        in_specs=[smem, inside, piece_spec, anywhere, pl.BlockSpec(memory_space=pl.ANY)]
        + [anywhere] * (2 + len(ins)),
        out_specs=(piece_spec,) + (inside,) * len(held),
        scratch_shapes=[
            pltpu.VMEM((ROWS, PERIOD), BF),
            pltpu.VMEM((columns, noise_count, ROWS, CHUNK), BF),
            pltpu.VMEM((2,) + OWN.shape, BF),
            pltpu.SemaphoreType.DMA((1 + 3 * columns + len(ins),)),
        ],
    )
    grad = grad_own + grad_other
    grads = [grad] + shifted([grad] * len(shifts), shifts)
    spread = call(
        back_body,
        bf16(BLOCKS, RANK, FREQ),
        (place, weights, *grads, *vmem(*staged)),
        in_specs=[smem] * 2 + [piece_spec] * KERN + [inside] * len(held),
        out_specs=pl.BlockSpec((BLOCKS, RANK, FREQ), lambda: (0, 0, 0)),
        scratch_shapes=[pltpu.VMEM((KERN * ROWS, COARSE), F32)],
    )
    back = lax.all_to_all(spread, ("kern", "noise"), 0, 0, tiled=True)
    return call(
        final_body,
        f32(ROWS, PERIOD),
        (back, jnp.asarray(BASIS_BACK, F32), jnp.asarray(BASIS, F32), *(jnp.asarray(t) for t in np_split(LINE)), jnp.asarray(LAST, F32)),
    )


def solution(mesh):
    return jax.shard_map(
        body,
        mesh=mesh,
        in_specs=(
            P(("kern", "noise"), "tile"),
            P("kern", None, None, None),
            P("kern"),
            P(("kern", "noise"), "tile"),
            P("noise", "kern", "tile"),
        ),
        out_specs=P(("kern", "noise"), "tile"),
        check_vma=False,
    )
```
